32 devices in a mesh: row: 4 (over y, x), col: 8 (over z, core).
Axes of the slice: x: 2, y: 2, z: 4, core: 2. Of those that a mesh axis runs over, the one named last changes fastest.
Arguments:
- region_inverse: float32 [4096, 4096], P('row', 'col'), may hold values from -6 to 6
- factor_cols: float32 [3, 4096, 512], P(None, 'row'), may hold values from -0.09375 to 0.09375
- parent_factor: float32 [2, 512, 512], P(None, 'col'), may hold values from -0.25 to 0.25
- diag_inverse: float32 [3, 512, 512], P(None, 'col'), may hold values from -6 to 6
- listed: int32 [3, 8], replicated, may hold values from 0 to 1, as said below
Outputs:
- col_blocks: float32 [3, 4096, 512], P(None, ('row', 'col'))
- diag_blocks: float32 [3, 512, 512], P(None, 'col')
- parent_rows: float32 [2, 512, 512], P(None, 'col')
The draws below stay inside these ranges and needn't reach their ends.
Inputs may be any that keep to these rules, and one draw needn't show every extreme that they name: listed[0] has exactly 6 ones; listed[1] and listed[2] have exactly 4 ones each, all at blocks that listed[0] also lists.
All inputs are finite; a program needn't handle non-finite values.
Results may differ from the reference program's by a relative error of at most 0.0001.
Values sent between devices are 32-bit elements; how exact they have to be, the bound alone decides.
No kernel may reach another device: no remote copies, remote signals or barrier semaphores. Data moves between devices by JAX's collectives and lax.ppermute only.
A program may use at most 128 MiB of HBM per device.

```python
import jax
import jax.numpy as jnp
from jax import lax

B = 512
NB = 8
R = 4096
LP = 6
LC = 4


def draw_listed(key, part):
    first = jax.random.permutation(jax.random.fold_in(key, 11), NB)
    parent = jnp.zeros((NB,), jnp.int32).at[first[:LP]].set(1)
    result_rows = [parent]
    for member in range(2):
        order = jax.random.permutation(jax.random.fold_in(key, 21 + member), LP)
        picked = first[order[:LC]]
        result_rows.append(jnp.zeros((NB,), jnp.int32).at[picked].set(1))
    return jnp.stack(result_rows)


def raised(values, stream_key, source, target, shards_of, factor):
    def block_of(dim):
        return (jnp.arange(values.shape[dim]) // (values.shape[dim] // shards_of)).reshape((-1,) + (1,) * (values.ndim - 1 - dim))

    first = jax.random.permutation(stream_key, shards_of)[block_of(target)]
    other_side = (block_of(target) + shards_of // 2) % shards_of
    return jnp.where((block_of(source) == first) | (block_of(source) == other_side), factor * values, values)


def block_levels(key, dims, split, smallest, largest):
    factor_of, own = 1.0, jax.random.fold_in(key, 6)
    for position, parts in split:
        draws = jnp.exp(jax.random.uniform(jax.random.fold_in(own, position), (parts,), jnp.float32, smallest / len(split), largest / len(split)))
        factor_of = factor_of * jnp.repeat(draws, dims[position] // parts).reshape([-1 if axis == position else 1 for axis in range(len(dims))])
    return factor_of


def scatter_about(key, dims, deviation, most, split=(), dtype=jnp.bfloat16):
    result = jax.random.normal(key, dims, jnp.float32) * deviation
    if len(split) > 0:
        result = block_levels(key, dims, split, -0.22, 0.18) * result
    return jnp.clip(result, min=-most, max=most).astype(dtype)


def gaussian_with(stream_key, dims, width, limit, pieces, heavy, kind=jnp.bfloat16):
    drawn = width * jax.random.normal(stream_key, dims, jnp.float32)
    if pieces:
        drawn = drawn * block_levels(stream_key, dims, pieces, -0.22, 0.18)
    return jnp.clip(raised(drawn, jax.random.fold_in(stream_key, 3), *heavy), -limit, limit).astype(kind)


def setup_inputs(seed: int = 0) -> dict:
    key_list = jax.random.split(jax.random.key(seed), 6)
    return {
        "region_inverse": gaussian_with(key_list[0], (R, R), 1.0, 6.0, ((0, 4), (1, 8)), (1, 0, 8, 2.0), jnp.float32),
        "factor_cols": scatter_about(key_list[1], (3, R, B), R ** -0.5, 0.09375, ((1, 4),), jnp.float32),
        "parent_factor": scatter_about(key_list[2], (2, B, B), B ** -0.5, 0.25, ((1, 8),), jnp.float32),
        "diag_inverse": scatter_about(key_list[3], (3, B, B), 1.0, 6.0, ((1, 8),), jnp.float32),
        "listed": draw_listed(jax.random.fold_in(key_list[5], 71), 0),
    }


def product(left, right):
    return jnp.dot(left, right, precision=lax.Precision.HIGHEST, preferred_element_type=jnp.float32)


def reference(region_inverse, factor_cols, parent_factor, diag_inverse, listed):
    weights = listed.astype(jnp.float32)
    masks = [jnp.repeat(weights[member], B) for member in range(3)]
    factors = [factor_cols[member] * masks[member][:, None] for member in range(3)]
    parent_col = -product(region_inverse, factors[0]) * masks[0][:, None]
    parent_diag = diag_inverse[0] - product(factors[0].T, parent_col)
    col_list = [parent_col]
    diag_list = [parent_diag]
    upper_list = []
    for member in (1, 2):
        link = parent_factor[member - 1]
        column = -(product(region_inverse, factors[member]) + product(parent_col, link)) * masks[member][:, None]
        upper = -(product(parent_col.T, factors[member]) + product(parent_diag, link))
        diagonal = diag_inverse[member] - product(factors[member].T, column) - product(link.T, upper)
        col_list.append(column)
        diag_list.append(diagonal)
        upper_list.append(upper)
    return jnp.stack(col_list), jnp.stack(diag_list), jnp.stack(upper_list)
```

```python
import jax
import jax.numpy as jnp
from jax import lax
from jax.sharding import PartitionSpec as P

AXES = ("row", "col")
HIGH = lax.Precision.HIGH


def dot(left, right):
    return jnp.dot(left, right, precision=HIGH, preferred_element_type=jnp.float32)


def dot_left(left, right):
    return lax.dot_general(
        left, right, (((0,), (0,)), ((), ())), precision=HIGH, preferred_element_type=jnp.float32
    )


def gray(place):
    return place ^ (place >> 1)


def reversed_bits(count):
    order = [0]
    step = 1
    while step < count:
        order = [value + bit * step for value in order for bit in (0, 1)]
        step *= 2
    return order


def row_weights(listed_row, first_row, count, width):
    block_ids = (first_row + lax.iota(jnp.int32, count)) // width
    table = lax.iota(jnp.int32, listed_row.shape[0])
    hits = (block_ids[:, None] == table[None, :]) & (listed_row[None, :] != 0)
    return jnp.any(hits, axis=1).astype(jnp.float32)


def swap(value, axis, size, bit):
    return lax.ppermute(value, axis, [(place, place ^ (1 << bit)) for place in range(size)])


def shards(region_inverse, factor_cols, parent_factor, diag_inverse, listed):
    row_count = lax.axis_size("row")
    col_count = lax.axis_size("col")
    row_place = lax.axis_index("row")
    col_place = lax.axis_index("col")
    row_bits = row_count.bit_length() - 1
    col_bits = col_count.bit_length() - 1
    rows_here, cols_here = region_inverse.shape
    members, _, width = factor_cols.shape
    group = rows_here // col_count
    ratio = col_count // row_count
    diag_width = width // col_count
    first_row = row_place * rows_here
    source = col_place // ratio

    gathered = lax.all_gather(
        jnp.concatenate([parent_factor, diag_inverse[:1]]), "col", axis=1, tiled=True
    )
    links, full_diag = gathered[:2], gathered[2]

    order = reversed_bits(col_count)
    relative = jnp.array(order, jnp.int32) ^ col_place
    region = jnp.take(region_inverse.reshape(col_count, group, cols_here), relative, axis=0)
    region = region.reshape(rows_here, cols_here)

    own_first = first_row + col_place * group
    own_masks = [row_weights(listed[j], own_first, group, width)[:, None] for j in range(members)]
    own = [
        lax.dynamic_slice_in_dim(factor_cols[j], col_place * group, group, 0) * own_masks[j]
        for j in range(members)
    ]

    def ring(step, forward):
        pairs = []
        for col in range(col_count):
            start = col // ratio
            at = step if forward else -step % row_count
            to = step + 1 if forward else (-step - 1) % row_count
            pairs.append(
                ((start ^ gray(at)) * col_count + col, (start ^ gray(to)) * col_count + col)
            )
        return pairs

    is_source = row_place == source
    col_first = col_place * cols_here

    def received(j):
        block = lax.dynamic_slice_in_dim(
            factor_cols[j], (col_place % ratio) * cols_here, cols_here, 0
        )
        half = cols_here // 2
        parts = []
        for piece, forward in ((block[:half], True), (block[half:], False)):
            total = jnp.where(is_source, piece, 0)
            moving = piece
            for step in range(row_count - 1):
                moving = lax.ppermute(moving, AXES, ring(step, forward))
                total = total + moving
            parts.append(total)
        mask = row_weights(listed[j], col_first, cols_here, width)[:, None]
        return jnp.concatenate(parts) * mask

    def column_sums(j):
        right = received(j)
        keep = None
        size = rows_here // 2
        send = dot(region[size:], right)
        keep = dot(region[:size], right)
        for bit in range(col_bits):
            arrived = swap(send, "col", col_count, bit)
            if bit + 1 < col_bits:
                size //= 2
                send = keep[size:] + arrived[size:]
                keep = keep[:size] + arrived[:size]
            else:
                keep = keep + arrived
        return keep

    def total_rows(matrices):
        count = len(matrices)
        stacked = jnp.stack(matrices).reshape(count, col_count, diag_width, width)
        stacked = jnp.take(stacked, relative, axis=1).transpose(1, 0, 2, 3)
        stacked = stacked.reshape(col_count, count * diag_width, width)
        half = col_count // 2
        value = stacked[:half] + swap(stacked[half:], "col", col_count, 0)
        middle = count * diag_width // 2
        done = []
        for piece, bits in (
            (value[:, :middle], range(row_bits)),
            (value[:, middle:], range(row_bits - 1, -1, -1)),
        ):
            for bit in bits:
                size = piece.shape[1] // 2
                side = (row_place >> bit) & 1
                kept = lax.dynamic_slice_in_dim(piece, side * size, size, 1)
                sent = lax.dynamic_slice_in_dim(piece, (1 - side) * size, size, 1)
                piece = kept + swap(sent, "row", row_count, bit)
            for bit in range(1, col_bits):
                size = piece.shape[0] // 2
                piece = piece[:size] + swap(piece[size:], "col", col_count, bit)
            piece = piece[0]
            for bit in reversed(list(bits)):
                other = swap(piece, "row", row_count, bit)
                side = (row_place >> bit) & 1
                low = jnp.where(side == 0, piece, other)
                high = jnp.where(side == 0, other, piece)
                piece = jnp.concatenate([low, high])
            done.append(piece)
        return jnp.concatenate(done).reshape(count, diag_width, width)

    sums = [column_sums(j) for j in range(members)]
    parent_col = -sums[0] * own_masks[0]
    turned = [dot(parent_col, links[c]) for c in range(2)]
    lifted = [dot(own[0], links[c]) for c in range(2)]
    parent_terms = [-dot_left(own[0], parent_col)]
    for c in range(2):
        parent_terms.append(dot_left(own[0], turned[c]) - dot_left(parent_col, own[c + 1]))
    parent_totals = total_rows(parent_terms)
    child_cols = []
    child_terms = []
    for c in range(2):
        column = -(sums[c + 1] + turned[c]) * own_masks[c + 1]
        child_cols.append(column)
        left = jnp.concatenate([own[c + 1], turned[c], lifted[c]])
        right = jnp.concatenate([-column, own[c + 1], -turned[c]])
        child_terms.append(dot_left(left, right))
    child_totals = total_rows(child_terms)

    start = col_place * diag_width
    uppers = []
    diags = [diag_inverse[0] + parent_totals[0]]
    for c in range(2):
        uppers.append(parent_totals[1 + c] - dot(diag_inverse[0], links[c]))
        link_cols = lax.dynamic_slice_in_dim(links[c], start, diag_width, 1)
        framed = dot(dot_left(link_cols, full_diag), links[c])
        diags.append(diag_inverse[c + 1] + framed + child_totals[c])
    return jnp.stack([parent_col] + child_cols), jnp.stack(diags), jnp.stack(uppers)


def solution(mesh):
    in_specs = (
        P("row", "col"),
        P(None, "row", None),
        P(None, "col", None),
        P(None, "col", None),
        P(),
    )
    out_specs = (P(None, ("row", "col"), None), P(None, "col", None), P(None, "col", None))
    return jax.shard_map(shards, mesh=mesh, in_specs=in_specs, out_specs=out_specs, check_vma=False)
```

```python
import functools

import jax
import jax.numpy as jnp
from jax import lax
from jax.experimental import pallas as pl
from jax.experimental.pallas import tpu as pltpu
from jax.sharding import PartitionSpec as P

AXES = ("row", "col")
F32 = jnp.float32
BF16 = jnp.bfloat16
NN = (((1,), (0,)), ((), ()))
TN = (((0,), (0,)), ((), ()))
VMEM_BYTES = 40 * 1024 * 1024


def split(value):
    high = value.astype(BF16)
    return high, (value - high.astype(F32)).astype(BF16)


def product(left, right, dims=NN):
    def one(a, b):
        return lax.dot_general(a, b, dims, preferred_element_type=F32)

    return one(left[0], right[0]) + (one(left[0], right[1]) + one(left[1], right[0]))


def reordered(chooser, value):
    high, low = split(value)
    return jnp.dot(chooser, high, preferred_element_type=F32) + jnp.dot(
        chooser, low, preferred_element_type=F32
    )


def call(body, out_shapes, flops, *args, smem=0):
    specs = [pl.BlockSpec(memory_space=pltpu.SMEM)] * smem
    specs += [pl.BlockSpec(memory_space=pltpu.VMEM)] * (len(args) - smem)
    moved = sum(a.size * a.dtype.itemsize for a in args)
    moved += sum(s.size * s.dtype.itemsize for s in out_shapes)
    return pl.pallas_call(
        body,
        out_shape=out_shapes,
        in_specs=specs,
        out_specs=[pl.BlockSpec(memory_space=pltpu.VMEM)] * len(out_shapes),
        compiler_params=pltpu.CompilerParams(vmem_limit_bytes=VMEM_BYTES),
        cost_estimate=pl.CostEstimate(flops=flops, bytes_accessed=moved, transcendentals=0),
    )(*args)


def shape(*dims, dtype=F32):
    return jax.ShapeDtypeStruct(dims, dtype)


def gray(place):
    return place ^ (place >> 1)


def reversed_bits(count):
    order = [0]
    step = 1
    while step < count:
        order = [value + bit * step for value in order for bit in (0, 1)]
        step *= 2
    return order


def row_weights(listed_row, first_row, count, width):
    block_ids = (first_row + lax.iota(jnp.int32, count)) // width
    table = lax.iota(jnp.int32, listed_row.shape[0])
    hits = (block_ids[:, None] == table[None, :]) & (listed_row[None, :] != 0)
    return jnp.any(hits, axis=1).astype(F32)


def swap(value, axis, size, change):
    return lax.ppermute(value, axis, [(place, place ^ change) for place in range(size)])


def split_rows_kernel(order_ref, in_ref, mask_ref, high_ref, low_ref):
    high, low = split(in_ref[0] * mask_ref[...])
    high_ref[...] = high
    low_ref[...] = low


def split_rows(array, member, order, group, mask):
    _, rows, columns = array.shape
    block = pl.BlockSpec((group, columns), lambda g, order_ref: (g, 0))
    return pl.pallas_call(
        split_rows_kernel,
        out_shape=[shape(rows, columns, dtype=BF16)] * 2,
        grid_spec=pltpu.PrefetchScalarGridSpec(
            num_scalar_prefetch=1,
            grid=(rows // group,),
            in_specs=[
                pl.BlockSpec((1, group, columns), lambda g, order_ref: (member, order_ref[g], 0)),
                pl.BlockSpec((group, 1), lambda g, order_ref: (order_ref[g], 0)),
            ],
            out_specs=[block, block],
        ),
        cost_estimate=pl.CostEstimate(
            flops=2 * rows * columns, bytes_accessed=8 * rows * columns, transcendentals=0
        ),
    )(order, array, mask)


def unit_kernel(count, place_ref, high_ref, low_ref, *refs):
    ways = (refs[:count], refs[count : 2 * count])
    send_ref, keep_ref = refs[2 * count :]
    half = ways[0][0].shape[0]
    total = None
    for way, candidates in enumerate(ways):
        place = place_ref[way]
        chosen = candidates[0][...]
        for at in range(1, count):
            chosen = jnp.where(place == at, candidates[at][...], chosen)
        columns = slice(way * half, (way + 1) * half)
        part = product((high_ref[:, columns], low_ref[:, columns]), split(chosen))
        total = part if total is None else total + part
    middle = total.shape[0] // 2
    keep_ref[...] = total[:middle]
    send_ref[...] = total[middle:]


def unit_gram_kernel(high_ref, low_ref, keep_ref, send_ref, out_ref):
    middle = keep_ref.shape[0]
    out_ref[...] = product(
        (high_ref[:, :middle], low_ref[:, :middle]), split(keep_ref[...])
    ) + product((high_ref[:, middle:], low_ref[:, middle:]), split(send_ref[...]))


def store_halves(keep_ref, send_ref, index, value):
    middle = value.shape[0] // 2
    keep_ref[index] = value[:middle]
    send_ref[index] = value[middle:]


def parent_kernel(
    children, chooser_ref, mask_ref, left_ref, right_ref, own_ref, links_ref,
    col_ref, turned_ref, keep_ref, send_ref,
):
    sums = jnp.concatenate([left_ref[...], right_ref[...]], axis=1)
    column = -sums * mask_ref[...]
    col_ref[...] = column
    column_pair = split(column)
    parent_pair = split(own_ref[0])
    chooser = chooser_ref[...]
    store_halves(
        keep_ref, send_ref, 0, reordered(chooser, -product(parent_pair, column_pair, TN))
    )
    for c in range(children):
        turned = product(column_pair, split(links_ref[c]))
        turned_ref[c] = turned
        upper = product(parent_pair, split(turned), TN)
        upper -= product(column_pair, split(own_ref[c + 1]), TN)
        store_halves(keep_ref, send_ref, 1 + c, reordered(chooser, upper))


def link_kernel(children, share, own_ref, links_ref, slices_ref, diag_ref, lifted_ref, framed_ref, corner_ref):
    parent_pair = split(own_ref[0])
    diag_pair = split(diag_ref[0])
    for c in range(children):
        link_pair = split(links_ref[c])
        lifted_ref[c] = product(parent_pair, link_pair)
        framed = product(diag_pair, link_pair)
        framed_ref[c] = framed
        corner_ref[c] = share * product(split(slices_ref[c]), split(framed), TN)


def child_kernel(
    children, chooser_ref, own_ref, turned_ref, lifted_ref, corner_ref, *refs
):
    keep_ref, send_ref = refs[-2:]
    for c in range(children):
        left_ref, right_ref = refs[2 * c : 2 * c + 2]
        own = split(own_ref[c + 1])
        turned = split(turned_ref[c])
        total = corner_ref[c] + jnp.concatenate([left_ref[...], right_ref[...]], axis=1)
        total += product(own, turned, TN) + product(turned, own, TN)
        total -= product(split(lifted_ref[c]), turned, TN)
        store_halves(keep_ref, send_ref, c, reordered(chooser_ref[...], total))


def shards(region_inverse, factor_cols, parent_factor, diag_inverse, listed):
    row_count = lax.axis_size("row")
    col_count = lax.axis_size("col")
    row_place = lax.axis_index("row")
    col_place = lax.axis_index("col")
    col_bits = col_count.bit_length() - 1
    rows_here, cols_here = region_inverse.shape
    members, _, width = factor_cols.shape
    children = members - 1
    group = rows_here // col_count
    ratio = col_count // row_count
    diag_width = width // col_count
    part = diag_width // row_count
    first_row = row_place * rows_here
    source = col_place // ratio
    unit = width // 2
    units = [(j, lo) for j in range(members) for lo in range(0, width, unit)]

    links = lax.all_gather(parent_factor, "col", axis=1, tiled=True)

    def ring(forward):
        pairs = []
        for col in range(col_count):
            start = col // ratio
            for place in range(row_count):
                at = (start ^ gray(place)) * col_count + col
                to = (start ^ gray((place + 1) % row_count)) * col_count + col
                pairs.append((at, to) if forward else (to, at))
        return pairs

    distance = row_place ^ source
    forward_place = distance
    shift = 1
    while shift < row_count:
        forward_place = forward_place ^ (forward_place >> shift)
        shift *= 2
    backward_place = (row_count - forward_place) % row_count
    places = jnp.stack([forward_place, backward_place]).astype(jnp.int32)
    is_source = row_place == source
    col_first = col_place * cols_here
    half = cols_here // 2
    col_masks = [row_weights(listed[j], col_first, cols_here, width)[:, None] for j in range(members)]

    def chunk(j, lo, way):
        start = (col_place % ratio) * cols_here + way * half
        block = lax.dynamic_slice(factor_cols, (j, start, lo), (1, half, unit))[0]
        return block * col_masks[j][way * half : (way + 1) * half]

    chunks = [[chunk(j, lo, way) for j, lo in units] for way in range(2)]
    received = [[], []]
    for stage in range(len(units) + row_count - 2):
        for way in range(2):
            if stage == 0:
                moving = chunks[way][0]
            elif stage < len(units):
                moving = jnp.where(is_source, chunks[way][stage], received[way][-1])
            else:
                moving = received[way][-1]
            received[way].append(lax.ppermute(moving, AXES, ring(way == 0)))

    relative = jnp.array(reversed_bits(col_count), jnp.int32) ^ col_place
    ones = jnp.ones((rows_here, 1), F32)
    region = split_rows(region_inverse[None], 0, relative, group, ones)
    row_masks = [row_weights(listed[j], first_row, rows_here, width)[:, None] for j in range(members)]
    turned_factors = []
    for c in range(children):
        pair = split_rows(factor_cols, c + 1, relative, group, row_masks[c + 1])
        turned_factors.append([value.T for value in pair])

    own_first = first_row + col_place * group
    own_masks = [row_weights(listed[j], own_first, group, width)[:, None] for j in range(members)]
    own = lax.dynamic_slice_in_dim(factor_cols, col_place * group, group, 1) * jnp.stack(own_masks)

    halving = jnp.array(reversed_bits(col_count), jnp.int32).reshape(2, 1, col_count // 2, 1)
    by_row = lax.iota(jnp.int32, row_count).reshape(1, row_count, 1, 1) ^ row_place
    inner = lax.iota(jnp.int32, part).reshape(1, 1, 1, part)
    wanted = ((halving ^ col_place) * diag_width + by_row * part + inner).reshape(width, 1)
    chooser = (wanted == lax.iota(jnp.int32, width)[None, :]).astype(BF16)

    def column_unit(index):
        candidates = []
        for way in range(2):
            candidates.append(chunks[way][index])
            candidates += received[way][index : index + row_count - 1]
        size = rows_here // 2
        return call(
            functools.partial(unit_kernel, row_count),
            [shape(size, unit)] * 2,
            6 * rows_here * cols_here * unit,
            places, *region, *candidates,
            smem=1,
        )

    def halved(send, keep):
        size = keep.shape[0]
        for bit in range(col_bits):
            arrived = swap(send, "col", col_count, 1 << bit)
            if bit + 1 < col_bits:
                size //= 2
                send = keep[size:] + arrived[size:]
                keep = keep[:size] + arrived[:size]
            else:
                keep = keep + arrived
        return keep

    def total_rows(keep, send):
        value = keep + swap(send, "col", col_count, 1)
        size = value.shape[1] // row_count
        piece = value[:, :size]
        for change in range(1, row_count):
            sent = value[:, change * size : (change + 1) * size]
            piece = piece + swap(sent, "row", row_count, change)
        for bit in range(1, col_bits):
            size //= 2
            piece = piece[:, :size] + swap(piece[:, size:], "col", col_count, 1 << bit)
        pieces = [piece] + [swap(piece, "row", row_count, d) for d in range(1, row_count)]
        stacked = []
        for row in range(row_count):
            chosen = pieces[0]
            for change in range(1, row_count):
                chosen = jnp.where(row_place ^ change == row, pieces[change], chosen)
            stacked.append(chosen)
        return jnp.concatenate(stacked, axis=1)

    sums = []
    grams = []
    for index, (j, lo) in enumerate(units):
        send, keep = column_unit(index)
        sums.append(halved(send, keep))
        if j > 0:
            grams += call(
                unit_gram_kernel,
                [shape(width, unit)],
                6 * rows_here * width * unit,
                *turned_factors[j - 1], keep, send,
            )

    parent_col, turned, keep, send = call(
        functools.partial(parent_kernel, children),
        [shape(group, width), shape(children, group, width)]
        + [shape(members, width // 2, width)] * 2,
        6 * (1 + 3 * children) * group * width * width,
        chooser, own_masks[0], sums[0], sums[1], own, links,
    )
    parent_totals = total_rows(keep, send)

    lifted, framed, corner = call(
        functools.partial(link_kernel, children, 1.0 / row_count),
        [shape(children, group, width), shape(children, diag_width, width),
         shape(children, width, width)],
        6 * children * (group + 2 * diag_width) * width * width,
        own, links, parent_factor, diag_inverse,
    )
    keep, send = call(
        functools.partial(child_kernel, children),
        [shape(children, width // 2, width)] * 2,
        18 * children * group * width * width,
        chooser, own, turned, lifted, corner, *grams,
    )
    child_totals = total_rows(keep, send)

    child_cols = []
    for c in range(children):
        column = jnp.concatenate(sums[2 * c + 2 : 2 * c + 4], axis=1)
        child_cols.append(-(column + turned[c]) * own_masks[c + 1])
    uppers = parent_totals[1:] - framed
    diags = diag_inverse + jnp.concatenate([parent_totals[:1], child_totals])
    return jnp.stack([parent_col] + child_cols), diags, uppers


def solution(mesh):
    in_specs = (
        P("row", "col"),
        P(None, "row", None),
        P(None, "col", None),
        P(None, "col", None),
        P(),
    )
    out_specs = (P(None, ("row", "col"), None), P(None, "col", None), P(None, "col", None))
    return jax.shard_map(shards, mesh=mesh, in_specs=in_specs, out_specs=out_specs, check_vma=False)
```

```python
import functools

import jax
import jax.numpy as jnp
from jax import lax
from jax.experimental import pallas as pl
from jax.experimental.pallas import tpu as pltpu
from jax.sharding import PartitionSpec as P

AXES = ("row", "col")
F32 = jnp.float32
BF16 = jnp.bfloat16
NN = (((1,), (0,)), ((), ()))
TN = (((0,), (0,)), ((), ()))
VMEM_BYTES = 40 * 1024 * 1024


def split(value):
    high = value.astype(BF16)
    return high, (value - high.astype(F32)).astype(BF16)


def product(left, right, dims=NN):
    def one(a, b):
        return lax.dot_general(a, b, dims, preferred_element_type=F32)

    return one(left[0], right[0]) + (one(left[0], right[1]) + one(left[1], right[0]))


def reordered(chooser, value):
    high, low = split(value)
    return jnp.dot(chooser, high, preferred_element_type=F32) + jnp.dot(
        chooser, low, preferred_element_type=F32
    )


def call(body, out_shapes, flops, *args, smem=0, scratch=()):
    specs = [pl.BlockSpec(memory_space=pltpu.SMEM)] * smem
    specs += [pl.BlockSpec(memory_space=pltpu.VMEM)] * (len(args) - smem)
    moved = sum(a.size * a.dtype.itemsize for a in args)
    moved += sum(s.size * s.dtype.itemsize for s in out_shapes)
    return pl.pallas_call(
        body,
        out_shape=out_shapes,
        in_specs=specs,
        out_specs=[pl.BlockSpec(memory_space=pltpu.VMEM)] * len(out_shapes),
        scratch_shapes=scratch,
        compiler_params=pltpu.CompilerParams(vmem_limit_bytes=VMEM_BYTES),
        cost_estimate=pl.CostEstimate(flops=flops, bytes_accessed=moved, transcendentals=0),
    )(*args)


def shape(*dims, dtype=F32):
    return jax.ShapeDtypeStruct(dims, dtype)


def gray(place):
    return place ^ (place >> 1)


def reversed_bits(count):
    order = [0]
    step = 1
    while step < count:
        order = [value + bit * step for value in order for bit in (0, 1)]
        step *= 2
    return order


def relative_links(count, place):
    return jnp.arange(count, dtype=jnp.int32) ^ place


def swap(value, axis, size, change):
    return lax.ppermute(value, axis, [(place, place ^ change) for place in range(size)])


def region_kernel(groups, info_ref, in_ref, high_ref, low_ref):
    size = in_ref.shape[0] // groups
    for g in range(groups):
        value = in_ref[pl.ds(pl.multiple_of(info_ref[g] * size, size), size), :]
        high_ref[g * size : (g + 1) * size, :], low_ref[g * size : (g + 1) * size, :] = split(value)


def factor_kernel(groups, info_ref, in_ref, high_ref, low_ref, ordered_ref):
    size = in_ref.shape[1] // groups
    for g in range(groups):
        value = in_ref[0, pl.ds(pl.multiple_of(info_ref[g] * size, size), size), :]
        weight = info_ref[groups + g].astype(F32)
        ordered_ref[g * size : (g + 1) * size, :] = value * weight
    high_ref[...], low_ref[...] = split(ordered_ref[...].T)


def place_kernel(groups, info_ref, in_ref, out_ref):
    size = in_ref.shape[2]
    for g in range(groups):
        start = pl.ds(pl.multiple_of(info_ref[g] * size, size), size)
        for c in range(in_ref.shape[1]):
            out_ref[c, start, :] = in_ref[g, c]


def ring_kernel(member, first, waits, info_ref, *refs):
    outs = refs[-2:]
    for way in range(2):
        own = refs[way][0] * info_ref[3 + member].astype(F32)
        if first:
            outs[way][...] = own
        else:
            outs[way][...] = jnp.where(info_ref[2] != 0, own, refs[2 + way][...])


def ring_stage(info, factors, member, column, half, unit, arrived, tokens):
    block = [
        pl.BlockSpec((1, half, unit), lambda i, info_ref, way=way: (member, info_ref[way], column))
        for way in range(2)
    ]
    whole = pl.BlockSpec((half, unit), lambda i, info_ref: (0, 0))
    return pl.pallas_call(
        functools.partial(ring_kernel, member, not arrived, len(tokens)),
        out_shape=[shape(half, unit)] * 2,
        grid_spec=pltpu.PrefetchScalarGridSpec(
            num_scalar_prefetch=1,
            grid=(1,),
            in_specs=block
            + [whole] * len(arrived)
            + [pl.BlockSpec(memory_space=pl.ANY)] * len(tokens),
            out_specs=[whole, whole],
        ),
        cost_estimate=pl.CostEstimate(
            flops=2 * half * unit, bytes_accessed=24 * half * unit, transcendentals=0
        ),
    )(info, factors, factors, *arrived, *tokens)


def unit_kernel(count, place_ref, high_ref, low_ref, *refs):
    ways = (refs[:count], refs[count : 2 * count])
    send_ref, keep_ref = refs[2 * count :]
    half = ways[0][0].shape[0]
    total = None
    for way, candidates in enumerate(ways):
        place = place_ref[way]
        chosen = candidates[0][...]
        for at in range(1, count):
            chosen = jnp.where(place == at, candidates[at][...], chosen)
        columns = slice(way * half, (way + 1) * half)
        part = product((high_ref[:, columns], low_ref[:, columns]), split(chosen))
        total = part if total is None else total + part
    middle = total.shape[0] // 2
    keep_ref[...] = total[:middle]
    send_ref[...] = total[middle:]


def unit_gram_kernel(high_ref, low_ref, keep_ref, send_ref, out_ref):
    middle = keep_ref.shape[0]
    out_ref[...] = product(
        (high_ref[:, :middle], low_ref[:, :middle]), split(keep_ref[...])
    ) + product((high_ref[:, middle:], low_ref[:, middle:]), split(send_ref[...]))


def store_halves(keep_ref, send_ref, index, value):
    middle = value.shape[0] // 2
    keep_ref[index] = value[:middle]
    send_ref[index] = value[middle:]


def parent_kernel(
    children, weight_ref, chooser_ref, left_ref, right_ref, own_ref, links_ref,
    col_ref, turned_ref, keep_ref, send_ref,
):
    sums = jnp.concatenate([left_ref[...], right_ref[...]], axis=1)
    column = -sums * weight_ref[0].astype(F32)
    col_ref[...] = column
    column_pair = split(column)
    parent_pair = split(own_ref[0])
    chooser = chooser_ref[...]
    store_halves(
        keep_ref, send_ref, 0, reordered(chooser, -product(parent_pair, column_pair, TN))
    )
    for c in range(children):
        turned = product(column_pair, split(links_ref[c]))
        turned_ref[c] = turned
        upper = product(parent_pair, split(turned), TN)
        upper -= product(column_pair, split(own_ref[c + 1]), TN)
        store_halves(keep_ref, send_ref, 1 + c, reordered(chooser, upper))


def link_kernel(children, share, own_ref, links_ref, slices_ref, diag_ref, lifted_ref, framed_ref, corner_ref):
    parent_pair = split(own_ref[0])
    diag_pair = split(diag_ref[0])
    for c in range(children):
        link_pair = split(links_ref[c])
        lifted_ref[c] = product(parent_pair, link_pair)
        framed = product(diag_pair, link_pair)
        framed_ref[c] = framed
        corner_ref[c] = share * product(split(slices_ref[c]), split(framed), TN)


def child_kernel(
    children, chooser_ref, own_ref, turned_ref, lifted_ref, corner_ref, *refs
):
    keep_ref, send_ref = refs[-2:]
    for c in range(children):
        left_ref, right_ref = refs[2 * c : 2 * c + 2]
        own = split(own_ref[c + 1])
        turned = split(turned_ref[c])
        total = corner_ref[c] + jnp.concatenate([left_ref[...], right_ref[...]], axis=1)
        total += product(own, turned, TN) + product(turned, own, TN)
        total -= product(split(lifted_ref[c]), turned, TN)
        store_halves(keep_ref, send_ref, c, reordered(chooser_ref[...], total))


def shards(region_inverse, factor_cols, parent_factor, diag_inverse, listed):
    row_count = lax.axis_size("row")
    col_count = lax.axis_size("col")
    row_place = lax.axis_index("row")
    col_place = lax.axis_index("col")
    col_bits = col_count.bit_length() - 1
    rows_here, cols_here = region_inverse.shape
    members, _, width = factor_cols.shape
    children = members - 1
    group = rows_here // col_count
    ratio = col_count // row_count
    diag_width = width // col_count
    part = diag_width // row_count
    first_row = row_place * rows_here
    source = col_place // ratio
    unit = width // 2
    units = [(j, lo) for j in range(members) for lo in range(0, width, unit)]

    def ring(forward):
        pairs = []
        for col in range(col_count):
            start = col // ratio
            for place in range(row_count):
                at = (start ^ gray(place)) * col_count + col
                to = (start ^ gray((place + 1) % row_count)) * col_count + col
                pairs.append((at, to) if forward else (to, at))
        return pairs

    distance = row_place ^ source
    forward_place = distance
    shift = 1
    while shift < row_count:
        forward_place = forward_place ^ (forward_place >> shift)
        shift *= 2
    backward_place = (row_count - forward_place) % row_count
    places = jnp.stack([forward_place, backward_place]).astype(jnp.int32)
    is_source = row_place == source
    half = cols_here // 2

    relative = jnp.array(reversed_bits(col_count), jnp.int32) ^ col_place
    col_weights = listed[:, col_place * cols_here // width]
    own_weights = listed[:, (first_row + col_place * group) // width]
    group_weights = jnp.take(listed, (first_row + relative * group) // width, axis=1)

    gathered = parent_factor[None]
    for bit in reversed(range(col_bits)):
        gathered = jnp.stack([gathered, swap(gathered, "col", col_count, 1 << bit)], axis=1)
        gathered = gathered.reshape((-1,) + parent_factor.shape)

    first_block = (col_place % ratio) * 2
    info = jnp.concatenate(
        [jnp.stack([first_block, first_block + 1, is_source.astype(jnp.int32)]), col_weights]
    ).astype(jnp.int32)
    lanes = len(units) // members
    moved = [[[], []] for _ in range(lanes)]
    received = [[[], []] for _ in range(lanes)]
    tokens = []
    prepared = []

    def prepare(stage):
        if stage == 0:
            prepared.append(
                call(
                    functools.partial(region_kernel, col_count),
                    [shape(rows_here, cols_here, dtype=BF16)] * 2,
                    rows_here * cols_here,
                    relative, region_inverse,
                    smem=1,
                )
            )
        elif stage <= children:
            prepared.append(
                call(
                    functools.partial(factor_kernel, col_count),
                    [shape(width, rows_here, dtype=BF16)] * 2,
                    rows_here * width,
                    jnp.concatenate([relative, group_weights[stage]]),
                    lax.slice_in_dim(factor_cols, stage, stage + 1, axis=0),
                    smem=1,
                    scratch=[pltpu.VMEM((rows_here, width), F32)],
                )
            )
        else:
            return []
        return [prepared[-1][0]]

    for stage in range(members + row_count - 2):
        for lane in range(lanes):
            arrived = [received[lane][way][-1] for way in range(2)] if stage else []
            if stage < members:
                moving = ring_stage(
                    info, factor_cols, stage, lane, half, unit, arrived, tokens
                )
                tokens = [moving[0]]
            else:
                moving = arrived
            for way in range(2):
                moved[lane][way].append(moving[way])
                received[lane][way].append(lax.ppermute(moving[way], AXES, ring(way == 0)))
        tokens = tokens + prepare(stage)

    region, *turned_factors = prepared

    links = call(
        functools.partial(place_kernel, col_count),
        [shape(*parent_factor.shape[:1], width, width)],
        0,
        relative_links(col_count, col_place), gathered,
        smem=1,
    )[0]
    own = lax.dynamic_slice_in_dim(factor_cols, col_place * group, group, 1)
    own = own * own_weights.astype(F32)[:, None, None]

    halving = jnp.array(reversed_bits(col_count), jnp.int32).reshape(2, 1, col_count // 2, 1)
    by_row = lax.iota(jnp.int32, row_count).reshape(1, row_count, 1, 1) ^ row_place
    inner = lax.iota(jnp.int32, part).reshape(1, 1, 1, part)
    wanted = ((halving ^ col_place) * diag_width + by_row * part + inner).reshape(width, 1)
    chooser = (wanted == lax.iota(jnp.int32, width)[None, :]).astype(BF16)

    def column_unit(index):
        member, lane = divmod(index, lanes)
        candidates = []
        for way in range(2):
            candidates.append(moved[lane][way][member])
            candidates += received[lane][way][member : member + row_count - 1]
        size = rows_here // 2
        return call(
            functools.partial(unit_kernel, row_count),
            [shape(size, unit)] * 2,
            6 * rows_here * cols_here * unit,
            places, *region, *candidates,
            smem=1,
        )

    def halved(send, keep):
        size = keep.shape[0]
        for bit in range(col_bits):
            arrived = swap(send, "col", col_count, 1 << bit)
            if bit + 1 < col_bits:
                size //= 2
                send = keep[size:] + arrived[size:]
                keep = keep[:size] + arrived[:size]
            else:
                keep = keep + arrived
        return keep

    def total_rows(keep, send):
        value = keep + swap(send, "col", col_count, 1)
        size = value.shape[1] // row_count
        piece = value[:, :size]
        for change in range(1, row_count):
            sent = value[:, change * size : (change + 1) * size]
            piece = piece + swap(sent, "row", row_count, change)
        for bit in range(1, col_bits):
            size //= 2
            piece = piece[:, :size] + swap(piece[:, size:], "col", col_count, 1 << bit)
        pieces = [piece] + [swap(piece, "row", row_count, d) for d in range(1, row_count)]
        stacked = []
        for row in range(row_count):
            chosen = pieces[0]
            for change in range(1, row_count):
                chosen = jnp.where(row_place ^ change == row, pieces[change], chosen)
            stacked.append(chosen)
        return jnp.concatenate(stacked, axis=1)

    sums = []
    grams = []
    for index, (j, lo) in enumerate(units):
        send, keep = column_unit(index)
        sums.append(halved(send, keep))
        if j > 0:
            grams += call(
                unit_gram_kernel,
                [shape(width, unit)],
                6 * rows_here * width * unit,
                *turned_factors[j - 1], keep, send,
            )

    parent_col, turned, keep, send = call(
        functools.partial(parent_kernel, children),
        [shape(group, width), shape(children, group, width)]
        + [shape(members, width // 2, width)] * 2,
        6 * (1 + 3 * children) * group * width * width,
        own_weights, chooser, sums[0], sums[1], own, links,
        smem=1,
    )
    parent_totals = total_rows(keep, send)

    lifted, framed, corner = call(
        functools.partial(link_kernel, children, 1.0 / row_count),
        [shape(children, group, width), shape(children, diag_width, width),
         shape(children, width, width)],
        6 * children * (group + 2 * diag_width) * width * width,
        own, links, parent_factor, diag_inverse,
    )
    keep, send = call(
        functools.partial(child_kernel, children),
        [shape(children, width // 2, width)] * 2,
        18 * children * group * width * width,
        chooser, own, turned, lifted, corner, *grams,
    )
    child_totals = total_rows(keep, send)

    child_cols = []
    for c in range(children):
        column = jnp.concatenate(sums[2 * c + 2 : 2 * c + 4], axis=1)
        child_cols.append(-(column + turned[c]) * own_weights[c + 1].astype(F32))
    uppers = parent_totals[1:] - framed
    diags = diag_inverse + jnp.concatenate([parent_totals[:1], child_totals])
    return jnp.stack([parent_col] + child_cols), diags, uppers


def solution(mesh):
    in_specs = (
        P("row", "col"),
        P(None, "row", None),
        P(None, "col", None),
        P(None, "col", None),
        P(),
    )
    out_specs = (P(None, ("row", "col"), None), P(None, "col", None), P(None, "col", None))
    return jax.shard_map(shards, mesh=mesh, in_specs=in_specs, out_specs=out_specs, check_vma=False)
```

```python
import functools

import jax
import jax.numpy as jnp
from jax import lax
from jax.experimental import pallas as pl
from jax.experimental.pallas import tpu as pltpu
from jax.sharding import PartitionSpec as P

AXES = ("row", "col")
F32 = jnp.float32
BF16 = jnp.bfloat16
NN = (((1,), (0,)), ((), ()))
TN = (((0,), (0,)), ((), ()))
VMEM_BYTES = 40 * 1024 * 1024
HINT = 32


def split(value):
    high = value.astype(BF16)
    return high, (value - high.astype(F32)).astype(BF16)


def product(left, right, dims=NN):
    def one(a, b):
        return lax.dot_general(a, b, dims, preferred_element_type=F32)

    return one(left[0], right[0]) + (one(left[0], right[1]) + one(left[1], right[0]))


def reordered(chooser, value):
    high, low = split(value)
    return jnp.dot(chooser, high, preferred_element_type=F32) + jnp.dot(
        chooser, low, preferred_element_type=F32
    )


def call(body, out_shapes, flops, *args, smem=0, scratch=(), after=()):
    specs = [pl.BlockSpec(memory_space=pltpu.SMEM)] * smem
    specs += [pl.BlockSpec(memory_space=pltpu.VMEM)] * (len(args) - smem)
    moved = sum(a.size * a.dtype.itemsize for a in args)
    if after:
        inner, count = body, len(args)

        def body(*refs):
            inner(*refs[:count], *refs[count + len(after) :])

        specs += [pl.BlockSpec(memory_space=pl.ANY)] * len(after)
        args = args + tuple(after)
    moved += sum(s.size * s.dtype.itemsize for s in out_shapes)
    return pl.pallas_call(
        body,
        out_shape=out_shapes,
        in_specs=specs,
        out_specs=[pl.BlockSpec(memory_space=pltpu.VMEM)] * len(out_shapes),
        scratch_shapes=scratch,
        compiler_params=pltpu.CompilerParams(vmem_limit_bytes=VMEM_BYTES),
        cost_estimate=pl.CostEstimate(
            flops=flops // HINT, bytes_accessed=moved // HINT, transcendentals=0
        ),
    )(*args)


def shape(*dims, dtype=F32):
    return jax.ShapeDtypeStruct(dims, dtype)


def gray(place):
    return place ^ (place >> 1)


def reversed_bits(count):
    order = [0]
    step = 1
    while step < count:
        order = [value + bit * step for value in order for bit in (0, 1)]
        step *= 2
    return order


def relative_links(count, place):
    return jnp.arange(count, dtype=jnp.int32) ^ place


def swap(value, axis, size, change):
    return lax.ppermute(value, axis, [(place, place ^ change) for place in range(size)])


def region_kernel(groups, info_ref, in_ref, high_ref, low_ref):
    size = in_ref.shape[0] // groups
    for g in range(groups):
        value = in_ref[pl.ds(pl.multiple_of(info_ref[g] * size, size), size), :]
        high_ref[g * size : (g + 1) * size, :], low_ref[g * size : (g + 1) * size, :] = split(value)


def factor_kernel(groups, info_ref, in_ref, high_ref, low_ref, ordered_ref):
    size = in_ref.shape[1] // groups
    for g in range(groups):
        value = in_ref[0, pl.ds(pl.multiple_of(info_ref[g] * size, size), size), :]
        weight = info_ref[groups + g].astype(F32)
        ordered_ref[g * size : (g + 1) * size, :] = value * weight
    high_ref[...], low_ref[...] = split(ordered_ref[...].T)


def factor_halves(info, factors, member, groups):
    _, rows, columns = factors.shape
    whole = pl.BlockSpec((columns, rows), lambda i, info_ref: (0, 0))
    return pl.pallas_call(
        functools.partial(factor_kernel, groups),
        out_shape=[shape(columns, rows, dtype=BF16)] * 2,
        grid_spec=pltpu.PrefetchScalarGridSpec(
            num_scalar_prefetch=1,
            grid=(1,),
            in_specs=[pl.BlockSpec((1, rows, columns), lambda i, info_ref: (member, 0, 0))],
            out_specs=[whole, whole],
            scratch_shapes=[pltpu.VMEM((rows, columns), F32)],
        ),
        compiler_params=pltpu.CompilerParams(vmem_limit_bytes=VMEM_BYTES),
        cost_estimate=pl.CostEstimate(
            flops=rows * columns // HINT, bytes_accessed=8 * rows * columns // HINT, transcendentals=0
        ),
    )(info, factors)


def place_kernel(groups, info_ref, in_ref, out_ref):
    size = in_ref.shape[2]
    for g in range(groups):
        start = pl.ds(pl.multiple_of(info_ref[g] * size, size), size)
        for c in range(in_ref.shape[1]):
            out_ref[c, start, :] = in_ref[g, c]


def chunk_kernel(members, lanes, info_ref, *refs):
    place = 0
    for at, member in enumerate(members):
        weight = info_ref[1 + member].astype(F32)
        block = refs[at]
        rows = block.shape[1] // 2
        columns = block.shape[2] // lanes
        for lane in range(lanes):
            for way in range(2):
                out_ref = refs[len(members) + place]
                place += 1
                out_ref[...] = weight * block[
                    0, way * rows : (way + 1) * rows, lane * columns : (lane + 1) * columns
                ]


def own_chunks(info, factors, members, rows, lanes):
    width = factors.shape[2]
    dims = (rows // 2, width // lanes)
    count = len(members) * lanes * 2
    flat = pl.pallas_call(
        functools.partial(chunk_kernel, members, lanes),
        out_shape=[shape(*dims)] * count,
        grid_spec=pltpu.PrefetchScalarGridSpec(
            num_scalar_prefetch=1,
            grid=(1,),
            in_specs=[
                pl.BlockSpec((1, rows, width), lambda i, info_ref, j=j: (j, info_ref[0], 0))
                for j in members
            ],
            out_specs=[pl.BlockSpec(dims, lambda i, info_ref: (0, 0))] * count,
        ),
        compiler_params=pltpu.CompilerParams(vmem_limit_bytes=VMEM_BYTES),
        cost_estimate=pl.CostEstimate(
            flops=rows * width // HINT, bytes_accessed=8 * rows * width // HINT, transcendentals=0
        ),
    )(info, *[factors] * len(members))
    return [[flat[(m * lanes + lane) * 2 :][:2] for lane in range(lanes)] for m in range(len(members))]


def ring_kernel(info_ref, *refs):
    outs = refs[-2:]
    for way in range(2):
        outs[way][...] = jnp.where(info_ref[0] != 0, refs[way][...], refs[2 + way][...])


def ring_stage(info, own, arrived, tokens):
    vmem = pl.BlockSpec(memory_space=pltpu.VMEM)
    return pl.pallas_call(
        ring_kernel,
        out_shape=[shape(*own[0].shape)] * 2,
        in_specs=[pl.BlockSpec(memory_space=pltpu.SMEM)]
        + [vmem] * 4
        + [pl.BlockSpec(memory_space=pl.ANY)] * len(tokens),
        out_specs=[vmem, vmem],
        cost_estimate=pl.CostEstimate(flops=0, bytes_accessed=own[0].size, transcendentals=0),
    )(info, *own, *arrived, *tokens)


def unit_kernel(count, lanes, place_ref, high_ref, low_ref, *refs):
    keep_ref, send_ref = refs[-2:]
    middle = keep_ref.shape[0]
    for lane in range(lanes):
        total = None
        for way in range(2):
            candidates = refs[(2 * lane + way) * count :][:count]
            half, unit = candidates[0].shape
            chosen = candidates[0][...]
            for at in range(1, count):
                chosen = jnp.where(place_ref[way] == at, candidates[at][...], chosen)
            columns = slice(way * half, (way + 1) * half)
            part = product((high_ref[:, columns], low_ref[:, columns]), split(chosen))
            total = part if total is None else total + part
        out = slice(lane * unit, (lane + 1) * unit)
        keep_ref[:, out] = total[:middle]
        send_ref[:, out] = total[middle:]


def unit_gram_kernel(high_ref, low_ref, keep_ref, send_ref, out_ref):
    middle = keep_ref.shape[0]
    out_ref[...] = product(
        (high_ref[:, :middle], low_ref[:, :middle]), split(keep_ref[...])
    ) + product((high_ref[:, middle:], low_ref[:, middle:]), split(send_ref[...]))


def store_halves(keep_ref, send_ref, index, value):
    middle = value.shape[0] // 2
    keep_ref[index] = value[:middle]
    send_ref[index] = value[middle:]


def parent_kernel(
    children, weight_ref, chooser_ref, left_ref, right_ref, own_ref, links_ref,
    col_ref, turned_ref, keep_ref, send_ref,
):
    sums = jnp.concatenate([left_ref[...], right_ref[...]], axis=1)
    column = -sums * weight_ref[0].astype(F32)
    col_ref[...] = column
    column_pair = split(column)
    parent_pair = split(own_ref[0])
    chooser = chooser_ref[...]
    store_halves(
        keep_ref, send_ref, 0, reordered(chooser, -product(parent_pair, column_pair, TN))
    )
    for c in range(children):
        turned = product(column_pair, split(links_ref[c]))
        turned_ref[c] = turned
        upper = product(parent_pair, split(turned), TN)
        upper -= product(column_pair, split(own_ref[c + 1]), TN)
        store_halves(keep_ref, send_ref, 1 + c, reordered(chooser, upper))


def link_kernel(children, share, own_ref, links_ref, slices_ref, diag_ref, lifted_ref, framed_ref, corner_ref):
    parent_pair = split(own_ref[0])
    diag_pair = split(diag_ref[0])
    for c in range(children):
        link_pair = split(links_ref[c])
        lifted_ref[c] = product(parent_pair, link_pair)
        framed = product(diag_pair, link_pair)
        framed_ref[c] = framed
        corner_ref[c] = share * product(split(slices_ref[c]), split(framed), TN)


def child_kernel(
    children, chooser_ref, own_ref, turned_ref, lifted_ref, corner_ref, *refs
):
    keep_ref, send_ref = refs[-2:]
    for c in range(children):
        own = split(own_ref[c + 1])
        turned = split(turned_ref[c])
        total = corner_ref[c] + refs[c][...]
        total += product(own, turned, TN) + product(turned, own, TN)
        total -= product(split(lifted_ref[c]), turned, TN)
        store_halves(keep_ref, send_ref, c, reordered(chooser_ref[...], total))


def shards(region_inverse, factor_cols, parent_factor, diag_inverse, listed):
    row_count = lax.axis_size("row")
    col_count = lax.axis_size("col")
    row_place = lax.axis_index("row")
    col_place = lax.axis_index("col")
    col_bits = col_count.bit_length() - 1
    rows_here, cols_here = region_inverse.shape
    members, _, width = factor_cols.shape
    children = members - 1
    group = rows_here // col_count
    ratio = col_count // row_count
    diag_width = width // col_count
    part = diag_width // row_count
    first_row = row_place * rows_here
    source = col_place // ratio
    lanes = 2
    unit = width // lanes

    def ring(forward):
        pairs = []
        for col in range(col_count):
            start = col // ratio
            for place in range(row_count):
                at = (start ^ gray(place)) * col_count + col
                to = (start ^ gray((place + 1) % row_count)) * col_count + col
                pairs.append((at, to) if forward else (to, at))
        return pairs

    distance = row_place ^ source
    forward_place = distance
    shift = 1
    while shift < row_count:
        forward_place = forward_place ^ (forward_place >> shift)
        shift *= 2
    backward_place = (row_count - forward_place) % row_count
    places = jnp.stack([forward_place, backward_place]).astype(jnp.int32)
    is_source = row_place == source
    half = cols_here // 2

    relative = jnp.array(reversed_bits(col_count), jnp.int32) ^ col_place
    col_weights = listed[:, col_place * cols_here // width]
    own_weights = listed[:, (first_row + col_place * group) // width]
    group_weights = jnp.take(listed, (first_row + relative * group) // width, axis=1)

    gathered = parent_factor[None]
    for bit in reversed(range(col_bits)):
        gathered = jnp.stack([gathered, swap(gathered, "col", col_count, 1 << bit)], axis=1)
        gathered = gathered.reshape((-1,) + parent_factor.shape)

    first_block = (col_place % ratio)[None]
    info = jnp.concatenate([first_block, col_weights]).astype(jnp.int32)
    chunks = own_chunks(info, factor_cols, (0,), cols_here, lanes)
    source_flag = is_source.astype(jnp.int32)[None]
    moved = [[[], []] for _ in range(lanes)]
    received = [[[], []] for _ in range(lanes)]
    tokens = []
    prepared = []

    def prepare(stage):
        if stage == 0:
            chunks.extend(own_chunks(info, factor_cols, tuple(range(1, members)), cols_here, lanes))
            prepared.append(
                call(
                    functools.partial(region_kernel, col_count),
                    [shape(rows_here, cols_here, dtype=BF16)] * 2,
                    rows_here * cols_here,
                    relative, region_inverse,
                    smem=1,
                )
            )
        elif stage <= children:
            order = jnp.concatenate([relative, group_weights[stage]])
            prepared.append(factor_halves(order, factor_cols, stage, col_count))
        else:
            return []
        return [prepared[-1][0]]

    for stage in range(members + row_count - 2):
        for lane in range(lanes):
            if stage == 0:
                moving = chunks[0][lane]
            else:
                moving = [received[lane][way][-1] for way in range(2)]
                if stage < members:
                    moving = ring_stage(source_flag, chunks[stage][lane], moving, tokens)
                    tokens = [moving[0]]
            for way in range(2):
                moved[lane][way].append(moving[way])
                received[lane][way].append(lax.ppermute(moving[way], AXES, ring(way == 0)))
        tokens = tokens + prepare(stage)

    region, *turned_factors = prepared

    links = call(
        functools.partial(place_kernel, col_count),
        [shape(*parent_factor.shape[:1], width, width)],
        0,
        relative_links(col_count, col_place), gathered,
        smem=1,
    )[0]
    own = lax.dynamic_slice_in_dim(factor_cols, col_place * group, group, 1)
    own = own * own_weights.astype(F32)[:, None, None]

    halving = jnp.array(reversed_bits(col_count), jnp.int32).reshape(2, 1, col_count // 2, 1)
    by_row = lax.iota(jnp.int32, row_count).reshape(1, row_count, 1, 1) ^ row_place
    inner = lax.iota(jnp.int32, part).reshape(1, 1, 1, part)
    wanted = ((halving ^ col_place) * diag_width + by_row * part + inner).reshape(width, 1)
    chooser = (wanted == lax.iota(jnp.int32, width)[None, :]).astype(BF16)

    def column_unit(member, chosen_lanes):
        candidates = []
        for lane in chosen_lanes:
            for way in range(2):
                candidates.append(moved[lane][way][member])
                candidates += received[lane][way][member : member + row_count - 1]
        columns = unit * len(chosen_lanes)
        return call(
            functools.partial(unit_kernel, row_count, len(chosen_lanes)),
            [shape(rows_here // 2, columns)] * 2,
            6 * rows_here * cols_here * columns,
            places, *region, *candidates,
            smem=1,
        )

    def halved(send, keep, sent=None):
        size = keep.shape[0]
        for bit in range(col_bits):
            arrived = swap(send, "col", col_count, 1 << bit)
            if bit + 1 < col_bits:
                size //= 2
                send = keep[size:] + arrived[size:]
                keep = keep[:size] + arrived[:size]
                if sent is not None:
                    sent.append(send)
            else:
                keep = keep + arrived
        return keep

    def total_rows(keep, send):
        value = keep + swap(send, "col", col_count, 1)
        size = value.shape[1] // row_count
        piece = value[:, :size]
        for change in range(1, row_count):
            sent = value[:, change * size : (change + 1) * size]
            piece = piece + swap(sent, "row", row_count, change)
        for bit in range(1, col_bits):
            size //= 2
            piece = piece[:, :size] + swap(piece[:, size:], "col", col_count, 1 << bit)
        pieces = [piece] + [swap(piece, "row", row_count, d) for d in range(1, row_count)]
        stacked = []
        for row in range(row_count):
            chosen = pieces[0]
            for change in range(1, row_count):
                chosen = jnp.where(row_place ^ change == row, pieces[change], chosen)
            stacked.append(chosen)
        return jnp.concatenate(stacked, axis=1)

    parent_sums = []
    for lane in range(lanes):
        keep, send = column_unit(0, [lane])
        parent_sums.append(halved(send, keep))
    child_sums = []
    first_sent = []
    grams = []
    for c in range(children):
        keep, send = column_unit(c + 1, range(lanes))
        sent = []
        child_sums.append(halved(send, keep, sent))
        first_sent.append(sent[0])
        grams += call(
            unit_gram_kernel,
            [shape(width, width)],
            6 * rows_here * width * width,
            *turned_factors[c], keep, send,
        )

    parent_col, turned, keep, send = call(
        functools.partial(parent_kernel, children),
        [shape(group, width), shape(children, group, width)]
        + [shape(members, width // 2, width)] * 2,
        6 * (1 + 3 * children) * group * width * width,
        own_weights, chooser, *parent_sums, own, links,
        smem=1, after=first_sent,
    )
    parent_totals = total_rows(keep, send)

    lifted, framed, corner = call(
        functools.partial(link_kernel, children, 1.0 / row_count),
        [shape(children, group, width), shape(children, diag_width, width),
         shape(children, width, width)],
        6 * children * (group + 2 * diag_width) * width * width,
        own, links, parent_factor, diag_inverse,
    )
    keep, send = call(
        functools.partial(child_kernel, children),
        [shape(children, width // 2, width)] * 2,
        18 * children * group * width * width,
        chooser, own, turned, lifted, corner, *grams,
    )
    child_totals = total_rows(keep, send)

    child_cols = []
    for c in range(children):
        child_cols.append(-(child_sums[c] + turned[c]) * own_weights[c + 1].astype(F32))
    uppers = parent_totals[1:] - framed
    diags = diag_inverse + jnp.concatenate([parent_totals[:1], child_totals])
    return jnp.stack([parent_col] + child_cols), diags, uppers


def solution(mesh):
    in_specs = (
        P("row", "col"),
        P(None, "row", None),
        P(None, "col", None),
        P(None, "col", None),
        P(),
    )
    out_specs = (P(None, ("row", "col"), None), P(None, "col", None), P(None, "col", None))
    return jax.shard_map(shards, mesh=mesh, in_specs=in_specs, out_specs=out_specs, check_vma=False)
```

```python
import functools

import jax
import jax.numpy as jnp
from jax import lax
from jax.experimental import pallas as pl
from jax.experimental.pallas import tpu as pltpu
from jax.sharding import PartitionSpec as P

AXES = ("row", "col")
F32 = jnp.float32
BF16 = jnp.bfloat16
NN = (((1,), (0,)), ((), ()))
NT = (((1,), (1,)), ((), ()))
MIB = 1024 * 1024
WAIT = ("wait",)


def split(value):
    high = value.astype(BF16)
    return high, (value - high.astype(F32)).astype(BF16)


def one_pass(left, right, dims=NN):
    return lax.dot_general(left, right, dims, preferred_element_type=F32)


def product(left, right):
    return one_pass(left[0], right[0]) + (
        one_pass(left[0], right[1]) + one_pass(left[1], right[0])
    )


def turn(chooser, pair):
    return [one_pass(chooser, half, NT).astype(BF16) for half in pair]


def pair_of(high_ref, low_ref, *index):
    return (high_ref[index], low_ref[index]) if index else (high_ref[...], low_ref[...])


def store_pair(high_ref, low_ref, pair, *index):
    index = index if index else ...
    high_ref[index], low_ref[index] = pair


def shape(*dims, dtype=F32):
    return jax.ShapeDtypeStruct(dims, dtype)


def gray(place):
    return place ^ (place >> 1)


def reversed_bits(count):
    order = [0]
    step = 1
    while step < count:
        order = [value + bit * step for value in order for bit in (0, 1)]
        step *= 2
    return order


def swap(value, axis, size, change):
    return lax.ppermute(value, axis, [(place, place ^ change) for place in range(size)])


def call(body, outs, args, smem=0, hbm=0, scratch=(), vmem=8, after=None):
    places = [pltpu.SMEM] * smem + [pltpu.HBM] * hbm
    places += [pltpu.VMEM] * (len(args) - len(places))
    count = len(args)
    args = list(args)
    inner = body
    if after is not None:
        args.append(after)
        places.append(pl.ANY)

        def inner(*refs):
            body(*refs[:count], *refs[count + 1 :])

    results = pl.pallas_call(
        inner,
        out_shape=outs,
        in_specs=[pl.BlockSpec(memory_space=place) for place in places],
        out_specs=[pl.BlockSpec(memory_space=pltpu.VMEM)] * len(outs),
        scratch_shapes=scratch,
        compiler_params=pltpu.CompilerParams(vmem_limit_bytes=vmem * MIB),
        cost_estimate=pl.CostEstimate(flops=1024, bytes_accessed=1024, transcendentals=0),
    )(*args)
    return list(results)


def cut_kernel(members, lanes, info_ref, factors_ref, *refs):
    *outs, sems = refs
    half, unit = outs[0].shape
    first = pl.multiple_of(info_ref[0] * (2 * half), 2 * half)
    copies = []
    for at, out_ref in enumerate(outs):
        member, lane, way = at // (2 * lanes), at // 2 % lanes, at % 2
        source = factors_ref.at[
            member, pl.ds(first + way * half, half), lane * unit : (lane + 1) * unit
        ]
        copies.append(pltpu.make_async_copy(source, out_ref, sems.at[at]))
        copies[-1].start()
    for at, out_ref in enumerate(outs):
        copies[at].wait()
        out_ref[...] = out_ref[...] * info_ref[1 + at // (2 * lanes)].astype(F32)


def fetch_groups(order_ref, source_ref, target_ref, sems, groups):
    size = source_ref.shape[0] // groups
    copies = []
    for g in range(groups):
        start = pl.multiple_of(order_ref[g] * size, size)
        copies.append(
            pltpu.make_async_copy(
                source_ref.at[pl.ds(start, size), :],
                target_ref.at[pl.ds(g * size, size), :],
                sems.at[g],
            )
        )
        copies[-1].start()
    return copies


def region_kernel(groups, order_ref, region_ref, high_ref, low_ref, held_ref, sems):
    size = region_ref.shape[0] // groups
    copies = fetch_groups(order_ref, region_ref, held_ref, sems, groups)
    for g in range(groups):
        copies[g].wait()
        rows = slice(g * size, (g + 1) * size)
        store_pair(high_ref, low_ref, split(held_ref[rows, :]), rows)


def factor_kernel(groups, member, order_ref, factors_ref, chooser_ref, high_ref, low_ref, held_ref, sems):
    size = factors_ref.shape[1] // groups
    copies = fetch_groups(order_ref, factors_ref.at[member], held_ref, sems, groups)
    for g in range(groups):
        copies[g].wait()
        rows = slice(g * size, (g + 1) * size)
        held_ref[rows, :] = held_ref[rows, :] * order_ref[groups + g].astype(F32)
    store_pair(high_ref, low_ref, turn(chooser_ref[...], split(held_ref[...])))


def own_kernel(info_ref, factors_ref, chooser_ref, high_ref, low_ref, thigh_ref, tlow_ref, held_ref, sems):
    members, rows, _ = held_ref.shape
    start = pl.multiple_of(info_ref[0] * rows, rows)
    copies = []
    for j in range(members):
        copies.append(
            pltpu.make_async_copy(
                factors_ref.at[j, pl.ds(start, rows), :], held_ref.at[j], sems.at[j]
            )
        )
        copies[-1].start()
    for j in range(members):
        copies[j].wait()
        pair = split(held_ref[j] * info_ref[1 + j].astype(F32))
        store_pair(high_ref, low_ref, pair, j)
        store_pair(thigh_ref, tlow_ref, turn(chooser_ref[...], pair), j)


def link_kernel(
    groups, children, share, order_ref, gathered_ref, slices_ref, diag_ref, chooser_ref,
    own_high_ref, own_low_ref, high_ref, low_ref, lift_high_ref, lift_low_ref, framed_ref,
    corner_ref, held_ref,
):
    size = slices_ref.shape[1]
    chooser = chooser_ref[...]
    for g in range(groups):
        start = pl.ds(pl.multiple_of(order_ref[g] * size, size), size)
        for c in range(children):
            held_ref[c, start, :] = gathered_ref[g, c]
    for c in range(children):
        pair = split(held_ref[c])
        store_pair(high_ref, low_ref, pair, c)
        lifted = product(pair_of(own_high_ref, own_low_ref, 0), pair)
        store_pair(lift_high_ref, lift_low_ref, turn(chooser, split(lifted)), c)
        framed = product(split(diag_ref[0]), pair)
        framed_ref[c] = framed
        corner_ref[c] = share * product(turn(chooser, split(slices_ref[c])), split(framed))


def unit_kernel(count, place_ref, high_ref, low_ref, *refs):
    keep_ref, send_ref = refs[-2:]
    middle = keep_ref.shape[0]
    chosen = []
    for way in range(2):
        candidates = refs[way * count :][:count]
        value = candidates[0][...]
        for at in range(1, count):
            value = jnp.where(place_ref[way] == at, candidates[at][...], value)
        chosen.append(value)
    right = split(jnp.concatenate(chosen))
    send_ref[...] = product((high_ref[middle:], low_ref[middle:]), right)
    keep_ref[...] = product((high_ref[:middle], low_ref[:middle]), right)


def unit_gram_kernel(high_ref, low_ref, keep_ref, send_ref, out_ref):
    middle = keep_ref.shape[0]
    out_ref[...] = product(
        (high_ref[:, :middle], low_ref[:, :middle]), split(keep_ref[...])
    ) + product((high_ref[:, middle:], low_ref[:, middle:]), split(send_ref[...]))


def store_halves(keep_ref, send_ref, index, value):
    middle = value.shape[0] // 2
    keep_ref[index] = value[:middle]
    send_ref[index] = value[middle:]


def parent_kernel(
    children, weight_ref, chooser_ref, own_high_ref, own_low_ref, own_thigh_ref, own_tlow_ref,
    link_high_ref, link_low_ref, left_ref, right_ref,
    col_ref, turned_ref, high_ref, low_ref, thigh_ref, tlow_ref, keep_ref, send_ref,
):
    chooser = chooser_ref[...]
    column = -jnp.concatenate([left_ref[...], right_ref[...]], axis=1)
    column = column * weight_ref[0].astype(F32)
    col_ref[...] = column
    pair = split(column)
    turned_pair = turn(chooser, pair)
    parent = pair_of(own_thigh_ref, own_tlow_ref, 0)
    store_halves(keep_ref, send_ref, 0, -product(parent, pair))
    for c in range(children):
        turned = product(pair, pair_of(link_high_ref, link_low_ref, c))
        turned_ref[c] = turned
        lifted = split(turned)
        store_pair(high_ref, low_ref, lifted, c)
        store_pair(thigh_ref, tlow_ref, turn(chooser, lifted), c)
        upper = product(parent, lifted) - product(
            turned_pair, pair_of(own_high_ref, own_low_ref, c + 1)
        )
        store_halves(keep_ref, send_ref, 1 + c, upper)


def child_kernel(
    children, lanes, own_high_ref, own_low_ref, own_thigh_ref, own_tlow_ref,
    high_ref, low_ref, thigh_ref, tlow_ref, lift_high_ref, lift_low_ref, corner_ref, *refs
):
    keep_ref, send_ref = refs[-2:]
    for c in range(children):
        grams = [ref[...] for ref in refs[c * lanes : (c + 1) * lanes]]
        turned = pair_of(high_ref, low_ref, c)
        total = corner_ref[c] + jnp.concatenate(grams, axis=1)
        total += product(pair_of(own_thigh_ref, own_tlow_ref, c + 1), turned)
        total += product(
            pair_of(thigh_ref, tlow_ref, c), pair_of(own_high_ref, own_low_ref, c + 1)
        )
        total -= product(pair_of(lift_high_ref, lift_low_ref, c), turned)
        store_halves(keep_ref, send_ref, c, total)


def column_kernel(children, lanes, weight_ref, col_ref, turned_ref, *refs):
    out_ref = refs[-1]
    out_ref[0] = col_ref[...]
    for c in range(children):
        total = jnp.concatenate([ref[...] for ref in refs[c * lanes : (c + 1) * lanes]], axis=1)
        out_ref[c + 1] = -(total + turned_ref[c]) * weight_ref[c + 1].astype(F32)


def finish_kernel(rows, place_ref, diag_ref, framed_ref, *refs):
    parents, offspring = refs[:rows], refs[rows : 2 * rows]
    diags_ref, uppers_ref = refs[2 * rows :]
    part = parents[0].shape[1]

    def chosen(pieces, row):
        value = pieces[0][...]
        for change in range(1, rows):
            value = jnp.where(place_ref[0] ^ change == row, pieces[change][...], value)
        return value

    for row in range(rows):
        at = slice(row * part, (row + 1) * part)
        above, below = chosen(parents, row), chosen(offspring, row)
        diags_ref[0, at] = diag_ref[0, at] + above[0]
        diags_ref[1:, at] = diag_ref[1:, at] + below
        uppers_ref[:, at] = above[1:] - framed_ref[:, at]


def select_step(flag_ref, ins, outs):
    for way in range(2):
        outs[way][...] = jnp.where(flag_ref[0] != 0, ins[way][...], ins[2 + way][...])


def stack_step(flag_ref, ins, outs):
    for at in range(ins[0].shape[0]):
        for side in range(2):
            outs[0][2 * at + side] = ins[side][at]


def halve_step(flag_ref, ins, outs):
    size = outs[0].shape[-2]
    for at, out in enumerate(outs):
        rows = pl.ds(at * size, size)
        index = (rows,) if len(out.shape) == 2 else (slice(None), rows)
        total = ins[0][index]
        for other in ins[1:]:
            total = total + other[index]
        out[...] = total


def step_kernel(tasks, flag_ref, *refs):
    start = 0
    end = sum(ins for _, ins, _ in tasks)
    for body, ins, outs in tasks:
        body(flag_ref, refs[start : start + ins], refs[end : end + outs])
        start += ins
        end += outs


def shards(region_inverse, factor_cols, parent_factor, diag_inverse, listed):
    row_count = lax.axis_size("row")
    col_count = lax.axis_size("col")
    row_place = lax.axis_index("row")
    col_place = lax.axis_index("col")
    col_bits = col_count.bit_length() - 1
    rows_here, cols_here = region_inverse.shape
    members, _, width = factor_cols.shape
    children = members - 1
    group = rows_here // col_count
    ratio = col_count // row_count
    diag_width = width // col_count
    part = diag_width // row_count
    first_row = row_place * rows_here
    source = col_place // ratio
    lanes = 2
    unit = width // lanes
    half = cols_here // 2

    def ring(forward):
        pairs = []
        for col in range(col_count):
            start = col // ratio
            for place in range(row_count):
                at = (start ^ gray(place)) * col_count + col
                to = (start ^ gray((place + 1) % row_count)) * col_count + col
                pairs.append((at, to) if forward else (to, at))
        return pairs

    rings = (ring(True), ring(False))

    column_info = jnp.concatenate(
        [(col_place % ratio)[None], listed[:, col_place * cols_here // width]]
    ).astype(jnp.int32)
    flat = call(
        functools.partial(cut_kernel, members, lanes),
        [shape(half, unit)] * (members * lanes * 2),
        [column_info, factor_cols],
        smem=1, hbm=1, vmem=56,
        scratch=[pltpu.SemaphoreType.DMA((members * lanes * 2,))],
    )
    chunks = [
        [flat[(j * lanes + lane) * 2 :][:2] for lane in range(lanes)] for j in range(members)
    ]

    source_flag = (row_place == source).astype(jnp.int32)[None]
    forward_place = row_place ^ source
    shift = 1
    while shift < row_count:
        forward_place = forward_place ^ (forward_place >> shift)
        shift *= 2
    places = jnp.stack([forward_place, (row_count - forward_place) % row_count]).astype(jnp.int32)

    relative = jnp.array(reversed_bits(col_count), jnp.int32) ^ col_place
    own_weights = listed[:, (first_row + col_place * group) // width]
    own_info = jnp.concatenate([col_place[None], own_weights]).astype(jnp.int32)
    group_weights = jnp.take(listed, (first_row + relative * group) // width, axis=1)

    halving = jnp.array(reversed_bits(col_count), jnp.int32).reshape(2, 1, col_count // 2, 1)
    by_row = lax.iota(jnp.int32, row_count).reshape(1, row_count, 1, 1) ^ row_place
    inner = lax.iota(jnp.int32, part).reshape(1, 1, 1, part)
    wanted = ((halving ^ col_place) * diag_width + by_row * part + inner).reshape(width, 1)
    chooser = (wanted == lax.iota(jnp.int32, width)[None, :]).astype(BF16)

    last = [flat[0]]
    held = {}
    moved = [[] for _ in range(lanes)]
    received = [[] for _ in range(lanes)]

    def heavy(body, outs, args, **options):
        results = call(body, outs, args, after=last[0], **options)
        last[0] = results[0]
        return results

    def ring_flow(lane):
        for _ in range(lane):
            yield WAIT
        stages = members + row_count - 2
        for stage in range(stages):
            arrived = received[lane][-1] if stage else None
            if stage == 0:
                moving = chunks[0][lane]
            elif stage < members:
                moving = yield (select_step, chunks[stage][lane] + arrived, [shape(half, unit)] * 2)
            else:
                yield WAIT
                moving = arrived
            moved[lane].append(moving)
            received[lane].append(
                [lax.ppermute(moving[way], AXES, rings[way]) for way in range(2)]
            )
            for _ in range(lanes - 1):
                yield WAIT
            if stage > row_count - 3:
                held["ready", stage - row_count + 2, lane] = True

    def link_flow():
        gathered = parent_factor[None]
        for bit in reversed(range(col_bits)):
            arrived = swap(gathered, "col", col_count, 1 << bit)
            if bit:
                yield WAIT
            dims = (2 * gathered.shape[0],) + parent_factor.shape
            (gathered,) = yield (stack_step, [gathered, arrived], [shape(*dims)])
        order = jnp.arange(col_count, dtype=jnp.int32) ^ col_place
        held["links"] = heavy(
            functools.partial(link_kernel, col_count, children, 1.0 / row_count),
            [shape(children, width, width, dtype=BF16)] * 2
            + [shape(children, width, group, dtype=BF16)] * 2
            + [shape(children, diag_width, width), shape(children, width, width)],
            [order, gathered, parent_factor, diag_inverse, chooser, *held["own"][:2]],
            smem=1, vmem=20,
            scratch=[pltpu.VMEM((children, width, width), F32)],
        )

    def prepare_flow():
        held["region"] = heavy(
            functools.partial(region_kernel, col_count),
            [shape(rows_here, cols_here, dtype=BF16)] * 2,
            [relative, region_inverse],
            smem=1, hbm=1,
            scratch=[
                pltpu.VMEM((rows_here, cols_here), F32), pltpu.SemaphoreType.DMA((col_count,))
            ],
        )
        yield WAIT
        held["own"] = heavy(
            own_kernel,
            [shape(members, group, width, dtype=BF16)] * 2
            + [shape(members, width, group, dtype=BF16)] * 2,
            [own_info, factor_cols, chooser],
            smem=1, hbm=1,
            scratch=[
                pltpu.VMEM((members, group, width), F32), pltpu.SemaphoreType.DMA((members,))
            ],
        )
        for member in range(1, members):
            yield WAIT
            held["turned", member] = heavy(
                functools.partial(factor_kernel, col_count, member),
                [shape(width, rows_here, dtype=BF16)] * 2,
                [jnp.concatenate([relative, group_weights[member]]), factor_cols, chooser],
                smem=1, hbm=1, vmem=20,
                scratch=[
                    pltpu.VMEM((rows_here, width), F32), pltpu.SemaphoreType.DMA((col_count,))
                ],
            )

    def unit_flow(member, lane):
        while ("ready", member, lane) not in held:
            yield WAIT
        candidates = []
        for way in range(2):
            candidates.append(moved[lane][member][way])
            candidates += [received[lane][member + at][way] for at in range(row_count - 1)]
        size = rows_here // 2
        keep, send = heavy(
            functools.partial(unit_kernel, row_count),
            [shape(size, unit)] * 2,
            [places, *held["region"], *candidates],
            smem=1, vmem=12,
        )
        arrived = swap(send, "col", col_count, 1)
        if member:
            held["gram", member, lane] = heavy(
                unit_gram_kernel,
                [shape(width, unit)],
                [*held["turned", member], keep, send],
                vmem=12,
            )[0]
        yield WAIT
        for bit in range(1, col_bits):
            size //= 2
            keep, send = yield (halve_step, [keep, arrived], [shape(size, unit)] * 2)
            arrived = swap(send, "col", col_count, 1 << bit)
        held["sum", member, lane] = (yield (halve_step, [keep, arrived], [shape(size, unit)]))[0]

    def total_flow(keep, send):
        count = keep.shape[0]
        size = keep.shape[1] // row_count
        arrived = swap(send, "col", col_count, 1)
        pieces = yield (halve_step, [keep, arrived], [shape(count, size, width)] * row_count)
        arrived = [swap(pieces[d], "row", row_count, d) for d in range(1, row_count)]
        inputs = [pieces[0]] + arrived
        for bit in range(1, col_bits):
            size //= 2
            keep, send = yield (halve_step, inputs, [shape(count, size, width)] * 2)
            inputs = [keep, swap(send, "col", col_count, 1 << bit)]
        (piece,) = yield (halve_step, inputs, [shape(count, size, width)])
        return [piece] + [swap(piece, "row", row_count, d) for d in range(1, row_count)]

    def parent_flow():
        names = [("sum", 0, lane) for lane in range(lanes)] + ["links"]
        while any(name not in held for name in names):
            yield WAIT
        col, turned, *pairs, keep, send = heavy(
            functools.partial(parent_kernel, children),
            [shape(group, width), shape(children, group, width)]
            + [shape(children, group, width, dtype=BF16)] * 2
            + [shape(children, width, group, dtype=BF16)] * 2
            + [shape(members, width // 2, width)] * 2,
            [own_weights, chooser, *held["own"], *held["links"][:2]]
            + [held["sum", 0, lane] for lane in range(lanes)],
            smem=1, vmem=20,
        )
        held["parent"] = (col, turned, pairs)
        yield WAIT
        held["parent totals"] = yield from total_flow(keep, send)

    def child_flow():
        names = [("gram", 1 + c, lane) for c in range(children) for lane in range(lanes)]
        while any(name not in held for name in names + ["parent"]):
            yield WAIT
        keep, send = heavy(
            functools.partial(child_kernel, children, lanes),
            [shape(children, width // 2, width)] * 2,
            [*held["own"], *held["parent"][2], *held["links"][2:4], held["links"][5]]
            + [held[name] for name in names],
            vmem=20,
        )
        held["child totals"] = yield from total_flow(keep, send)

    def column_flow():
        names = [("sum", 1 + c, lane) for c in range(children) for lane in range(lanes)]
        while any(name not in held for name in names + ["parent"]):
            yield WAIT
        col, turned, _ = held["parent"]
        held["columns"] = heavy(
            functools.partial(column_kernel, children, lanes),
            [shape(members, group, width)],
            [own_weights, col, turned] + [held[name] for name in names],
            smem=1,
        )[0]

    flows = [ring_flow(lane) for lane in range(lanes)] + [link_flow(), prepare_flow()]
    flows += [unit_flow(j, lane) for j in range(members) for lane in range(lanes)]
    flows += [parent_flow(), child_flow(), column_flow()]
    waiting = [(flow, None) for flow in flows]
    while waiting:
        tasks = [wish for _, wish in waiting if wish not in (None, WAIT)]
        results = iter(())
        if tasks:
            outs = [out for _, _, shapes in tasks for out in shapes]
            args = [value for _, values, _ in tasks for value in values]
            sizes = [(body, len(values), len(shapes)) for body, values, shapes in tasks]
            results = iter(
                heavy(
                    functools.partial(step_kernel, sizes), outs, [source_flag, *args], smem=1
                )
            )
        answered = []
        for flow, wish in waiting:
            answer = None
            if wish not in (None, WAIT):
                answer = [next(results) for _ in wish[2]]
            answered.append((flow, answer))
        waiting = []
        for flow, answer in answered:
            try:
                waiting.append((flow, flow.send(answer)))
            except StopIteration:
                pass

    diags, uppers = heavy(
        functools.partial(finish_kernel, row_count),
        [shape(members, diag_width, width), shape(children, diag_width, width)],
        [row_place[None], diag_inverse, held["links"][4]]
        + held["parent totals"] + held["child totals"],
        smem=1,
    )
    return held["columns"], diags, uppers


def solution(mesh):
    in_specs = (
        P("row", "col"),
        P(None, "row", None),
        P(None, "col", None),
        P(None, "col", None),
        P(),
    )
    out_specs = (P(None, ("row", "col"), None), P(None, "col", None), P(None, "col", None))
    return jax.shard_map(shards, mesh=mesh, in_specs=in_specs, out_specs=out_specs, check_vma=False)
```

```python
import functools

import jax
import jax.numpy as jnp
from jax import lax
from jax.experimental import pallas as pl
from jax.experimental.pallas import tpu as pltpu
from jax.sharding import PartitionSpec as P

AXES = ("row", "col")
F32 = jnp.float32
BF16 = jnp.bfloat16
NN = (((1,), (0,)), ((), ()))
NT = (((1,), (1,)), ((), ()))
MIB = 1024 * 1024
WAIT = ("wait",)


def split(value):
    high = value.astype(BF16)
    return high, (value - high.astype(F32)).astype(BF16)


def one_pass(left, right, dims=NN):
    return lax.dot_general(left, right, dims, preferred_element_type=F32)


def product(left, right):
    return one_pass(left[0], right[0]) + (
        one_pass(left[0], right[1]) + one_pass(left[1], right[0])
    )


def turn(chooser, pair):
    return [one_pass(chooser, half, NT).astype(BF16) for half in pair]


def pair_of(high_ref, low_ref, *index):
    return (high_ref[index], low_ref[index]) if index else (high_ref[...], low_ref[...])


def store_pair(high_ref, low_ref, pair, *index):
    index = index if index else ...
    high_ref[index], low_ref[index] = pair


def shape(*dims, dtype=F32):
    return jax.ShapeDtypeStruct(dims, dtype)


def gray(place):
    return place ^ (place >> 1)


def reversed_bits(count):
    order = [0]
    step = 1
    while step < count:
        order = [value + bit * step for value in order for bit in (0, 1)]
        step *= 2
    return order


def swap(value, axis, size, change):
    return lax.ppermute(value, axis, [(place, place ^ change) for place in range(size)])


def call(body, outs, args, smem=0, hbm=0, scratch=(), vmem=8, after=None):
    places = [pltpu.SMEM] * smem + [pltpu.HBM] * hbm
    places += [pltpu.VMEM] * (len(args) - len(places))
    count = len(args)
    args = list(args)
    inner = body
    if after is not None:
        args.append(after)
        places.append(pl.ANY)

        def inner(*refs):
            body(*refs[:count], *refs[count + 1 :])

    results = pl.pallas_call(
        inner,
        out_shape=outs,
        in_specs=[pl.BlockSpec(memory_space=place) for place in places],
        out_specs=[pl.BlockSpec(memory_space=pltpu.VMEM)] * len(outs),
        scratch_shapes=scratch,
        compiler_params=pltpu.CompilerParams(vmem_limit_bytes=vmem * MIB),
        cost_estimate=pl.CostEstimate(flops=1024, bytes_accessed=1024, transcendentals=0),
    )(*args)
    return list(results)


def cut_kernel(cuts, info_ref, factors_ref, *refs):
    *outs, sems = refs
    half, unit = outs[0].shape
    first = pl.multiple_of(info_ref[0] * (2 * half), 2 * half)
    copies = []
    for at, out_ref in enumerate(outs):
        member, cut, way = at // (2 * cuts), at // 2 % cuts, at % 2
        source = factors_ref.at[
            member, pl.ds(first + way * half, half), cut * unit : (cut + 1) * unit
        ]
        copies.append(pltpu.make_async_copy(source, out_ref, sems.at[at]))
        copies[-1].start()
    for at, out_ref in enumerate(outs):
        copies[at].wait()
        out_ref[...] = out_ref[...] * info_ref[1 + at // (2 * cuts)].astype(F32)


def fetch_groups(order_ref, source_ref, target_ref, sems, groups):
    size = source_ref.shape[0] // groups
    copies = []
    for g in range(groups):
        start = pl.multiple_of(order_ref[g] * size, size)
        copies.append(
            pltpu.make_async_copy(
                source_ref.at[pl.ds(start, size), :],
                target_ref.at[pl.ds(g * size, size), :],
                sems.at[g],
            )
        )
        copies[-1].start()
    return copies


def region_kernel(groups, order_ref, region_ref, high_ref, low_ref, held_ref, sems):
    size = region_ref.shape[0] // groups
    copies = fetch_groups(order_ref, region_ref, held_ref, sems, groups)
    for g in range(groups):
        copies[g].wait()
        rows = slice(g * size, (g + 1) * size)
        store_pair(high_ref, low_ref, split(held_ref[rows, :]), rows)


def factor_kernel(groups, member, order_ref, factors_ref, chooser_ref, high_ref, low_ref, held_ref, sems):
    size = factors_ref.shape[1] // groups
    copies = fetch_groups(order_ref, factors_ref.at[member], held_ref, sems, groups)
    for g in range(groups):
        copies[g].wait()
        rows = slice(g * size, (g + 1) * size)
        held_ref[rows, :] = held_ref[rows, :] * order_ref[groups + g].astype(F32)
    store_pair(high_ref, low_ref, turn(chooser_ref[...], split(held_ref[...])))


def own_kernel(info_ref, factors_ref, chooser_ref, high_ref, low_ref, thigh_ref, tlow_ref, held_ref, sems):
    members, rows, _ = held_ref.shape
    start = pl.multiple_of(info_ref[0] * rows, rows)
    copies = []
    for j in range(members):
        copies.append(
            pltpu.make_async_copy(
                factors_ref.at[j, pl.ds(start, rows), :], held_ref.at[j], sems.at[j]
            )
        )
        copies[-1].start()
    for j in range(members):
        copies[j].wait()
        pair = split(held_ref[j] * info_ref[1 + j].astype(F32))
        store_pair(high_ref, low_ref, pair, j)
        store_pair(thigh_ref, tlow_ref, turn(chooser_ref[...], pair), j)


def link_kernel(
    groups, children, share, order_ref, gathered_ref, slices_ref, diag_ref, chooser_ref,
    own_high_ref, own_low_ref, high_ref, low_ref, lift_high_ref, lift_low_ref, framed_ref,
    corner_ref, held_ref,
):
    size = slices_ref.shape[1]
    chooser = chooser_ref[...]
    for g in range(groups):
        start = pl.ds(pl.multiple_of(order_ref[g] * size, size), size)
        for c in range(children):
            held_ref[c, start, :] = gathered_ref[g, c]
    for c in range(children):
        pair = split(held_ref[c])
        store_pair(high_ref, low_ref, pair, c)
        lifted = product(pair_of(own_high_ref, own_low_ref, 0), pair)
        store_pair(lift_high_ref, lift_low_ref, turn(chooser, split(lifted)), c)
        framed = product(split(diag_ref[0]), pair)
        framed_ref[c] = framed
        corner_ref[c] = share * product(turn(chooser, split(slices_ref[c])), split(framed))


def unit_kernel(count, cuts, place_ref, high_ref, low_ref, *refs):
    keep_ref, send_ref = refs[-2:]
    middle = keep_ref.shape[0]
    for cut in range(cuts):
        chosen = []
        for way in range(2):
            candidates = refs[(2 * cut + way) * count :][:count]
            value = candidates[0][...]
            for at in range(1, count):
                value = jnp.where(place_ref[way] == at, candidates[at][...], value)
            chosen.append(value)
        right = split(jnp.concatenate(chosen))
        unit = right[0].shape[1]
        columns = slice(cut * unit, (cut + 1) * unit)
        send_ref[:, columns] = product((high_ref[middle:], low_ref[middle:]), right)
        keep_ref[:, columns] = product((high_ref[:middle], low_ref[:middle]), right)


def unit_gram_kernel(high_ref, low_ref, keep_ref, send_ref, out_ref):
    middle = keep_ref.shape[0]
    out_ref[...] = product(
        (high_ref[:, :middle], low_ref[:, :middle]), split(keep_ref[...])
    ) + product((high_ref[:, middle:], low_ref[:, middle:]), split(send_ref[...]))


def store_halves(keep_ref, send_ref, index, value):
    middle = value.shape[0] // 2
    keep_ref[index] = value[:middle]
    send_ref[index] = value[middle:]


def parent_kernel(
    children, weight_ref, chooser_ref, own_high_ref, own_low_ref, own_thigh_ref, own_tlow_ref,
    link_high_ref, link_low_ref, sum_ref,
    col_ref, turned_ref, high_ref, low_ref, thigh_ref, tlow_ref, keep_ref, send_ref,
):
    chooser = chooser_ref[...]
    column = -sum_ref[...] * weight_ref[0].astype(F32)
    col_ref[...] = column
    pair = split(column)
    turned_pair = turn(chooser, pair)
    parent = pair_of(own_thigh_ref, own_tlow_ref, 0)
    store_halves(keep_ref, send_ref, 0, -product(parent, pair))
    for c in range(children):
        turned = product(pair, pair_of(link_high_ref, link_low_ref, c))
        turned_ref[c] = turned
        lifted = split(turned)
        store_pair(high_ref, low_ref, lifted, c)
        store_pair(thigh_ref, tlow_ref, turn(chooser, lifted), c)
        upper = product(parent, lifted) - product(
            turned_pair, pair_of(own_high_ref, own_low_ref, c + 1)
        )
        store_halves(keep_ref, send_ref, 1 + c, upper)


def child_kernel(
    children, own_high_ref, own_low_ref, own_thigh_ref, own_tlow_ref,
    high_ref, low_ref, thigh_ref, tlow_ref, lift_high_ref, lift_low_ref, corner_ref, *refs
):
    keep_ref, send_ref = refs[-2:]
    for c in range(children):
        turned = pair_of(high_ref, low_ref, c)
        total = corner_ref[c] + refs[c][...]
        total += product(pair_of(own_thigh_ref, own_tlow_ref, c + 1), turned)
        total += product(
            pair_of(thigh_ref, tlow_ref, c), pair_of(own_high_ref, own_low_ref, c + 1)
        )
        total -= product(pair_of(lift_high_ref, lift_low_ref, c), turned)
        store_halves(keep_ref, send_ref, c, total)


def column_kernel(children, weight_ref, col_ref, turned_ref, *refs):
    out_ref = refs[-1]
    out_ref[0] = col_ref[...]
    for c in range(children):
        out_ref[c + 1] = -(refs[c][...] + turned_ref[c]) * weight_ref[c + 1].astype(F32)


def finish_kernel(rows, place_ref, diag_ref, framed_ref, *refs):
    parents, offspring = refs[:rows], refs[rows : 2 * rows]
    diags_ref, uppers_ref = refs[2 * rows :]
    part = parents[0].shape[1]

    def chosen(pieces, row):
        value = pieces[0][...]
        for change in range(1, rows):
            value = jnp.where(place_ref[0] ^ change == row, pieces[change][...], value)
        return value

    for row in range(rows):
        at = slice(row * part, (row + 1) * part)
        above, below = chosen(parents, row), chosen(offspring, row)
        diags_ref[0, at] = diag_ref[0, at] + above[0]
        diags_ref[1:, at] = diag_ref[1:, at] + below
        uppers_ref[:, at] = above[1:] - framed_ref[:, at]


def select_step(flag_ref, ins, outs):
    for way in range(2):
        outs[way][...] = jnp.where(flag_ref[0] != 0, ins[way][...], ins[2 + way][...])


def stack_step(flag_ref, ins, outs):
    for at in range(ins[0].shape[0]):
        for side in range(2):
            outs[0][2 * at + side] = ins[side][at]


def halve_step(flag_ref, ins, outs):
    size = outs[0].shape[-2]
    for at, out in enumerate(outs):
        rows = pl.ds(at * size, size)
        index = (rows,) if len(out.shape) == 2 else (slice(None), rows)
        total = ins[0][index]
        for other in ins[1:]:
            total = total + other[index]
        out[...] = total


def step_kernel(tasks, flag_ref, *refs):
    start = 0
    end = sum(ins for _, ins, _ in tasks)
    for body, ins, outs in tasks:
        body(flag_ref, refs[start : start + ins], refs[end : end + outs])
        start += ins
        end += outs


def shards(region_inverse, factor_cols, parent_factor, diag_inverse, listed):
    row_count = lax.axis_size("row")
    col_count = lax.axis_size("col")
    row_place = lax.axis_index("row")
    col_place = lax.axis_index("col")
    col_bits = col_count.bit_length() - 1
    rows_here, cols_here = region_inverse.shape
    members, _, width = factor_cols.shape
    children = members - 1
    group = rows_here // col_count
    ratio = col_count // row_count
    diag_width = width // col_count
    part = diag_width // row_count
    first_row = row_place * rows_here
    source = col_place // ratio
    cuts = 2
    unit = width // cuts
    chunk_count = members * cuts
    half = cols_here // 2

    def ring(forward):
        pairs = []
        for col in range(col_count):
            start = col // ratio
            for place in range(row_count):
                at = (start ^ gray(place)) * col_count + col
                to = (start ^ gray((place + 1) % row_count)) * col_count + col
                pairs.append((at, to) if forward else (to, at))
        return pairs

    rings = (ring(True), ring(False))

    column_info = jnp.concatenate(
        [(col_place % ratio)[None], listed[:, col_place * cols_here // width]]
    ).astype(jnp.int32)
    flat = call(
        functools.partial(cut_kernel, cuts),
        [shape(half, unit)] * (chunk_count * 2),
        [column_info, factor_cols],
        smem=1, hbm=1, vmem=48,
        scratch=[pltpu.SemaphoreType.DMA((chunk_count * 2,))],
    )
    chunks = [flat[at * 2 :][:2] for at in range(chunk_count)]

    source_flag = (row_place == source).astype(jnp.int32)[None]
    forward_place = row_place ^ source
    shift = 1
    while shift < row_count:
        forward_place = forward_place ^ (forward_place >> shift)
        shift *= 2
    places = jnp.stack([forward_place, (row_count - forward_place) % row_count]).astype(jnp.int32)

    relative = jnp.array(reversed_bits(col_count), jnp.int32) ^ col_place
    own_weights = listed[:, (first_row + col_place * group) // width]
    own_info = jnp.concatenate([col_place[None], own_weights]).astype(jnp.int32)
    group_weights = jnp.take(listed, (first_row + relative * group) // width, axis=1)

    halving = jnp.array(reversed_bits(col_count), jnp.int32).reshape(2, 1, col_count // 2, 1)
    by_row = lax.iota(jnp.int32, row_count).reshape(1, row_count, 1, 1) ^ row_place
    inner = lax.iota(jnp.int32, part).reshape(1, 1, 1, part)
    wanted = ((halving ^ col_place) * diag_width + by_row * part + inner).reshape(width, 1)
    chooser = (wanted == lax.iota(jnp.int32, width)[None, :]).astype(BF16)

    last = [flat[0]]
    held = {}
    moved = []
    received = []
    stages = chunk_count + row_count - 2

    def heavy(body, outs, args, **options):
        results = call(body, outs, args, after=last[0], **options)
        last[0] = results[0]
        return results

    def ring_flow():
        for stage in range(stages):
            if stage == 0:
                moving = chunks[0]
            elif stage < chunk_count:
                wish = (select_step, chunks[stage] + received[-1], [shape(half, unit)] * 2)
                moving = yield wish
            else:
                moving = received[-1]
                yield WAIT
            moved.append(moving)
            received.append([lax.ppermute(moving[way], AXES, rings[way]) for way in range(2)])

    def link_flow():
        gathered = parent_factor[None]
        for bit in reversed(range(col_bits)):
            arrived = swap(gathered, "col", col_count, 1 << bit)
            if bit:
                yield WAIT
            dims = (2 * gathered.shape[0],) + parent_factor.shape
            (gathered,) = yield (stack_step, [gathered, arrived], [shape(*dims)])
        order = jnp.arange(col_count, dtype=jnp.int32) ^ col_place
        held["links"] = heavy(
            functools.partial(link_kernel, col_count, children, 1.0 / row_count),
            [shape(children, width, width, dtype=BF16)] * 2
            + [shape(children, width, group, dtype=BF16)] * 2
            + [shape(children, diag_width, width), shape(children, width, width)],
            [order, gathered, parent_factor, diag_inverse, chooser, *held["own"][:2]],
            smem=1, vmem=20,
            scratch=[pltpu.VMEM((children, width, width), F32)],
        )

    def prepare_flow():
        held["region"] = heavy(
            functools.partial(region_kernel, col_count),
            [shape(rows_here, cols_here, dtype=BF16)] * 2,
            [relative, region_inverse],
            smem=1, hbm=1,
            scratch=[
                pltpu.VMEM((rows_here, cols_here), F32), pltpu.SemaphoreType.DMA((col_count,))
            ],
        )
        yield WAIT
        held["own"] = heavy(
            own_kernel,
            [shape(members, group, width, dtype=BF16)] * 2
            + [shape(members, width, group, dtype=BF16)] * 2,
            [own_info, factor_cols, chooser],
            smem=1, hbm=1,
            scratch=[
                pltpu.VMEM((members, group, width), F32), pltpu.SemaphoreType.DMA((members,))
            ],
        )
        for member in range(1, members):
            yield WAIT
            held["turned", member] = heavy(
                functools.partial(factor_kernel, col_count, member),
                [shape(width, rows_here, dtype=BF16)] * 2,
                [jnp.concatenate([relative, group_weights[member]]), factor_cols, chooser],
                smem=1, hbm=1, vmem=20,
                scratch=[
                    pltpu.VMEM((rows_here, width), F32), pltpu.SemaphoreType.DMA((col_count,))
                ],
            )

    def unit_flow(member):
        chunk = (member + 1) * cuts - 1
        while len(received) < chunk + row_count - 1:
            yield WAIT
        candidates = []
        for at in range(member * cuts, (member + 1) * cuts):
            for way in range(2):
                candidates.append(moved[at][way])
                candidates += [received[at + hop][way] for hop in range(row_count - 1)]
        size = rows_here // 2
        keep, send = heavy(
            functools.partial(unit_kernel, row_count, cuts),
            [shape(size, width)] * 2,
            [places, *held["region"], *candidates],
            smem=1, vmem=16,
        )
        arrived = swap(send, "col", col_count, 1)
        if member:
            held["gram", member] = heavy(
                unit_gram_kernel,
                [shape(width, width)],
                [*held["turned", member], keep, send],
                vmem=16,
            )[0]
        size //= 2
        keep, send = heavy(
            functools.partial(step_kernel, [(halve_step, 2, 2)]),
            [shape(size, width)] * 2,
            [source_flag, keep, arrived],
            smem=1,
        )
        for bit in range(1, col_bits):
            arrived = swap(send, "col", col_count, 1 << bit)
            if len(received) < stages:
                yield WAIT
            if bit + 1 < col_bits:
                size //= 2
                keep, send = yield (halve_step, [keep, arrived], [shape(size, width)] * 2)
        held["sum", member] = (yield (halve_step, [keep, arrived], [shape(size, width)]))[0]

    def total_flow(keep, send):
        count = keep.shape[0]
        size = keep.shape[1] // row_count
        arrived = swap(send, "col", col_count, 1)
        pieces = yield (halve_step, [keep, arrived], [shape(count, size, width)] * row_count)
        arrived = [swap(pieces[d], "row", row_count, d) for d in range(1, row_count)]
        inputs = [pieces[0]] + arrived
        for bit in range(1, col_bits):
            size //= 2
            keep, send = yield (halve_step, inputs, [shape(count, size, width)] * 2)
            inputs = [keep, swap(send, "col", col_count, 1 << bit)]
        (piece,) = yield (halve_step, inputs, [shape(count, size, width)])
        return [piece] + [swap(piece, "row", row_count, d) for d in range(1, row_count)]

    def parent_flow():
        names = [("sum", 0), "links"]
        while any(name not in held for name in names):
            yield WAIT
        col, turned, *pairs, keep, send = heavy(
            functools.partial(parent_kernel, children),
            [shape(group, width), shape(children, group, width)]
            + [shape(children, group, width, dtype=BF16)] * 2
            + [shape(children, width, group, dtype=BF16)] * 2
            + [shape(members, width // 2, width)] * 2,
            [own_weights, chooser, *held["own"], *held["links"][:2], held["sum", 0]],
            smem=1, vmem=20,
        )
        held["parent"] = (col, turned, pairs)
        held["parent totals"] = yield from total_flow(keep, send)

    def child_flow():
        names = [("gram", 1 + c) for c in range(children)]
        while any(name not in held for name in names + ["parent"]):
            yield WAIT
        keep, send = heavy(
            functools.partial(child_kernel, children),
            [shape(children, width // 2, width)] * 2,
            [*held["own"], *held["parent"][2], *held["links"][2:4], held["links"][5]]
            + [held[name] for name in names],
            vmem=20,
        )
        held["child totals"] = yield from total_flow(keep, send)

    def column_flow():
        names = [("sum", 1 + c) for c in range(children)]
        while any(name not in held for name in names + ["parent"]):
            yield WAIT
        col, turned, _ = held["parent"]
        held["columns"] = heavy(
            functools.partial(column_kernel, children),
            [shape(members, group, width)],
            [own_weights, col, turned] + [held[name] for name in names],
            smem=1,
        )[0]

    flows = [ring_flow(), link_flow(), prepare_flow()]
    flows += [unit_flow(member) for member in range(members)]
    flows += [parent_flow(), child_flow(), column_flow()]
    waiting = [(flow, None) for flow in flows]
    while waiting:
        tasks = [wish for _, wish in waiting if wish not in (None, WAIT)]
        results = iter(())
        if tasks:
            outs = [out for _, _, shapes in tasks for out in shapes]
            args = [value for _, values, _ in tasks for value in values]
            sizes = [(body, len(values), len(shapes)) for body, values, shapes in tasks]
            results = iter(
                heavy(
                    functools.partial(step_kernel, sizes), outs, [source_flag, *args], smem=1
                )
            )
        answered = []
        for flow, wish in waiting:
            answer = None
            if wish not in (None, WAIT):
                answer = [next(results) for _ in wish[2]]
            answered.append((flow, answer))
        waiting = []
        for flow, answer in answered:
            try:
                waiting.append((flow, flow.send(answer)))
            except StopIteration:
                pass

    diags, uppers = heavy(
        functools.partial(finish_kernel, row_count),
        [shape(members, diag_width, width), shape(children, diag_width, width)],
        [row_place[None], diag_inverse, held["links"][4]]
        + held["parent totals"] + held["child totals"],
        smem=1,
    )
    return held["columns"], diags, uppers


def solution(mesh):
    in_specs = (
        P("row", "col"),
        P(None, "row", None),
        P(None, "col", None),
        P(None, "col", None),
        P(),
    )
    out_specs = (P(None, ("row", "col"), None), P(None, "col", None), P(None, "col", None))
    return jax.shard_map(shards, mesh=mesh, in_specs=in_specs, out_specs=out_specs, check_vma=False)
```

```python
import functools

import jax
import jax.numpy as jnp
from jax import lax
from jax.experimental import pallas as pl
from jax.experimental.pallas import tpu as pltpu
from jax.sharding import PartitionSpec as P

AXES = ("row", "col")
F32 = jnp.float32
BF16 = jnp.bfloat16
NN = (((1,), (0,)), ((), ()))
NT = (((1,), (1,)), ((), ()))
MIB = 1024 * 1024
WAIT = ("wait",)


def split(value):
    high = value.astype(BF16)
    return high, (value - high.astype(F32)).astype(BF16)


def one_pass(left, right, dims=NN):
    return lax.dot_general(left, right, dims, preferred_element_type=F32)


def product(left, right):
    return one_pass(left[0], right[0]) + (
        one_pass(left[0], right[1]) + one_pass(left[1], right[0])
    )


def turn(chooser, pair):
    return [one_pass(chooser, half, NT).astype(BF16) for half in pair]


def pair_of(high_ref, low_ref, *index):
    return (high_ref[index], low_ref[index]) if index else (high_ref[...], low_ref[...])


def store_pair(high_ref, low_ref, pair, *index):
    index = index if index else ...
    high_ref[index], low_ref[index] = pair


def shape(*dims, dtype=F32):
    return jax.ShapeDtypeStruct(dims, dtype)


def gray(place):
    return place ^ (place >> 1)


def reversed_bits(count):
    order = [0]
    step = 1
    while step < count:
        order = [value + bit * step for value in order for bit in (0, 1)]
        step *= 2
    return order


def swap(value, axis, size, change):
    return lax.ppermute(value, axis, [(place, place ^ change) for place in range(size)])


def block(index, size):
    return pl.ds(pl.multiple_of(index * size, size), size)


def core_of(info_ref):
    return info_ref[1] & 1


def call(body, outs, args, smem=0, hbm=0, scratch=(), vmem=8, after=None):
    places = [pltpu.SMEM] * smem + [pltpu.HBM] * hbm
    places += [pltpu.VMEM] * (len(args) - len(places))
    count = len(args)
    args = list(args)
    inner = body
    if after is not None:
        args.append(after)
        places.append(pl.ANY)

        def inner(*refs):
            body(*refs[:count], *refs[count + 1 :])

    results = pl.pallas_call(
        inner,
        out_shape=outs,
        in_specs=[pl.BlockSpec(memory_space=place) for place in places],
        out_specs=[pl.BlockSpec(memory_space=pltpu.VMEM)] * len(outs),
        scratch_shapes=scratch,
        compiler_params=pltpu.CompilerParams(vmem_limit_bytes=vmem * MIB),
        cost_estimate=pl.CostEstimate(flops=1024, bytes_accessed=1024, transcendentals=0),
    )(*args)
    return list(results)


def cut_kernel(ratio, cuts, info_ref, listed_ref, factors_ref, *refs):
    *outs, sems = refs
    size, unit = outs[0].shape
    width = factors_ref.shape[2]
    column = info_ref[1]
    pair = (column % ratio) // 2
    copies = []
    for at, out_ref in enumerate(outs):
        member, cut, way = at // (2 * cuts), at // 2 % cuts, at % 2
        source = factors_ref.at[
            member, block(2 * pair + way, size), block(core_of(info_ref) * cuts + cut, unit)
        ]
        copies.append(pltpu.make_async_copy(source, out_ref, sems.at[at]))
        copies[-1].start()
    for at, out_ref in enumerate(outs):
        copies[at].wait()
        owner = column - core_of(info_ref) + at % 2
        weight = listed_ref[at // (2 * cuts), owner * size // width]
        out_ref[...] = out_ref[...] * weight.astype(F32)


def chooser_kernel(rows, columns, info_ref, out_ref):
    width = out_ref.shape[0]
    size = width // columns
    part = size // rows
    place = lax.broadcasted_iota(jnp.int32, out_ref.shape, 0)
    inner = place % part
    core = place // part % 2
    level = place // (2 * part) % (columns // 2)
    by_row = place // (2 * part * (columns // 2))
    turned = jnp.zeros_like(level)
    bits = (columns // 2).bit_length() - 1
    for bit in range(bits):
        turned = turned | (((level >> bit) & 1) << (bits - 1 - bit))
    column = (turned * 2 + core) ^ info_ref[1]
    wanted = column * size + (by_row ^ info_ref[0]) * part + inner
    hit = wanted == lax.broadcasted_iota(jnp.int32, out_ref.shape, 1)
    out_ref[...] = hit.astype(F32).astype(BF16)


def region_kernel(order, info_ref, own_ref, other_ref, high_ref, low_ref, held_ref, sems):
    groups = len(order)
    size = own_ref.shape[0] // groups
    width = own_ref.shape[1]
    column = info_ref[1] >> 1
    copies = []
    for g in range(groups):
        for side, source_ref in enumerate((own_ref, other_ref)):
            copies.append(
                pltpu.make_async_copy(
                    source_ref.at[block(order[g] ^ column, size), :],
                    held_ref.at[side, pl.ds(g * size, size), :],
                    sems.at[side, g],
                )
            )
            copies[-1].start()
    for g in range(groups):
        rows = slice(g * size, (g + 1) * size)
        for side in range(2):
            copies[2 * g + side].wait()
            columns = block(core_of(info_ref) ^ side, width)
            high, low = split(held_ref[side, rows, :])
            high_ref[rows, columns] = high
            low_ref[rows, columns] = low


def factor_kernel(
    order, member, info_ref, listed_ref, factors_ref, chooser_ref, high_ref, low_ref, held_ref, sems
):
    groups = len(order)
    _, rows_here, width = factors_ref.shape
    size = rows_here // groups
    column = info_ref[1] >> 1
    copies = []
    for g in range(groups):
        copies.append(
            pltpu.make_async_copy(
                factors_ref.at[member, block(order[g] ^ column, size), :],
                held_ref.at[pl.ds(g * size, size), :],
                sems.at[g],
            )
        )
        copies[-1].start()
    for g in range(groups):
        copies[g].wait()
        rows = slice(g * size, (g + 1) * size)
        first = info_ref[0] * rows_here + (order[g] ^ column) * size
        held_ref[rows, :] = held_ref[rows, :] * listed_ref[member, first // width].astype(F32)
    store_pair(high_ref, low_ref, turn(chooser_ref[...], split(held_ref[...])))


def own_weight(info_ref, listed_ref, member, size, rows_here, width):
    first = info_ref[0] * rows_here + (info_ref[1] >> 1) * size
    return listed_ref[member, first // width].astype(F32)


def own_kernel(
    info_ref, listed_ref, factors_ref, chooser_ref, high_ref, low_ref, thigh_ref, tlow_ref,
    held_ref, sems,
):
    members, rows, width = held_ref.shape
    copies = []
    for j in range(members):
        copies.append(
            pltpu.make_async_copy(
                factors_ref.at[j, block(info_ref[1] >> 1, rows), :], held_ref.at[j], sems.at[j]
            )
        )
        copies[-1].start()
    for j in range(members):
        copies[j].wait()
        weight = own_weight(info_ref, listed_ref, j, rows, factors_ref.shape[1], width)
        pair = split(held_ref[j] * weight)
        store_pair(high_ref, low_ref, pair, j)
        store_pair(thigh_ref, tlow_ref, turn(chooser_ref[...], pair), j)


def link_kernel(
    children, share, info_ref, gathered_ref, diag_ref, other_ref, chooser_ref,
    own_high_ref, own_low_ref, high_ref, low_ref, lift_high_ref, lift_low_ref, framed_ref,
    corner_ref, held_ref, rows_ref, frame_ref,
):
    groups, _, size, width = gathered_ref.shape
    half = corner_ref.shape[2]
    core = core_of(info_ref)
    chooser = chooser_ref[...]
    for g in range(groups):
        for c in range(children):
            held_ref[c, block(info_ref[1] ^ g, size), :] = gathered_ref[g, c]
    rows_ref[block(core, size), :] = diag_ref[0]
    rows_ref[block(1 - core, size), :] = other_ref[0]
    diag = split(rows_ref[...])
    for c in range(children):
        pair = split(held_ref[c])
        store_pair(high_ref, low_ref, pair, c)
        lifted = product(pair_of(own_high_ref, own_low_ref, 0), pair)
        store_pair(lift_high_ref, lift_low_ref, turn(chooser, split(lifted)), c)
        frame_ref[...] = product(diag, pair)
        framed_ref[c] = frame_ref[block(core, size), :]
        slices = split(held_ref[c, block(info_ref[1] >> 1, 2 * size), :])
        corner = product(turn(chooser, slices), split(frame_ref[:, block(core, half)]))
        corner_ref[c] = share * corner


def unit_kernel(count, ratio, cuts, info_ref, high_ref, low_ref, *refs):
    keep_ref, send_ref = refs[-2:]
    middle = keep_ref.shape[0]
    place = info_ref[0] ^ (info_ref[1] // ratio)
    shift = 1
    while shift < count:
        place = place ^ (place >> shift)
        shift *= 2
    places = (place, (count - place) % count)
    parts = []
    for cut in range(cuts):
        chosen = []
        for way in range(2):
            candidates = refs[(2 * cut + way) * count :][:count]
            value = candidates[0][...]
            for at in range(1, count):
                value = jnp.where(places[way] == at, candidates[at][...], value)
            chosen.append(value)
        parts.append(jnp.concatenate(chosen))
    right = split(jnp.concatenate(parts, axis=1))
    send_ref[...] = product((high_ref[middle:], low_ref[middle:]), right)
    keep_ref[...] = product((high_ref[:middle], low_ref[:middle]), right)


def unit_gram_kernel(high_ref, low_ref, keep_ref, send_ref, out_ref):
    middle = keep_ref.shape[0]
    out_ref[...] = product(
        (high_ref[:, :middle], low_ref[:, :middle]), split(keep_ref[...])
    ) + product((high_ref[:, middle:], low_ref[:, middle:]), split(send_ref[...]))


def store_parts(refs, index, value):
    size = refs[0].shape[1]
    for at, ref in enumerate(refs):
        ref[index] = value[at * size : (at + 1) * size]


def parent_kernel(
    children, rows_here, info_ref, listed_ref, chooser_ref, own_high_ref, own_low_ref,
    own_thigh_ref, own_tlow_ref, link_high_ref, link_low_ref, mine_ref, other_ref,
    col_ref, turned_ref, high_ref, low_ref, thigh_ref, tlow_ref, *refs
):
    *outs, full_ref = refs
    chooser = chooser_ref[...]
    rows, half = mine_ref.shape
    core = core_of(info_ref)
    weight = own_weight(info_ref, listed_ref, 0, rows, rows_here, chooser.shape[0])
    mine = -mine_ref[...] * weight
    full_ref[:, block(core, half)] = mine
    full_ref[:, block(1 - core, half)] = -other_ref[...] * weight
    output_rows = block(core, rows // 2)
    col_ref[...] = full_ref[output_rows, :]
    pair = split(full_ref[...])
    turned_pair = turn(chooser, pair)
    parent = pair_of(own_thigh_ref, own_tlow_ref, 0)
    columns = block(core, half)
    store_parts(outs, 0, -product(parent, split(mine)))
    for c in range(children):
        full_ref[...] = product(pair, pair_of(link_high_ref, link_low_ref, c))
        turned_ref[c] = full_ref[output_rows, :]
        lifted = split(full_ref[:, columns])
        store_pair(high_ref, low_ref, lifted, c)
        store_pair(thigh_ref, tlow_ref, turn(chooser, split(full_ref[...])), c)
        own = (own_high_ref[c + 1, :, columns], own_low_ref[c + 1, :, columns])
        store_parts(outs, 1 + c, product(parent, lifted) - product(turned_pair, own))


def child_kernel(
    children, info_ref, own_high_ref, own_low_ref, own_thigh_ref, own_tlow_ref,
    high_ref, low_ref, thigh_ref, tlow_ref, lift_high_ref, lift_low_ref, corner_ref, *refs
):
    outs = refs[children:]
    columns = block(core_of(info_ref), corner_ref.shape[2])
    for c in range(children):
        lifted = pair_of(high_ref, low_ref, c)
        own = (own_high_ref[c + 1, :, columns], own_low_ref[c + 1, :, columns])
        total = corner_ref[c] + refs[c][...]
        total += product(pair_of(own_thigh_ref, own_tlow_ref, c + 1), lifted)
        total += product(pair_of(thigh_ref, tlow_ref, c), own)
        total -= product(pair_of(lift_high_ref, lift_low_ref, c), lifted)
        store_parts(outs, c, total)


def column_kernel(children, rows_here, info_ref, listed_ref, col_ref, turned_ref, *refs):
    out_ref = refs[-1]
    rows, width = col_ref.shape
    half = width // 2
    core = core_of(info_ref)
    out_ref[0] = col_ref[...]
    for c in range(children):
        weight = own_weight(info_ref, listed_ref, c + 1, 2 * rows, rows_here, width)
        for side in range(2):
            columns = block(core ^ side, half)
            total = refs[2 * c + side][...] + turned_ref[c, :, columns]
            out_ref[c + 1, :, columns] = -total * weight


def finish_kernel(rows, info_ref, diag_ref, framed_ref, *refs):
    parents, offspring = refs[:rows], refs[rows : 2 * rows]
    diags_ref, uppers_ref = refs[2 * rows :]
    part = parents[0].shape[1]

    def chosen(pieces, row):
        value = pieces[0][...]
        for change in range(1, rows):
            value = jnp.where(info_ref[0] ^ change == row, pieces[change][...], value)
        return value

    for row in range(rows):
        at = slice(row * part, (row + 1) * part)
        above, below = chosen(parents, row), chosen(offspring, row)
        diags_ref[0, at] = diag_ref[0, at] + above[0]
        diags_ref[1:, at] = diag_ref[1:, at] + below
        uppers_ref[:, at] = above[1:] - framed_ref[:, at]


def select_step(ratio, info_ref, ins, outs):
    source = info_ref[0] == info_ref[1] // ratio
    for way in range(2):
        outs[way][...] = jnp.where(source, ins[way][...], ins[2 + way][...])


def pass_step(info_ref, ins, outs):
    for way in range(2):
        outs[way][...] = ins[way][...]


def stack_step(info_ref, ins, outs):
    for at in range(ins[0].shape[0]):
        for side in range(2):
            outs[0][2 * at + side] = ins[side][at]


def halve_step(info_ref, ins, outs):
    size = outs[0].shape[-2]
    for at, out in enumerate(outs):
        rows = pl.ds(at * size, size)
        index = (rows,) if len(out.shape) == 2 else (slice(None), rows)
        total = ins[0][index]
        for other in ins[1:]:
            total = total + other[index]
        out[...] = total


def part_step(info_ref, ins, outs):
    size = outs[0].shape[0]
    for side, out in enumerate(outs):
        rows = block(core_of(info_ref) ^ side, size)
        total = ins[0][rows, :]
        for other in ins[1:]:
            total = total + other[rows, :]
        out[...] = total


def join_step(info_ref, ins, outs):
    half = ins[0].shape[-1]
    for side, value in enumerate(ins):
        outs[0][:, :, block(core_of(info_ref) ^ side, half)] = value[...]


def step_kernel(tasks, info_ref, *refs):
    start = 0
    end = sum(ins for _, ins, _ in tasks)
    for body, ins, outs in tasks:
        body(info_ref, refs[start : start + ins], refs[end : end + outs])
        start += ins
        end += outs


def shards(region_inverse, factor_cols, parent_factor, diag_inverse, listed):
    row_count = lax.axis_size("row")
    col_count = lax.axis_size("col")
    col_bits = col_count.bit_length() - 1
    rows_here, cols_here = region_inverse.shape
    members, _, width = factor_cols.shape
    children = members - 1
    levels = col_count // 2
    group = rows_here // levels
    ratio = col_count // row_count
    diag_width = width // col_count
    part = diag_width // row_count
    half = width // 2
    cuts = 2
    unit = half // cuts
    chunk_count = members * cuts
    order = reversed_bits(levels)
    stages = chunk_count + row_count - 2

    def ring(forward):
        pairs = []
        for col in range(col_count):
            start = col // ratio
            for place in range(row_count):
                at = (start ^ gray(place)) * col_count + col
                to = (start ^ gray((place + 1) % row_count)) * col_count + col
                pairs.append((at, to) if forward else (to, at))
        return pairs

    rings = (ring(True), ring(False))
    info = jnp.stack([lax.axis_index("row"), lax.axis_index("col")]).astype(jnp.int32)

    flat = call(
        functools.partial(cut_kernel, ratio, cuts),
        [shape(cols_here, unit)] * (chunk_count * 2),
        [info, listed, factor_cols],
        smem=2, hbm=1, vmem=48,
        scratch=[pltpu.SemaphoreType.DMA((chunk_count * 2,))],
    )
    chunks = [flat[at * 2 :][:2] for at in range(chunk_count)]

    last = [flat[0]]
    held = {}
    moved = []
    received = []

    def heavy(body, outs, args, **options):
        results = call(body, outs, args, after=last[0], **options)
        last[0] = results[0]
        return results

    def ring_flow():
        shapes = [shape(cols_here, unit)] * 2
        for stage in range(stages):
            if stage == 0:
                moving = chunks[0]
            elif stage < chunk_count:
                step = functools.partial(select_step, ratio)
                moving = yield (step, chunks[stage] + received[-1], shapes)
            else:
                moving = yield (pass_step, received[-1], shapes)
            moved.append(moving)
            received.append([lax.ppermute(moving[way], AXES, rings[way]) for way in range(2)])

    def link_flow():
        gathered = parent_factor[None]
        for bit in reversed(range(col_bits)):
            arrived = swap(gathered, "col", col_count, 1 << bit)
            dims = (2 * gathered.shape[0],) + parent_factor.shape
            (gathered,) = yield (stack_step, [gathered, arrived], [shape(*dims)])
        held["links"] = heavy(
            functools.partial(link_kernel, children, 1.0 / row_count),
            [shape(children, width, width, dtype=BF16)] * 2
            + [shape(children, width, group, dtype=BF16)] * 2
            + [shape(children, diag_width, width), shape(children, width, half)],
            [info, gathered, diag_inverse, held["other diag"], held["chooser"], *held["own"][:2]],
            smem=1, vmem=20,
            scratch=[
                pltpu.VMEM((children, width, width), F32),
                pltpu.VMEM((2 * diag_width, width), F32),
                pltpu.VMEM((2 * diag_width, width), F32),
            ],
        )

    def prepare_flow():
        other_region = swap(region_inverse, "col", col_count, 1)
        held["other diag"] = swap(diag_inverse[:1], "col", col_count, 1)
        (held["chooser"],) = heavy(
            functools.partial(chooser_kernel, row_count, col_count),
            [shape(width, width, dtype=BF16)],
            [info],
            smem=1,
        )
        held["own"] = heavy(
            own_kernel,
            [shape(members, group, width, dtype=BF16)] * 2
            + [shape(members, width, group, dtype=BF16)] * 2,
            [info, listed, factor_cols, held["chooser"]],
            smem=2, hbm=1,
            scratch=[
                pltpu.VMEM((members, group, width), F32), pltpu.SemaphoreType.DMA((members,))
            ],
        )
        yield WAIT
        held["region"] = heavy(
            functools.partial(region_kernel, order),
            [shape(rows_here, 2 * cols_here, dtype=BF16)] * 2,
            [info, region_inverse, other_region],
            smem=1, hbm=2, vmem=12,
            scratch=[
                pltpu.VMEM((2, rows_here, cols_here), F32),
                pltpu.SemaphoreType.DMA((2, levels)),
            ],
        )
        for member in range(1, members):
            yield WAIT
            held["turned", member] = heavy(
                functools.partial(factor_kernel, order, member),
                [shape(width, rows_here, dtype=BF16)] * 2,
                [info, listed, factor_cols, held["chooser"]],
                smem=2, hbm=1, vmem=20,
                scratch=[
                    pltpu.VMEM((rows_here, width), F32), pltpu.SemaphoreType.DMA((levels,))
                ],
            )

    def unit_flow(member):
        chunk = (member + 1) * cuts - 1
        while len(received) < chunk + row_count - 1:
            yield WAIT
        candidates = []
        for at in range(member * cuts, (member + 1) * cuts):
            for way in range(2):
                candidates.append(moved[at][way])
                candidates += [received[at + hop][way] for hop in range(row_count - 1)]
        size = rows_here // 2
        keep, send = heavy(
            functools.partial(unit_kernel, row_count, ratio, cuts),
            [shape(size, half)] * 2,
            [info, *held["region"], *candidates],
            smem=1, vmem=16,
        )
        first = (keep, send)
        for bit in range(1, col_bits):
            arrived = swap(send, "col", col_count, 1 << bit)
            if bit == 1:
                yield WAIT
                if member:
                    held["gram", member] = heavy(
                        unit_gram_kernel,
                        [shape(width, half)],
                        [*held["turned", member], *first],
                        vmem=16,
                    )[0]
            if bit + 1 < col_bits:
                size //= 2
                keep, send = yield (halve_step, [keep, arrived], [shape(size, half)] * 2)
        if member == 0:
            (mine,) = yield (halve_step, [keep, arrived], [shape(size, half)])
            other = swap(mine, "col", col_count, 1)
        else:
            mine, theirs = yield (part_step, [keep, arrived], [shape(size // 2, half)] * 2)
            other = swap(theirs, "col", col_count, 1)
        held["sum", member] = [mine, other]

    def total_flow(pieces):
        count, size, _ = pieces[0].shape
        inputs = [pieces[0]] + [swap(pieces[d], "row", row_count, d) for d in range(1, row_count)]
        for bit in [*range(1, col_bits), 0]:
            size //= 2
            keep, send = yield (halve_step, inputs, [shape(count, size, half)] * 2)
            inputs = [keep, swap(send, "col", col_count, 1 << bit)]
        (piece,) = yield (join_step, inputs, [shape(count, size, width)])
        return [piece] + [swap(piece, "row", row_count, d) for d in range(1, row_count)]

    def parent_flow():
        names = [("sum", 0), "links"]
        while any(name not in held for name in names):
            yield WAIT
        col, turned, *rest = heavy(
            functools.partial(parent_kernel, children, rows_here),
            [shape(group // 2, width), shape(children, group // 2, width)]
            + [shape(children, group, half, dtype=BF16)] * 2
            + [shape(children, width, group, dtype=BF16)] * 2
            + [shape(members, width // row_count, half)] * row_count,
            [info, listed, held["chooser"], *held["own"], *held["links"][:2], *held["sum", 0]],
            smem=2, vmem=20,
            scratch=[pltpu.VMEM((group, width), F32)],
        )
        held["parent"] = (col, turned, rest[:4])
        held["parent totals"] = yield from total_flow(rest[4:])

    def child_flow():
        names = [("gram", 1 + c) for c in range(children)]
        while any(name not in held for name in names + ["parent"]):
            yield WAIT
        pieces = heavy(
            functools.partial(child_kernel, children),
            [shape(children, width // row_count, half)] * row_count,
            [info, *held["own"], *held["parent"][2], *held["links"][2:4], held["links"][5]]
            + [held[name] for name in names],
            smem=1, vmem=20,
        )
        held["child totals"] = yield from total_flow(pieces)

    def column_flow():
        names = [("sum", 1 + c) for c in range(children)]
        while any(name not in held for name in names + ["parent"]):
            yield WAIT
        yield WAIT
        col, turned, _ = held["parent"]
        held["columns"] = heavy(
            functools.partial(column_kernel, children, rows_here),
            [shape(members, group // 2, width)],
            [info, listed, col, turned] + [value for name in names for value in held[name]],
            smem=2,
        )[0]

    flows = [ring_flow(), link_flow(), prepare_flow()]
    flows += [unit_flow(member) for member in range(members)]
    flows += [parent_flow(), child_flow(), column_flow()]
    waiting = [(flow, None) for flow in flows]
    while waiting:
        tasks = [wish for _, wish in waiting if wish not in (None, WAIT)]
        results = iter(())
        if tasks:
            outs = [out for _, _, shapes in tasks for out in shapes]
            args = [value for _, values, _ in tasks for value in values]
            sizes = [(body, len(values), len(shapes)) for body, values, shapes in tasks]
            results = iter(
                heavy(functools.partial(step_kernel, sizes), outs, [info, *args], smem=1)
            )
        answered = []
        for flow, wish in waiting:
            answer = None
            if wish not in (None, WAIT):
                answer = [next(results) for _ in wish[2]]
            answered.append((flow, answer))
        waiting = []
        for flow, answer in answered:
            try:
                waiting.append((flow, flow.send(answer)))
            except StopIteration:
                pass

    diags, uppers = heavy(
        functools.partial(finish_kernel, row_count),
        [shape(members, diag_width, width), shape(children, diag_width, width)],
        [info, diag_inverse, held["links"][4]] + held["parent totals"] + held["child totals"],
        smem=1,
    )
    return held["columns"], diags, uppers


def solution(mesh):
    in_specs = (
        P("row", "col"),
        P(None, "row", None),
        P(None, "col", None),
        P(None, "col", None),
        P(),
    )
    out_specs = (P(None, ("row", "col"), None), P(None, "col", None), P(None, "col", None))
    return jax.shard_map(shards, mesh=mesh, in_specs=in_specs, out_specs=out_specs, check_vma=False)
```

```python
import functools

import jax
import jax.numpy as jnp
from jax import lax
from jax.experimental import pallas as pl
from jax.experimental.pallas import tpu as pltpu
from jax.sharding import PartitionSpec as P

AXES = ("row", "col")
F32 = jnp.float32
BF16 = jnp.bfloat16
NN = (((1,), (0,)), ((), ()))
NT = (((1,), (1,)), ((), ()))
MIB = 1024 * 1024
WAIT = ("wait",)


def split(value):
    high = value.astype(BF16)
    return high, (value - high.astype(F32)).astype(BF16)


def one_pass(left, right, dims=NN):
    return lax.dot_general(left, right, dims, preferred_element_type=F32)


def product(left, right):
    return one_pass(left[0], right[0]) + (
        one_pass(left[0], right[1]) + one_pass(left[1], right[0])
    )


def turn(chooser, pair):
    return [one_pass(chooser, half, NT).astype(BF16) for half in pair]


def pair_of(high_ref, low_ref, *index):
    return (high_ref[index], low_ref[index]) if index else (high_ref[...], low_ref[...])


def store_pair(high_ref, low_ref, pair, *index):
    index = index if index else ...
    high_ref[index], low_ref[index] = pair


def shape(*dims, dtype=F32):
    return jax.ShapeDtypeStruct(dims, dtype)


def gray(place):
    return place ^ (place >> 1)


def reversed_bits(count):
    order = [0]
    step = 1
    while step < count:
        order = [value + bit * step for value in order for bit in (0, 1)]
        step *= 2
    return order


def swap(value, axis, size, change):
    return lax.ppermute(value, axis, [(place, place ^ change) for place in range(size)])


def block(index, size):
    return pl.ds(pl.multiple_of(index * size, size), size)


def core_of(info_ref):
    return info_ref[1] & 1


def call(body, outs, args, smem=0, hbm=0, scratch=(), vmem=8, after=None):
    places = [pltpu.SMEM] * smem + [pltpu.HBM] * hbm
    places += [pltpu.VMEM] * (len(args) - len(places))
    count = len(args)
    args = list(args)
    inner = body
    if after is not None:
        args.append(after)
        places.append(pl.ANY)

        def inner(*refs):
            body(*refs[:count], *refs[count + 1 :])

    results = pl.pallas_call(
        inner,
        out_shape=outs,
        in_specs=[pl.BlockSpec(memory_space=place) for place in places],
        out_specs=[pl.BlockSpec(memory_space=pltpu.VMEM)] * len(outs),
        scratch_shapes=scratch,
        compiler_params=pltpu.CompilerParams(vmem_limit_bytes=vmem * MIB),
        cost_estimate=pl.CostEstimate(flops=1024, bytes_accessed=1024, transcendentals=0),
    )(*args)
    return list(results)


def cut_kernel(ratio, cuts, info_ref, listed_ref, factors_ref, slices_ref, *refs):
    *outs, through_ref, sems = refs
    through_ref[0] = slices_ref[...]
    size, unit = outs[0].shape
    width = factors_ref.shape[2]
    column = info_ref[1]
    pair = (column % ratio) // 2
    copies = []
    for at, out_ref in enumerate(outs):
        member, cut, way = at // (2 * cuts), at // 2 % cuts, at % 2
        source = factors_ref.at[
            member, block(2 * pair + way, size), block(core_of(info_ref) * cuts + cut, unit)
        ]
        copies.append(pltpu.make_async_copy(source, out_ref, sems.at[at]))
        copies[-1].start()
    for at, out_ref in enumerate(outs):
        copies[at].wait()
        owner = column - core_of(info_ref) + at % 2
        weight = listed_ref[at // (2 * cuts), owner * size // width]
        out_ref[...] = out_ref[...] * weight.astype(F32)


def chooser_kernel(rows, columns, info_ref, out_ref):
    width = out_ref.shape[0]
    size = width // columns
    part = size // rows
    place = lax.broadcasted_iota(jnp.int32, out_ref.shape, 0)
    inner = place % part
    core = place // part % 2
    level = place // (2 * part) % (columns // 2)
    by_row = place // (2 * part * (columns // 2))
    turned = jnp.zeros_like(level)
    bits = (columns // 2).bit_length() - 1
    for bit in range(bits):
        turned = turned | (((level >> bit) & 1) << (bits - 1 - bit))
    column = (turned * 2 + core) ^ info_ref[1]
    wanted = column * size + (by_row ^ info_ref[0]) * part + inner
    hit = wanted == lax.broadcasted_iota(jnp.int32, out_ref.shape, 1)
    out_ref[...] = hit.astype(F32).astype(BF16)


def region_kernel(order, info_ref, own_ref, other_ref, high_ref, low_ref, held_ref, sems):
    groups = len(order)
    size = own_ref.shape[0] // groups
    width = own_ref.shape[1]
    column = info_ref[1] >> 1
    copies = []
    for g in range(groups):
        for side, source_ref in enumerate((own_ref, other_ref)):
            copies.append(
                pltpu.make_async_copy(
                    source_ref.at[block(order[g] ^ column, size), :],
                    held_ref.at[side, pl.ds(g * size, size), :],
                    sems.at[side, g],
                )
            )
            copies[-1].start()
    for g in range(groups):
        rows = slice(g * size, (g + 1) * size)
        for side in range(2):
            copies[2 * g + side].wait()
            columns = block(core_of(info_ref) ^ side, width)
            high, low = split(held_ref[side, rows, :])
            high_ref[rows, columns] = high
            low_ref[rows, columns] = low


def factor_kernel(
    order, member, info_ref, listed_ref, factors_ref, chooser_ref, high_ref, low_ref, held_ref, sems
):
    groups = len(order)
    _, rows_here, width = factors_ref.shape
    size = rows_here // groups
    column = info_ref[1] >> 1
    copies = []
    for g in range(groups):
        copies.append(
            pltpu.make_async_copy(
                factors_ref.at[member, block(order[g] ^ column, size), :],
                held_ref.at[pl.ds(g * size, size), :],
                sems.at[g],
            )
        )
        copies[-1].start()
    for g in range(groups):
        copies[g].wait()
        rows = slice(g * size, (g + 1) * size)
        first = info_ref[0] * rows_here + (order[g] ^ column) * size
        held_ref[rows, :] = held_ref[rows, :] * listed_ref[member, first // width].astype(F32)
    store_pair(high_ref, low_ref, turn(chooser_ref[...], split(held_ref[...])))


def own_weight(info_ref, listed_ref, member, size, rows_here, width):
    first = info_ref[0] * rows_here + (info_ref[1] >> 1) * size
    return listed_ref[member, first // width].astype(F32)


def own_kernel(
    info_ref, listed_ref, factors_ref, chooser_ref, high_ref, low_ref, thigh_ref, tlow_ref,
    held_ref, sems,
):
    members, rows, width = held_ref.shape
    copies = []
    for j in range(members):
        copies.append(
            pltpu.make_async_copy(
                factors_ref.at[j, block(info_ref[1] >> 1, rows), :], held_ref.at[j], sems.at[j]
            )
        )
        copies[-1].start()
    for j in range(members):
        copies[j].wait()
        weight = own_weight(info_ref, listed_ref, j, rows, factors_ref.shape[1], width)
        pair = split(held_ref[j] * weight)
        store_pair(high_ref, low_ref, pair, j)
        store_pair(thigh_ref, tlow_ref, turn(chooser_ref[...], pair), j)


def link_kernel(
    children, share, info_ref, gathered_ref, diag_ref, other_ref, chooser_ref,
    own_high_ref, own_low_ref, high_ref, low_ref, lift_high_ref, lift_low_ref, framed_ref,
    corner_ref, held_ref, rows_ref, frame_ref,
):
    groups, _, size, width = gathered_ref.shape
    half = corner_ref.shape[2]
    core = core_of(info_ref)
    chooser = chooser_ref[...]
    for g in range(groups):
        for c in range(children):
            held_ref[c, block(info_ref[1] ^ g, size), :] = gathered_ref[g, c]
    rows_ref[block(core, size), :] = diag_ref[0]
    rows_ref[block(1 - core, size), :] = other_ref[0]
    diag = split(rows_ref[...])
    for c in range(children):
        pair = split(held_ref[c])
        store_pair(high_ref, low_ref, pair, c)
        lifted = product(pair_of(own_high_ref, own_low_ref, 0), pair)
        store_pair(lift_high_ref, lift_low_ref, turn(chooser, split(lifted)), c)
        frame_ref[...] = product(diag, pair)
        framed_ref[c] = frame_ref[block(core, size), :]
        slices = split(held_ref[c, block(info_ref[1] >> 1, 2 * size), :])
        corner = product(turn(chooser, slices), split(frame_ref[:, block(core, half)]))
        corner_ref[c] = share * corner


def unit_kernel(count, ratio, cuts, info_ref, high_ref, low_ref, *refs):
    keep_ref, send_ref = refs[-2:]
    middle = keep_ref.shape[0]
    place = info_ref[0] ^ (info_ref[1] // ratio)
    shift = 1
    while shift < count:
        place = place ^ (place >> shift)
        shift *= 2
    places = (place, (count - place) % count)
    parts = []
    for cut in range(cuts):
        chosen = []
        for way in range(2):
            candidates = refs[(2 * cut + way) * count :][:count]
            value = candidates[0][...]
            for at in range(1, count):
                value = jnp.where(places[way] == at, candidates[at][...], value)
            chosen.append(value)
        parts.append(jnp.concatenate(chosen))
    right = split(jnp.concatenate(parts, axis=1))
    send_ref[...] = product((high_ref[middle:], low_ref[middle:]), right)
    keep_ref[...] = product((high_ref[:middle], low_ref[:middle]), right)


def unit_gram_kernel(high_ref, low_ref, keep_ref, send_ref, out_ref):
    middle = keep_ref.shape[0]
    out_ref[...] = product(
        (high_ref[:, :middle], low_ref[:, :middle]), split(keep_ref[...])
    ) + product((high_ref[:, middle:], low_ref[:, middle:]), split(send_ref[...]))


def store_parts(refs, index, value):
    size = refs[0].shape[1]
    for at, ref in enumerate(refs):
        ref[index] = value[at * size : (at + 1) * size]


def parent_kernel(
    children, rows_here, info_ref, listed_ref, chooser_ref, own_high_ref, own_low_ref,
    own_thigh_ref, own_tlow_ref, link_high_ref, link_low_ref, mine_ref, other_ref,
    col_ref, turned_ref, high_ref, low_ref, thigh_ref, tlow_ref, *refs
):
    *outs, full_ref = refs
    chooser = chooser_ref[...]
    rows, half = mine_ref.shape
    core = core_of(info_ref)
    weight = own_weight(info_ref, listed_ref, 0, rows, rows_here, chooser.shape[0])
    mine = -mine_ref[...] * weight
    full_ref[:, block(core, half)] = mine
    full_ref[:, block(1 - core, half)] = -other_ref[...] * weight
    output_rows = block(core, rows // 2)
    col_ref[...] = full_ref[output_rows, :]
    pair = split(full_ref[...])
    turned_pair = turn(chooser, pair)
    parent = pair_of(own_thigh_ref, own_tlow_ref, 0)
    columns = block(core, half)
    store_parts(outs, 0, -product(parent, split(mine)))
    for c in range(children):
        full_ref[...] = product(pair, pair_of(link_high_ref, link_low_ref, c))
        turned_ref[c] = full_ref[output_rows, :]
        lifted = split(full_ref[:, columns])
        store_pair(high_ref, low_ref, lifted, c)
        store_pair(thigh_ref, tlow_ref, turn(chooser, split(full_ref[...])), c)
        own = (own_high_ref[c + 1, :, columns], own_low_ref[c + 1, :, columns])
        store_parts(outs, 1 + c, product(parent, lifted) - product(turned_pair, own))


def child_kernel(
    children, info_ref, own_high_ref, own_low_ref, own_thigh_ref, own_tlow_ref,
    high_ref, low_ref, thigh_ref, tlow_ref, lift_high_ref, lift_low_ref, corner_ref, *refs
):
    outs = refs[children:]
    columns = block(core_of(info_ref), corner_ref.shape[2])
    for c in range(children):
        lifted = pair_of(high_ref, low_ref, c)
        own = (own_high_ref[c + 1, :, columns], own_low_ref[c + 1, :, columns])
        total = corner_ref[c] + refs[c][...]
        total += product(pair_of(own_thigh_ref, own_tlow_ref, c + 1), lifted)
        total += product(pair_of(thigh_ref, tlow_ref, c), own)
        total -= product(pair_of(lift_high_ref, lift_low_ref, c), lifted)
        store_parts(outs, c, total)


def column_kernel(children, rows_here, info_ref, listed_ref, col_ref, turned_ref, *refs):
    out_ref = refs[-1]
    rows, width = col_ref.shape
    half = width // 2
    core = core_of(info_ref)
    out_ref[0] = col_ref[...]
    for c in range(children):
        weight = own_weight(info_ref, listed_ref, c + 1, 2 * rows, rows_here, width)
        for side in range(2):
            columns = block(core ^ side, half)
            total = refs[2 * c + side][...] + turned_ref[c, :, columns]
            out_ref[c + 1, :, columns] = -total * weight


def finish_kernel(rows, info_ref, diag_ref, framed_ref, *refs):
    parents, offspring = refs[:rows], refs[rows : 2 * rows]
    diags_ref, uppers_ref = refs[2 * rows :]
    part = parents[0].shape[1]

    def chosen(pieces, row):
        value = pieces[0][...]
        for change in range(1, rows):
            value = jnp.where(info_ref[0] ^ change == row, pieces[change][...], value)
        return value

    for row in range(rows):
        at = slice(row * part, (row + 1) * part)
        above, below = chosen(parents, row), chosen(offspring, row)
        diags_ref[0, at] = diag_ref[0, at] + above[0]
        diags_ref[1:, at] = diag_ref[1:, at] + below
        uppers_ref[:, at] = above[1:] - framed_ref[:, at]


def select_step(ratio, info_ref, ins, outs):
    source = info_ref[0] == info_ref[1] // ratio
    for way in range(2):
        outs[way][...] = jnp.where(source, ins[way][...], ins[2 + way][...])


def pass_step(info_ref, ins, outs):
    for way in range(2):
        outs[way][...] = ins[way][...]


def stack_step(info_ref, ins, outs):
    for at in range(ins[0].shape[0]):
        for side in range(2):
            outs[0][2 * at + side] = ins[side][at]


def halve_step(info_ref, ins, outs):
    size = outs[0].shape[-2]
    for at, out in enumerate(outs):
        rows = pl.ds(at * size, size)
        index = (rows,) if len(out.shape) == 2 else (slice(None), rows)
        total = ins[0][index]
        for other in ins[1:]:
            total = total + other[index]
        out[...] = total


def part_step(info_ref, ins, outs):
    size = outs[0].shape[0]
    for side, out in enumerate(outs):
        rows = block(core_of(info_ref) ^ side, size)
        total = ins[0][rows, :]
        for other in ins[1:]:
            total = total + other[rows, :]
        out[...] = total


def join_step(info_ref, ins, outs):
    half = ins[0].shape[-1]
    for side, value in enumerate(ins):
        outs[0][:, :, block(core_of(info_ref) ^ side, half)] = value[...]


def step_kernel(tasks, info_ref, *refs):
    start = 0
    end = sum(ins for _, ins, _ in tasks)
    for body, ins, outs in tasks:
        body(info_ref, refs[start : start + ins], refs[end : end + outs])
        start += ins
        end += outs


def shards(region_inverse, factor_cols, parent_factor, diag_inverse, listed):
    row_count = lax.axis_size("row")
    col_count = lax.axis_size("col")
    col_bits = col_count.bit_length() - 1
    rows_here, cols_here = region_inverse.shape
    members, _, width = factor_cols.shape
    children = members - 1
    levels = col_count // 2
    group = rows_here // levels
    ratio = col_count // row_count
    diag_width = width // col_count
    part = diag_width // row_count
    half = width // 2
    cuts = 1
    unit = half // cuts
    chunk_count = members * cuts
    order = reversed_bits(levels)
    stages = chunk_count + row_count - 2

    def ring(forward):
        pairs = []
        for col in range(col_count):
            start = col // ratio
            for place in range(row_count):
                at = (start ^ gray(place)) * col_count + col
                to = (start ^ gray((place + 1) % row_count)) * col_count + col
                pairs.append((at, to) if forward else (to, at))
        return pairs

    rings = (ring(True), ring(False))
    info = jnp.stack([lax.axis_index("row"), lax.axis_index("col")]).astype(jnp.int32)

    flat = call(
        functools.partial(cut_kernel, ratio, cuts),
        [shape(cols_here, unit)] * (chunk_count * 2) + [shape(1, *parent_factor.shape)],
        [info, listed, factor_cols, parent_factor],
        smem=2, hbm=1, vmem=48,
        scratch=[pltpu.SemaphoreType.DMA((chunk_count * 2,))],
    )
    chunks = [flat[at * 2 :][:2] for at in range(chunk_count)]

    last = [flat[0]]
    held = {}
    moved = []
    received = []

    def heavy(body, outs, args, **options):
        results = call(body, outs, args, after=last[0], **options)
        last[0] = results[0]
        return results

    def ring_flow():
        shapes = [shape(cols_here, unit)] * 2
        for stage in range(stages):
            if stage == 0:
                moving = chunks[0]
            elif stage < chunk_count:
                step = functools.partial(select_step, ratio)
                moving = yield (step, chunks[stage] + received[-1], shapes)
            else:
                moving = yield (pass_step, received[-1], shapes)
            moved.append(moving)
            received.append([lax.ppermute(moving[way], AXES, rings[way]) for way in range(2)])

    def link_flow():
        gathered = flat[-1]
        for bit in reversed(range(col_bits)):
            arrived = swap(gathered, "col", col_count, 1 << bit)
            dims = (2 * gathered.shape[0],) + parent_factor.shape
            (gathered,) = yield (stack_step, [gathered, arrived], [shape(*dims)])
        held["links"] = heavy(
            functools.partial(link_kernel, children, 1.0 / row_count),
            [shape(children, width, width, dtype=BF16)] * 2
            + [shape(children, width, group, dtype=BF16)] * 2
            + [shape(children, diag_width, width), shape(children, width, half)],
            [info, gathered, diag_inverse, held["other diag"], held["chooser"], *held["own"][:2]],
            smem=1, vmem=20,
            scratch=[
                pltpu.VMEM((children, width, width), F32),
                pltpu.VMEM((2 * diag_width, width), F32),
                pltpu.VMEM((2 * diag_width, width), F32),
            ],
        )

    def prepare_flow():
        other_region = swap(region_inverse, "col", col_count, 1)
        held["other diag"] = swap(diag_inverse[:1], "col", col_count, 1)
        (held["chooser"],) = heavy(
            functools.partial(chooser_kernel, row_count, col_count),
            [shape(width, width, dtype=BF16)],
            [info],
            smem=1,
        )
        held["own"] = heavy(
            own_kernel,
            [shape(members, group, width, dtype=BF16)] * 2
            + [shape(members, width, group, dtype=BF16)] * 2,
            [info, listed, factor_cols, held["chooser"]],
            smem=2, hbm=1,
            scratch=[
                pltpu.VMEM((members, group, width), F32), pltpu.SemaphoreType.DMA((members,))
            ],
        )
        yield WAIT
        held["region"] = heavy(
            functools.partial(region_kernel, order),
            [shape(rows_here, 2 * cols_here, dtype=BF16)] * 2,
            [info, region_inverse, other_region],
            smem=1, hbm=2, vmem=12,
            scratch=[
                pltpu.VMEM((2, rows_here, cols_here), F32),
                pltpu.SemaphoreType.DMA((2, levels)),
            ],
        )
        for member in range(1, members):
            yield WAIT
            held["turned", member] = heavy(
                functools.partial(factor_kernel, order, member),
                [shape(width, rows_here, dtype=BF16)] * 2,
                [info, listed, factor_cols, held["chooser"]],
                smem=2, hbm=1, vmem=20,
                scratch=[
                    pltpu.VMEM((rows_here, width), F32), pltpu.SemaphoreType.DMA((levels,))
                ],
            )

    def unit_flow(member):
        chunk = (member + 1) * cuts - 1
        while len(received) < chunk + row_count - 1:
            yield WAIT
        candidates = []
        for at in range(member * cuts, (member + 1) * cuts):
            for way in range(2):
                candidates.append(moved[at][way])
                candidates += [received[at + hop][way] for hop in range(row_count - 1)]
        size = rows_here // 2
        keep, send = heavy(
            functools.partial(unit_kernel, row_count, ratio, cuts),
            [shape(size, half)] * 2,
            [info, *held["region"], *candidates],
            smem=1, vmem=16,
        )
        first = (keep, send)
        for bit in range(1, col_bits):
            arrived = swap(send, "col", col_count, 1 << bit)
            if bit == 1:
                yield WAIT
                if member:
                    held["gram", member] = heavy(
                        unit_gram_kernel,
                        [shape(width, half)],
                        [*held["turned", member], *first],
                        vmem=16,
                    )[0]
            if bit + 1 < col_bits:
                size //= 2
                keep, send = yield (halve_step, [keep, arrived], [shape(size, half)] * 2)
        if member == 0:
            (mine,) = yield (halve_step, [keep, arrived], [shape(size, half)])
            other = swap(mine, "col", col_count, 1)
        else:
            mine, theirs = yield (part_step, [keep, arrived], [shape(size // 2, half)] * 2)
            other = swap(theirs, "col", col_count, 1)
        held["sum", member] = [mine, other]

    def total_flow(pieces):
        count, size, _ = pieces[0].shape
        inputs = [pieces[0]] + [swap(pieces[d], "row", row_count, d) for d in range(1, row_count)]
        size //= levels
        pieces = yield (halve_step, inputs, [shape(count, size, half)] * levels)
        inputs = [pieces[0]]
        for at in range(1, levels):
            inputs.append(swap(pieces[at], "col", col_count, order[at] << 1))
        size //= 2
        keep, send = yield (halve_step, inputs, [shape(count, size, half)] * 2)
        inputs = [keep, swap(send, "col", col_count, 1)]
        (piece,) = yield (join_step, inputs, [shape(count, size, width)])
        return [piece] + [swap(piece, "row", row_count, d) for d in range(1, row_count)]

    def parent_flow():
        names = [("sum", 0), "links"]
        while any(name not in held for name in names):
            yield WAIT
        col, turned, *rest = heavy(
            functools.partial(parent_kernel, children, rows_here),
            [shape(group // 2, width), shape(children, group // 2, width)]
            + [shape(children, group, half, dtype=BF16)] * 2
            + [shape(children, width, group, dtype=BF16)] * 2
            + [shape(members, width // row_count, half)] * row_count,
            [info, listed, held["chooser"], *held["own"], *held["links"][:2], *held["sum", 0]],
            smem=2, vmem=20,
            scratch=[pltpu.VMEM((group, width), F32)],
        )
        held["parent"] = (col, turned, rest[:4])
        held["parent totals"] = yield from total_flow(rest[4:])

    def child_flow():
        names = [("gram", 1 + c) for c in range(children)]
        while any(name not in held for name in names + ["parent"]):
            yield WAIT
        pieces = heavy(
            functools.partial(child_kernel, children),
            [shape(children, width // row_count, half)] * row_count,
            [info, *held["own"], *held["parent"][2], *held["links"][2:4], held["links"][5]]
            + [held[name] for name in names],
            smem=1, vmem=20,
        )
        yield WAIT
        held["child totals"] = yield from total_flow(pieces)

    def column_flow():
        names = [("sum", 1 + c) for c in range(children)]
        while any(name not in held for name in names + ["parent"]):
            yield WAIT
        yield WAIT
        col, turned, _ = held["parent"]
        held["columns"] = heavy(
            functools.partial(column_kernel, children, rows_here),
            [shape(members, group // 2, width)],
            [info, listed, col, turned] + [value for name in names for value in held[name]],
            smem=2,
        )[0]

    flows = [ring_flow(), link_flow(), prepare_flow()]
    flows += [unit_flow(member) for member in range(members)]
    flows += [parent_flow(), child_flow(), column_flow()]
    waiting = [(flow, None) for flow in flows]
    while waiting:
        tasks = [wish for _, wish in waiting if wish not in (None, WAIT)]
        results = iter(())
        if tasks:
            outs = [out for _, _, shapes in tasks for out in shapes]
            args = [value for _, values, _ in tasks for value in values]
            sizes = [(body, len(values), len(shapes)) for body, values, shapes in tasks]
            results = iter(
                heavy(functools.partial(step_kernel, sizes), outs, [info, *args], smem=1)
            )
        answered = []
        for flow, wish in waiting:
            answer = None
            if wish not in (None, WAIT):
                answer = [next(results) for _ in wish[2]]
            answered.append((flow, answer))
        waiting = []
        for flow, answer in answered:
            try:
                waiting.append((flow, flow.send(answer)))
            except StopIteration:
                pass

    diags, uppers = heavy(
        functools.partial(finish_kernel, row_count),
        [shape(members, diag_width, width), shape(children, diag_width, width)],
        [info, diag_inverse, held["links"][4]] + held["parent totals"] + held["child totals"],
        smem=1,
    )
    return held["columns"], diags, uppers


def solution(mesh):
    in_specs = (
        P("row", "col"),
        P(None, "row", None),
        P(None, "col", None),
        P(None, "col", None),
        P(),
    )
    out_specs = (P(None, ("row", "col"), None), P(None, "col", None), P(None, "col", None))
    return jax.shard_map(shards, mesh=mesh, in_specs=in_specs, out_specs=out_specs, check_vma=False)
```

```python
import functools

import jax
import jax.numpy as jnp
from jax import lax
from jax.experimental import pallas as pl
from jax.experimental.pallas import tpu as pltpu
from jax.sharding import PartitionSpec as P

AXES = ("row", "col")
F32 = jnp.float32
BF16 = jnp.bfloat16
NN = (((1,), (0,)), ((), ()))
NT = (((1,), (1,)), ((), ()))
MIB = 1024 * 1024
WAIT = ("wait",)


def split(value):
    high = value.astype(BF16)
    return high, (value - high.astype(F32)).astype(BF16)


def one_pass(left, right, dims=NN):
    return lax.dot_general(left, right, dims, preferred_element_type=F32)


def product(left, right):
    return one_pass(left[0], right[0]) + (
        one_pass(left[0], right[1]) + one_pass(left[1], right[0])
    )


def turn(chooser, pair):
    return [one_pass(chooser, half, NT).astype(BF16) for half in pair]


def pair_of(high_ref, low_ref, *index):
    return (high_ref[index], low_ref[index]) if index else (high_ref[...], low_ref[...])


def store_pair(high_ref, low_ref, pair, *index):
    index = index if index else ...
    high_ref[index], low_ref[index] = pair


def shape(*dims, dtype=F32):
    return jax.ShapeDtypeStruct(dims, dtype)


def gray(place):
    return place ^ (place >> 1)


def reversed_bits(count):
    order = [0]
    step = 1
    while step < count:
        order = [value + bit * step for value in order for bit in (0, 1)]
        step *= 2
    return order


def swap(value, axis, size, change):
    return lax.ppermute(value, axis, [(place, place ^ change) for place in range(size)])


def block(index, size):
    return pl.ds(pl.multiple_of(index * size, size), size)


def core_of(info_ref):
    return info_ref[1] & 1


def call(body, outs, args, smem=0, hbm=0, scratch=(), vmem=8, after=None):
    places = [pltpu.SMEM] * smem + [pltpu.HBM] * hbm
    places += [pltpu.VMEM] * (len(args) - len(places))
    count = len(args)
    args = list(args)
    inner = body
    if after is not None:
        args.append(after)
        places.append(pl.ANY)

        def inner(*refs):
            body(*refs[:count], *refs[count + 1 :])

    results = pl.pallas_call(
        inner,
        out_shape=outs,
        in_specs=[pl.BlockSpec(memory_space=place) for place in places],
        out_specs=[pl.BlockSpec(memory_space=pltpu.VMEM)] * len(outs),
        scratch_shapes=scratch,
        compiler_params=pltpu.CompilerParams(vmem_limit_bytes=vmem * MIB),
        cost_estimate=pl.CostEstimate(flops=1024, bytes_accessed=1024, transcendentals=0),
    )(*args)
    return list(results)


def cut_kernel(ratio, cuts, members, info_ref, listed_ref, factors_ref, *refs):
    *outs, sems = refs
    size, unit = outs[0].shape
    width = factors_ref.shape[2]
    column = info_ref[1]
    pair = (column % ratio) // 2
    copies = []
    for at, out_ref in enumerate(outs):
        member, cut, way = members[at // (2 * cuts)], at // 2 % cuts, at % 2
        source = factors_ref.at[
            member, block(2 * pair + way, size), block(core_of(info_ref) * cuts + cut, unit)
        ]
        copies.append(pltpu.make_async_copy(source, out_ref, sems.at[at]))
        copies[-1].start()
    for at, out_ref in enumerate(outs):
        copies[at].wait()
        owner = column - core_of(info_ref) + at % 2
        weight = listed_ref[members[at // (2 * cuts)], owner * size // width]
        out_ref[...] = out_ref[...] * weight.astype(F32)


def chooser_kernel(rows, columns, info_ref, out_ref):
    width = out_ref.shape[0]
    size = width // columns
    part = size // rows
    place = lax.broadcasted_iota(jnp.int32, out_ref.shape, 0)
    inner = place % part
    core = place // part % 2
    level = place // (2 * part) % (columns // 2)
    by_row = place // (2 * part * (columns // 2))
    turned = jnp.zeros_like(level)
    bits = (columns // 2).bit_length() - 1
    for bit in range(bits):
        turned = turned | (((level >> bit) & 1) << (bits - 1 - bit))
    column = (turned * 2 + core) ^ info_ref[1]
    wanted = column * size + (by_row ^ info_ref[0]) * part + inner
    hit = wanted == lax.broadcasted_iota(jnp.int32, out_ref.shape, 1)
    out_ref[...] = hit.astype(F32).astype(BF16)


def region_kernel(order, info_ref, own_ref, other_ref, high_ref, low_ref, held_ref, sems):
    groups = len(order)
    size = own_ref.shape[0] // groups
    width = own_ref.shape[1]
    column = info_ref[1] >> 1
    copies = []
    for g in range(groups):
        for side, source_ref in enumerate((own_ref, other_ref)):
            copies.append(
                pltpu.make_async_copy(
                    source_ref.at[block(order[g] ^ column, size), :],
                    held_ref.at[side, pl.ds(g * size, size), :],
                    sems.at[side, g],
                )
            )
            copies[-1].start()
    for g in range(groups):
        rows = slice(g * size, (g + 1) * size)
        for side in range(2):
            copies[2 * g + side].wait()
            columns = block(core_of(info_ref) ^ side, width)
            high, low = split(held_ref[side, rows, :])
            high_ref[rows, columns] = high
            low_ref[rows, columns] = low


def factor_kernel(
    order, member, info_ref, listed_ref, factors_ref, chooser_ref, high_ref, low_ref, held_ref, sems
):
    groups = len(order)
    _, rows_here, width = factors_ref.shape
    size = rows_here // groups
    column = info_ref[1] >> 1
    copies = []
    for g in range(groups):
        copies.append(
            pltpu.make_async_copy(
                factors_ref.at[member, block(order[g] ^ column, size), :],
                held_ref.at[pl.ds(g * size, size), :],
                sems.at[g],
            )
        )
        copies[-1].start()
    for g in range(groups):
        copies[g].wait()
        rows = slice(g * size, (g + 1) * size)
        first = info_ref[0] * rows_here + (order[g] ^ column) * size
        held_ref[rows, :] = held_ref[rows, :] * listed_ref[member, first // width].astype(F32)
    store_pair(high_ref, low_ref, turn(chooser_ref[...], split(held_ref[...])))


def own_weight(info_ref, listed_ref, member, size, rows_here, width):
    first = info_ref[0] * rows_here + (info_ref[1] >> 1) * size
    return listed_ref[member, first // width].astype(F32)


def own_kernel(
    info_ref, listed_ref, factors_ref, chooser_ref, high_ref, low_ref, thigh_ref, tlow_ref,
    held_ref, sems,
):
    members, rows, width = held_ref.shape
    copies = []
    for j in range(members):
        copies.append(
            pltpu.make_async_copy(
                factors_ref.at[j, block(info_ref[1] >> 1, rows), :], held_ref.at[j], sems.at[j]
            )
        )
        copies[-1].start()
    for j in range(members):
        copies[j].wait()
        weight = own_weight(info_ref, listed_ref, j, rows, factors_ref.shape[1], width)
        pair = split(held_ref[j] * weight)
        store_pair(high_ref, low_ref, pair, j)
        store_pair(thigh_ref, tlow_ref, turn(chooser_ref[...], pair), j)


def link_kernel(
    children, share, info_ref, gathered_ref, diag_ref, other_ref, chooser_ref,
    own_high_ref, own_low_ref, high_ref, low_ref, lift_high_ref, lift_low_ref, framed_ref,
    corner_ref, held_ref, rows_ref, frame_ref,
):
    groups, _, size, width = gathered_ref.shape
    half = corner_ref.shape[2]
    core = core_of(info_ref)
    chooser = chooser_ref[...]
    for g in range(groups):
        for c in range(children):
            held_ref[c, block(info_ref[1] ^ g, size), :] = gathered_ref[g, c]
    rows_ref[block(core, size), :] = diag_ref[0]
    rows_ref[block(1 - core, size), :] = other_ref[0]
    diag = split(rows_ref[...])
    for c in range(children):
        pair = split(held_ref[c])
        store_pair(high_ref, low_ref, pair, c)
        lifted = product(pair_of(own_high_ref, own_low_ref, 0), pair)
        store_pair(lift_high_ref, lift_low_ref, turn(chooser, split(lifted)), c)
        frame_ref[...] = product(diag, pair)
        framed_ref[c] = frame_ref[block(core, size), :]
        slices = split(held_ref[c, block(info_ref[1] >> 1, 2 * size), :])
        corner = product(turn(chooser, slices), split(frame_ref[:, block(core, half)]))
        corner_ref[c] = share * corner


def unit_kernel(count, ratio, cuts, info_ref, high_ref, low_ref, *refs):
    keep_ref, send_ref = refs[-2:]
    middle = keep_ref.shape[0]
    place = info_ref[0] ^ (info_ref[1] // ratio)
    shift = 1
    while shift < count:
        place = place ^ (place >> shift)
        shift *= 2
    places = (place, (count - place) % count)
    parts = []
    for cut in range(cuts):
        chosen = []
        for way in range(2):
            candidates = refs[(2 * cut + way) * count :][:count]
            value = candidates[0][...]
            for at in range(1, count):
                value = jnp.where(places[way] == at, candidates[at][...], value)
            chosen.append(value)
        parts.append(jnp.concatenate(chosen))
    right = split(jnp.concatenate(parts, axis=1))
    send_ref[...] = product((high_ref[middle:], low_ref[middle:]), right)
    keep_ref[...] = product((high_ref[:middle], low_ref[:middle]), right)


def unit_gram_kernel(high_ref, low_ref, keep_ref, send_ref, out_ref):
    middle = keep_ref.shape[0]
    out_ref[...] = product(
        (high_ref[:, :middle], low_ref[:, :middle]), split(keep_ref[...])
    ) + product((high_ref[:, middle:], low_ref[:, middle:]), split(send_ref[...]))


def store_parts(refs, index, value):
    size = refs[0].shape[1]
    for at, ref in enumerate(refs):
        ref[index] = value[at * size : (at + 1) * size]


def parent_kernel(
    children, rows_here, info_ref, listed_ref, chooser_ref, own_high_ref, own_low_ref,
    own_thigh_ref, own_tlow_ref, link_high_ref, link_low_ref, mine_ref, other_ref,
    col_ref, turned_ref, high_ref, low_ref, *refs
):
    *outs, full_ref = refs
    chooser = chooser_ref[...]
    rows, half = mine_ref.shape
    core = core_of(info_ref)
    weight = own_weight(info_ref, listed_ref, 0, rows, rows_here, chooser.shape[0])
    mine = -mine_ref[...] * weight
    full_ref[:, block(core, half)] = mine
    full_ref[:, block(1 - core, half)] = -other_ref[...] * weight
    output_rows = block(core, rows // 2)
    col_ref[...] = full_ref[output_rows, :]
    pair = split(full_ref[...])
    turned_pair = turn(chooser, pair)
    parent = pair_of(own_thigh_ref, own_tlow_ref, 0)
    columns = block(core, half)
    store_parts(outs, 0, -product(parent, split(mine)))
    for c in range(children):
        full_ref[...] = product(pair, pair_of(link_high_ref, link_low_ref, c))
        turned_ref[c] = full_ref[output_rows, :]
        lifted = split(full_ref[:, columns])
        store_pair(high_ref, low_ref, split(full_ref[...]), c)
        own = (own_high_ref[c + 1, :, columns], own_low_ref[c + 1, :, columns])
        store_parts(outs, 1 + c, product(parent, lifted) - product(turned_pair, own))


def child_kernel(
    children, info_ref, chooser_ref, own_high_ref, own_low_ref, own_thigh_ref, own_tlow_ref,
    high_ref, low_ref, lift_high_ref, lift_low_ref, corner_ref, *refs
):
    outs = refs[children:]
    columns = block(core_of(info_ref), corner_ref.shape[2])
    for c in range(children):
        lifted = (high_ref[c, :, columns], low_ref[c, :, columns])
        turned_pair = turn(chooser_ref[...], pair_of(high_ref, low_ref, c))
        own = (own_high_ref[c + 1, :, columns], own_low_ref[c + 1, :, columns])
        total = corner_ref[c] + refs[c][...]
        total += product(pair_of(own_thigh_ref, own_tlow_ref, c + 1), lifted)
        total += product(turned_pair, own)
        total -= product(pair_of(lift_high_ref, lift_low_ref, c), lifted)
        store_parts(outs, c, total)


def column_kernel(children, rows_here, info_ref, listed_ref, col_ref, turned_ref, *refs):
    out_ref = refs[-1]
    rows, width = col_ref.shape
    half = width // 2
    core = core_of(info_ref)
    out_ref[0] = col_ref[...]
    for c in range(children):
        weight = own_weight(info_ref, listed_ref, c + 1, 2 * rows, rows_here, width)
        for side in range(2):
            columns = block(core ^ side, half)
            total = refs[2 * c + side][...] + turned_ref[c, :, columns]
            out_ref[c + 1, :, columns] = -total * weight


def finish_kernel(rows, info_ref, diag_ref, framed_ref, *refs):
    parents, offspring = refs[:rows], refs[rows : 2 * rows]
    diags_ref, uppers_ref = refs[2 * rows :]
    part = parents[0].shape[1]

    def chosen(pieces, row):
        value = pieces[0][...]
        for change in range(1, rows):
            value = jnp.where(info_ref[0] ^ change == row, pieces[change][...], value)
        return value

    for row in range(rows):
        at = slice(row * part, (row + 1) * part)
        above, below = chosen(parents, row), chosen(offspring, row)
        diags_ref[0, at] = diag_ref[0, at] + above[0]
        diags_ref[1:, at] = diag_ref[1:, at] + below
        uppers_ref[:, at] = above[1:] - framed_ref[:, at]


def select_step(ratio, info_ref, ins, outs):
    source = info_ref[0] == info_ref[1] // ratio
    for way in range(2):
        outs[way][...] = jnp.where(source, ins[way][...], ins[2 + way][...])


def pass_step(info_ref, ins, outs):
    for way in range(2):
        outs[way][...] = ins[way][...]


def stack_step(info_ref, ins, outs):
    for at in range(ins[0].shape[0]):
        for side in range(2):
            outs[0][2 * at + side] = ins[side][at]


def halve_step(info_ref, ins, outs):
    size = outs[0].shape[-2]
    for at, out in enumerate(outs):
        rows = pl.ds(at * size, size)
        index = (rows,) if len(out.shape) == 2 else (slice(None), rows)
        total = ins[0][index]
        for other in ins[1:]:
            total = total + other[index]
        out[...] = total


def part_step(info_ref, ins, outs):
    size = outs[0].shape[0]
    for side, out in enumerate(outs):
        rows = block(core_of(info_ref) ^ side, size)
        total = ins[0][rows, :]
        for other in ins[1:]:
            total = total + other[rows, :]
        out[...] = total


def join_step(info_ref, ins, outs):
    half = ins[0].shape[-1]
    for side, value in enumerate(ins):
        outs[0][:, :, block(core_of(info_ref) ^ side, half)] = value[...]


def step_kernel(tasks, info_ref, *refs):
    start = 0
    end = sum(ins for _, ins, _ in tasks)
    for body, ins, outs in tasks:
        body(info_ref, refs[start : start + ins], refs[end : end + outs])
        start += ins
        end += outs


def shards(region_inverse, factor_cols, parent_factor, diag_inverse, listed):
    row_count = lax.axis_size("row")
    col_count = lax.axis_size("col")
    col_bits = col_count.bit_length() - 1
    rows_here, cols_here = region_inverse.shape
    members, _, width = factor_cols.shape
    children = members - 1
    levels = col_count // 2
    group = rows_here // levels
    ratio = col_count // row_count
    diag_width = width // col_count
    part = diag_width // row_count
    half = width // 2
    cuts = 1
    unit = half // cuts
    chunk_count = members * cuts
    order = reversed_bits(levels)
    stages = chunk_count + row_count - 2

    def ring(forward):
        pairs = []
        for col in range(col_count):
            start = col // ratio
            for place in range(row_count):
                at = (start ^ gray(place)) * col_count + col
                to = (start ^ gray((place + 1) % row_count)) * col_count + col
                pairs.append((at, to) if forward else (to, at))
        return pairs

    rings = (ring(True), ring(False))
    info = jnp.stack([lax.axis_index("row"), lax.axis_index("col")]).astype(jnp.int32)

    def cut(chosen, run):
        count = len(chosen) * cuts * 2
        flat = run(
            functools.partial(cut_kernel, ratio, cuts, chosen),
            [shape(cols_here, unit)] * count,
            [info, listed, factor_cols],
            smem=2, hbm=1, vmem=48,
            scratch=[pltpu.SemaphoreType.DMA((count,))],
        )
        return [flat[at : at + 2] for at in range(0, count, 2)]

    chunks = cut((0,), call)

    last = [chunks[0][0]]
    held = {}
    moved = []
    received = []

    def heavy(body, outs, args, **options):
        results = call(body, outs, args, after=last[0], **options)
        last[0] = results[0]
        return results

    chunks.extend(cut(tuple(range(1, members)), heavy))

    def ring_flow():
        shapes = [shape(cols_here, unit)] * 2
        for stage in range(stages):
            if stage == 0:
                moving = chunks[0]
            elif stage < chunk_count:
                step = functools.partial(select_step, ratio)
                moving = yield (step, chunks[stage] + received[-1], shapes)
            else:
                moving = yield (pass_step, received[-1], shapes)
            moved.append(moving)
            received.append([lax.ppermute(moving[way], AXES, rings[way]) for way in range(2)])

    def link_flow():
        gathered = parent_factor[None]
        for bit in reversed(range(col_bits)):
            arrived = swap(gathered, "col", col_count, 1 << bit)
            dims = (2 * gathered.shape[0],) + parent_factor.shape
            (gathered,) = yield (stack_step, [gathered, arrived], [shape(*dims)])
        held["links"] = heavy(
            functools.partial(link_kernel, children, 1.0 / row_count),
            [shape(children, width, width, dtype=BF16)] * 2
            + [shape(children, width, group, dtype=BF16)] * 2
            + [shape(children, diag_width, width), shape(children, width, half)],
            [info, gathered, diag_inverse, held["other diag"], held["chooser"], *held["own"][:2]],
            smem=1, vmem=20,
            scratch=[
                pltpu.VMEM((children, width, width), F32),
                pltpu.VMEM((2 * diag_width, width), F32),
                pltpu.VMEM((2 * diag_width, width), F32),
            ],
        )

    def prepare_flow():
        other_region = swap(region_inverse, "col", col_count, 1)
        held["other diag"] = swap(diag_inverse[:1], "col", col_count, 1)
        (held["chooser"],) = heavy(
            functools.partial(chooser_kernel, row_count, col_count),
            [shape(width, width, dtype=BF16)],
            [info],
            smem=1,
        )
        held["own"] = heavy(
            own_kernel,
            [shape(members, group, width, dtype=BF16)] * 2
            + [shape(members, width, group, dtype=BF16)] * 2,
            [info, listed, factor_cols, held["chooser"]],
            smem=2, hbm=1,
            scratch=[
                pltpu.VMEM((members, group, width), F32), pltpu.SemaphoreType.DMA((members,))
            ],
        )
        yield WAIT
        held["region"] = heavy(
            functools.partial(region_kernel, order),
            [shape(rows_here, 2 * cols_here, dtype=BF16)] * 2,
            [info, region_inverse, other_region],
            smem=1, hbm=2, vmem=12,
            scratch=[
                pltpu.VMEM((2, rows_here, cols_here), F32),
                pltpu.SemaphoreType.DMA((2, levels)),
            ],
        )
        for member in range(1, members):
            yield WAIT
            held["turned", member] = heavy(
                functools.partial(factor_kernel, order, member),
                [shape(width, rows_here, dtype=BF16)] * 2,
                [info, listed, factor_cols, held["chooser"]],
                smem=2, hbm=1, vmem=20,
                scratch=[
                    pltpu.VMEM((rows_here, width), F32), pltpu.SemaphoreType.DMA((levels,))
                ],
            )

    def unit_flow(member):
        chunk = (member + 1) * cuts - 1
        while len(received) < chunk + row_count - 1:
            yield WAIT
        final = member == members - 1
        if not final:
            yield WAIT
        candidates = []
        for at in range(member * cuts, (member + 1) * cuts):
            for way in range(2):
                candidates.append(moved[at][way])
                candidates += [received[at + hop][way] for hop in range(row_count - 1)]
        size = rows_here // 2
        keep, send = heavy(
            functools.partial(unit_kernel, row_count, ratio, cuts),
            [shape(size, half)] * 2,
            [info, *held["region"], *candidates],
            smem=1, vmem=16,
        )
        first = (keep, send)
        for bit in range(1, col_bits):
            arrived = swap(send, "col", col_count, 1 << bit)
            if bit == 1:
                if final:
                    yield WAIT
                if member:
                    held["gram", member] = heavy(
                        unit_gram_kernel,
                        [shape(width, half)],
                        [*held["turned", member], *first],
                        vmem=16,
                    )[0]
            if bit + 1 < col_bits:
                size //= 2
                keep, send = yield (halve_step, [keep, arrived], [shape(size, half)] * 2)
        if member == 0:
            held["last", 0] = [keep, arrived]
            return
        mine, theirs = yield (part_step, [keep, arrived], [shape(size // 2, half)] * 2)
        held["sum", member] = [mine, swap(theirs, "col", col_count, 1)]

    def total_flow(pieces):
        count, size, _ = pieces[0].shape
        inputs = [pieces[0]] + [swap(pieces[d], "row", row_count, d) for d in range(1, row_count)]
        size //= levels
        pieces = yield (halve_step, inputs, [shape(count, size, half)] * levels)
        inputs = [pieces[0]]
        for at in range(1, levels):
            inputs.append(swap(pieces[at], "col", col_count, order[at] << 1))
        size //= 2
        keep, send = yield (halve_step, inputs, [shape(count, size, half)] * 2)
        inputs = [keep, swap(send, "col", col_count, 1)]
        (piece,) = yield (join_step, inputs, [shape(count, size, width)])
        return [piece] + [swap(piece, "row", row_count, d) for d in range(1, row_count)]

    def parent_flow():
        names = [("last", 0), "links"]
        while any(name not in held for name in names):
            yield WAIT
        (mine,) = heavy(
            functools.partial(step_kernel, [(halve_step, 2, 1)]),
            [shape(group, half)],
            [info, *held["last", 0]],
            smem=1,
        )
        other = swap(mine, "col", col_count, 1)
        col, turned, *rest = heavy(
            functools.partial(parent_kernel, children, rows_here),
            [shape(group // 2, width), shape(children, group // 2, width)]
            + [shape(children, group, width, dtype=BF16)] * 2
            + [shape(members, width // row_count, half)] * row_count,
            [info, listed, held["chooser"], *held["own"], *held["links"][:2], mine, other],
            smem=2, vmem=20,
            scratch=[pltpu.VMEM((group, width), F32)],
        )
        held["parent"] = (col, turned, rest[:2])
        yield WAIT
        held["parent totals"] = yield from total_flow(rest[2:])

    def child_flow():
        names = [("gram", 1 + c) for c in range(children)]
        while any(name not in held for name in names + ["parent"]):
            yield WAIT
        pieces = heavy(
            functools.partial(child_kernel, children),
            [shape(children, width // row_count, half)] * row_count,
            [info, held["chooser"], *held["own"], *held["parent"][2], *held["links"][2:4]]
            + [held["links"][5]]
            + [held[name] for name in names],
            smem=1, vmem=20,
        )
        yield WAIT
        held["child totals"] = yield from total_flow(pieces)

    def column_flow():
        names = [("sum", 1 + c) for c in range(children)]
        while any(name not in held for name in names + ["parent"]):
            yield WAIT
        yield WAIT
        col, turned, _ = held["parent"]
        held["columns"] = heavy(
            functools.partial(column_kernel, children, rows_here),
            [shape(members, group // 2, width)],
            [info, listed, col, turned] + [value for name in names for value in held[name]],
            smem=2,
        )[0]

    flows = [ring_flow()] + [unit_flow(member) for member in range(children)]
    flows += [link_flow(), prepare_flow(), parent_flow()]
    flows += [unit_flow(children), child_flow(), column_flow()]
    waiting = [(flow, None) for flow in flows]
    while waiting:
        tasks = [wish for _, wish in waiting if wish not in (None, WAIT)]
        results = iter(())
        if tasks:
            outs = [out for _, _, shapes in tasks for out in shapes]
            args = [value for _, values, _ in tasks for value in values]
            sizes = [(body, len(values), len(shapes)) for body, values, shapes in tasks]
            results = iter(
                heavy(functools.partial(step_kernel, sizes), outs, [info, *args], smem=1)
            )
        answered = []
        for flow, wish in waiting:
            answer = None
            if wish not in (None, WAIT):
                answer = [next(results) for _ in wish[2]]
            answered.append((flow, answer))
        waiting = []
        for flow, answer in answered:
            try:
                waiting.append((flow, flow.send(answer)))
            except StopIteration:
                pass

    diags, uppers = heavy(
        functools.partial(finish_kernel, row_count),
        [shape(members, diag_width, width), shape(children, diag_width, width)],
        [info, diag_inverse, held["links"][4]] + held["parent totals"] + held["child totals"],
        smem=1,
    )
    return held["columns"], diags, uppers


def solution(mesh):
    in_specs = (
        P("row", "col"),
        P(None, "row", None),
        P(None, "col", None),
        P(None, "col", None),
        P(),
    )
    out_specs = (P(None, ("row", "col"), None), P(None, "col", None), P(None, "col", None))
    return jax.shard_map(shards, mesh=mesh, in_specs=in_specs, out_specs=out_specs, check_vma=False)
```

```python
import functools

import jax
import jax.numpy as jnp
from jax import lax
from jax.experimental import pallas as pl
from jax.experimental.pallas import tpu as pltpu
from jax.sharding import PartitionSpec as P

AXES = ("row", "col")
F32 = jnp.float32
BF16 = jnp.bfloat16
NN = (((1,), (0,)), ((), ()))
NT = (((1,), (1,)), ((), ()))
MIB = 1024 * 1024
WAIT = ("wait",)


def split(value):
    high = value.astype(BF16)
    return high, (value - high.astype(F32)).astype(BF16)


def one_pass(left, right, dims=NN):
    return lax.dot_general(left, right, dims, preferred_element_type=F32)


def product(left, right):
    return one_pass(left[0], right[0]) + (
        one_pass(left[0], right[1]) + one_pass(left[1], right[0])
    )


def turn(chooser, pair):
    return [one_pass(chooser, half, NT).astype(BF16) for half in pair]


def pair_of(high_ref, low_ref, *index):
    return (high_ref[index], low_ref[index]) if index else (high_ref[...], low_ref[...])


def store_pair(high_ref, low_ref, pair, *index):
    index = index if index else ...
    high_ref[index], low_ref[index] = pair


def shape(*dims, dtype=F32):
    return jax.ShapeDtypeStruct(dims, dtype)


def gray(place):
    return place ^ (place >> 1)


def reversed_bits(count):
    order = [0]
    step = 1
    while step < count:
        order = [value + bit * step for value in order for bit in (0, 1)]
        step *= 2
    return order


def swap(value, axis, size, change):
    return lax.ppermute(value, axis, [(place, place ^ change) for place in range(size)])


def block(index, size):
    return pl.ds(pl.multiple_of(index * size, size), size)


def core_of(info_ref):
    return info_ref[1] & 1


def call(body, outs, args, smem=0, hbm=0, scratch=(), vmem=8, after=None):
    places = [pltpu.SMEM] * smem + [pltpu.HBM] * hbm
    places += [pltpu.VMEM] * (len(args) - len(places))
    count = len(args)
    args = list(args)
    inner = body
    if after is not None:
        args.append(after)
        places.append(pl.ANY)

        def inner(*refs):
            body(*refs[:count], *refs[count + 1 :])

    results = pl.pallas_call(
        inner,
        out_shape=outs,
        in_specs=[pl.BlockSpec(memory_space=place) for place in places],
        out_specs=[pl.BlockSpec(memory_space=pltpu.VMEM)] * len(outs),
        scratch_shapes=scratch,
        compiler_params=pltpu.CompilerParams(vmem_limit_bytes=vmem * MIB),
        cost_estimate=pl.CostEstimate(flops=1024, bytes_accessed=1024, transcendentals=0),
    )(*args)
    return list(results)


def cut_kernel(ratio, cuts, members, info_ref, listed_ref, factors_ref, *refs):
    *outs, sems = refs
    size, unit = outs[0].shape
    width = factors_ref.shape[2]
    column = info_ref[1]
    pair = (column % ratio) // 2
    copies = []
    for at, out_ref in enumerate(outs):
        member, cut, way = members[at // (2 * cuts)], at // 2 % cuts, at % 2
        source = factors_ref.at[
            member, block(2 * pair + way, size), block(core_of(info_ref) * cuts + cut, unit)
        ]
        copies.append(pltpu.make_async_copy(source, out_ref, sems.at[at]))
        copies[-1].start()
    for at, out_ref in enumerate(outs):
        copies[at].wait()
        owner = column - core_of(info_ref) + at % 2
        weight = listed_ref[members[at // (2 * cuts)], owner * size // width]
        out_ref[...] = out_ref[...] * weight.astype(F32)


def chooser_kernel(rows, columns, info_ref, out_ref):
    width = out_ref.shape[0]
    size = width // columns
    part = size // rows
    place = lax.broadcasted_iota(jnp.int32, out_ref.shape, 0)
    column = place // part % columns
    by_row = place // (part * columns)
    wanted = column * size + (by_row ^ info_ref[0]) * part + place % part
    hit = wanted == lax.broadcasted_iota(jnp.int32, out_ref.shape, 1)
    out_ref[...] = hit.astype(F32).astype(BF16)


def region_kernel(order, info_ref, own_ref, other_ref, high_ref, low_ref, held_ref, sems):
    groups = len(order)
    size = own_ref.shape[0] // groups
    width = own_ref.shape[1]
    column = info_ref[1] >> 1
    copies = []
    for g in range(groups):
        for side, source_ref in enumerate((own_ref, other_ref)):
            copies.append(
                pltpu.make_async_copy(
                    source_ref.at[block(order[g] ^ column, size), :],
                    held_ref.at[side, pl.ds(g * size, size), :],
                    sems.at[side, g],
                )
            )
            copies[-1].start()
    for g in range(groups):
        rows = slice(g * size, (g + 1) * size)
        for side in range(2):
            copies[2 * g + side].wait()
            columns = block(core_of(info_ref) ^ side, width)
            high, low = split(held_ref[side, rows, :])
            high_ref[rows, columns] = high
            low_ref[rows, columns] = low


def factor_kernel(
    order, member, info_ref, listed_ref, factors_ref, chooser_ref, high_ref, low_ref, held_ref, sems
):
    groups = len(order)
    _, rows_here, width = factors_ref.shape
    size = rows_here // groups
    column = info_ref[1] >> 1
    copies = []
    for g in range(groups):
        copies.append(
            pltpu.make_async_copy(
                factors_ref.at[member, block(order[g] ^ column, size), :],
                held_ref.at[pl.ds(g * size, size), :],
                sems.at[g],
            )
        )
        copies[-1].start()
    for g in range(groups):
        copies[g].wait()
        rows = slice(g * size, (g + 1) * size)
        first = info_ref[0] * rows_here + (order[g] ^ column) * size
        held_ref[rows, :] = held_ref[rows, :] * listed_ref[member, first // width].astype(F32)
    store_pair(high_ref, low_ref, turn(chooser_ref[...], split(held_ref[...])))


def own_weight(info_ref, listed_ref, member, size, rows_here, width):
    first = info_ref[0] * rows_here + (info_ref[1] >> 1) * size
    return listed_ref[member, first // width].astype(F32)


def own_kernel(
    info_ref, listed_ref, factors_ref, chooser_ref, high_ref, low_ref, thigh_ref, tlow_ref,
    held_ref, sems,
):
    members, rows, width = held_ref.shape
    copies = []
    for j in range(members):
        copies.append(
            pltpu.make_async_copy(
                factors_ref.at[j, block(info_ref[1] >> 1, rows), :], held_ref.at[j], sems.at[j]
            )
        )
        copies[-1].start()
    for j in range(members):
        copies[j].wait()
        weight = own_weight(info_ref, listed_ref, j, rows, factors_ref.shape[1], width)
        pair = split(held_ref[j] * weight)
        store_pair(high_ref, low_ref, pair, j)
        store_pair(thigh_ref, tlow_ref, turn(chooser_ref[...], pair), j)


def link_kernel(
    children, share, info_ref, gathered_ref, diag_ref, other_ref, chooser_ref,
    own_high_ref, own_low_ref, high_ref, low_ref, lift_high_ref, lift_low_ref, framed_ref,
    corner_ref, held_ref, rows_ref, frame_ref,
):
    groups, _, size, width = gathered_ref.shape
    half = corner_ref.shape[2]
    core = core_of(info_ref)
    chooser = chooser_ref[...]
    for g in range(groups):
        for c in range(children):
            held_ref[c, block(info_ref[1] ^ g, size), :] = gathered_ref[g, c]
    rows_ref[block(core, size), :] = diag_ref[0]
    rows_ref[block(1 - core, size), :] = other_ref[0]
    diag = split(rows_ref[...])
    for c in range(children):
        pair = split(held_ref[c])
        store_pair(high_ref, low_ref, pair, c)
        lifted = product(pair_of(own_high_ref, own_low_ref, 0), pair)
        store_pair(lift_high_ref, lift_low_ref, turn(chooser, split(lifted)), c)
        frame_ref[...] = product(diag, pair)
        framed_ref[c] = frame_ref[block(core, size), :]
        slices = split(held_ref[c, block(info_ref[1] >> 1, 2 * size), :])
        corner = product(turn(chooser, slices), split(frame_ref[:, block(core, half)]))
        corner_ref[c] = share * corner


def unit_kernel(count, ratio, cuts, info_ref, high_ref, low_ref, *refs):
    keep_ref, send_ref = refs[-2:]
    middle = keep_ref.shape[0]
    place = info_ref[0] ^ (info_ref[1] // ratio)
    shift = 1
    while shift < count:
        place = place ^ (place >> shift)
        shift *= 2
    places = (place, (count - place) % count)
    parts = []
    for cut in range(cuts):
        chosen = []
        for way in range(2):
            candidates = refs[(2 * cut + way) * count :][:count]
            value = candidates[0][...]
            for at in range(1, count):
                value = jnp.where(places[way] == at, candidates[at][...], value)
            chosen.append(value)
        parts.append(jnp.concatenate(chosen))
    right = split(jnp.concatenate(parts, axis=1))
    send_ref[...] = product((high_ref[middle:], low_ref[middle:]), right)
    keep_ref[...] = product((high_ref[:middle], low_ref[:middle]), right)


def unit_gram_kernel(high_ref, low_ref, keep_ref, send_ref, out_ref):
    middle = keep_ref.shape[0]
    out_ref[...] = product(
        (high_ref[:, :middle], low_ref[:, :middle]), split(keep_ref[...])
    ) + product((high_ref[:, middle:], low_ref[:, middle:]), split(send_ref[...]))


def store_parts(refs, index, value):
    size = refs[0].shape[1]
    for at, ref in enumerate(refs):
        ref[index] = value[at * size : (at + 1) * size]


def parent_kernel(
    children, rows_here, info_ref, listed_ref, chooser_ref, own_high_ref, own_low_ref,
    own_thigh_ref, own_tlow_ref, link_high_ref, link_low_ref, mine_ref, other_ref,
    col_ref, turned_ref, high_ref, low_ref, *refs
):
    *outs, full_ref = refs
    chooser = chooser_ref[...]
    rows, half = mine_ref.shape
    core = core_of(info_ref)
    weight = own_weight(info_ref, listed_ref, 0, rows, rows_here, chooser.shape[0])
    mine = -mine_ref[...] * weight
    full_ref[:, block(core, half)] = mine
    full_ref[:, block(1 - core, half)] = -other_ref[...] * weight
    output_rows = block(core, rows // 2)
    col_ref[...] = full_ref[output_rows, :]
    pair = split(full_ref[...])
    turned_pair = turn(chooser, pair)
    parent = pair_of(own_thigh_ref, own_tlow_ref, 0)
    columns = block(core, half)
    store_parts(outs, 0, -product(parent, split(mine)))
    for c in range(children):
        full_ref[...] = product(pair, pair_of(link_high_ref, link_low_ref, c))
        turned_ref[c] = full_ref[output_rows, :]
        lifted = split(full_ref[:, columns])
        store_pair(high_ref, low_ref, split(full_ref[...]), c)
        own = (own_high_ref[c + 1, :, columns], own_low_ref[c + 1, :, columns])
        store_parts(outs, 1 + c, product(parent, lifted) - product(turned_pair, own))


def child_kernel(
    children, info_ref, chooser_ref, own_high_ref, own_low_ref, own_thigh_ref, own_tlow_ref,
    high_ref, low_ref, lift_high_ref, lift_low_ref, corner_ref, *refs
):
    outs = refs[children:]
    columns = block(core_of(info_ref), corner_ref.shape[2])
    for c in range(children):
        lifted = (high_ref[c, :, columns], low_ref[c, :, columns])
        turned_pair = turn(chooser_ref[...], pair_of(high_ref, low_ref, c))
        own = (own_high_ref[c + 1, :, columns], own_low_ref[c + 1, :, columns])
        total = corner_ref[c] + refs[c][...]
        total += product(pair_of(own_thigh_ref, own_tlow_ref, c + 1), lifted)
        total += product(turned_pair, own)
        total -= product(pair_of(lift_high_ref, lift_low_ref, c), lifted)
        store_parts(outs, c, total)


def column_kernel(children, rows_here, info_ref, listed_ref, col_ref, turned_ref, *refs):
    out_ref = refs[-1]
    rows, width = col_ref.shape
    half = width // 2
    core = core_of(info_ref)
    out_ref[0] = col_ref[...]
    for c in range(children):
        weight = own_weight(info_ref, listed_ref, c + 1, 2 * rows, rows_here, width)
        for side in range(2):
            columns = block(core ^ side, half)
            total = refs[2 * c + side][...] + turned_ref[c, :, columns]
            out_ref[c + 1, :, columns] = -total * weight


def finish_kernel(rows, info_ref, diag_ref, framed_ref, *refs):
    parents, offspring = refs[:rows], refs[rows : 2 * rows]
    diags_ref, uppers_ref = refs[2 * rows :]
    part = parents[0].shape[1]

    def chosen(pieces, row):
        value = pieces[0][...]
        for change in range(1, rows):
            value = jnp.where(info_ref[0] ^ change == row, pieces[change][...], value)
        return value

    for row in range(rows):
        at = slice(row * part, (row + 1) * part)
        above, below = chosen(parents, row), chosen(offspring, row)
        diags_ref[0, at] = diag_ref[0, at] + above[0]
        diags_ref[1:, at] = diag_ref[1:, at] + below
        uppers_ref[:, at] = above[1:] - framed_ref[:, at]


def select_step(ratio, info_ref, ins, outs):
    source = info_ref[0] == info_ref[1] // ratio
    for way in range(2):
        outs[way][...] = jnp.where(source, ins[way][...], ins[2 + way][...])


def pass_step(info_ref, ins, outs):
    for way in range(2):
        outs[way][...] = ins[way][...]


def stack_step(info_ref, ins, outs):
    for at in range(ins[0].shape[0]):
        for side in range(2):
            outs[0][2 * at + side] = ins[side][at]


def halve_step(info_ref, ins, outs):
    size = outs[0].shape[-2]
    for at, out in enumerate(outs):
        rows = pl.ds(at * size, size)
        index = (rows,) if len(out.shape) == 2 else (slice(None), rows)
        total = ins[0][index]
        for other in ins[1:]:
            total = total + other[index]
        out[...] = total


def part_step(info_ref, ins, outs):
    size = outs[0].shape[0]
    for side, out in enumerate(outs):
        rows = block(core_of(info_ref) ^ side, size)
        total = ins[0][rows, :]
        for other in ins[1:]:
            total = total + other[rows, :]
        out[...] = total


def pieces_step(info_ref, ins, outs):
    columns, _, size, _ = outs[0].shape
    for at in range(columns):
        rows = pl.ds(at * size, size)
        total = ins[0][:, rows]
        for other in ins[1:]:
            total = total + other[:, rows]
        outs[0][at] = total


def join_step(info_ref, ins, outs):
    columns, _, _, half = ins[0].shape
    for core in range(2):
        total = ins[0][core]
        for at in range(2 + core, columns, 2):
            total = total + ins[0][at]
        outs[0][:, :, core * half : (core + 1) * half] = total


def step_kernel(tasks, info_ref, *refs):
    start = 0
    end = sum(ins for _, ins, _ in tasks)
    for body, ins, outs in tasks:
        body(info_ref, refs[start : start + ins], refs[end : end + outs])
        start += ins
        end += outs


def shards(region_inverse, factor_cols, parent_factor, diag_inverse, listed):
    row_count = lax.axis_size("row")
    col_count = lax.axis_size("col")
    col_bits = col_count.bit_length() - 1
    rows_here, cols_here = region_inverse.shape
    members, _, width = factor_cols.shape
    children = members - 1
    levels = col_count // 2
    group = rows_here // levels
    ratio = col_count // row_count
    diag_width = width // col_count
    part = diag_width // row_count
    half = width // 2
    cuts = 1
    unit = half // cuts
    chunk_count = members * cuts
    order = reversed_bits(levels)
    stages = chunk_count + row_count - 2

    def ring(forward):
        pairs = []
        for col in range(col_count):
            start = col // ratio
            for place in range(row_count):
                at = (start ^ gray(place)) * col_count + col
                to = (start ^ gray((place + 1) % row_count)) * col_count + col
                pairs.append((at, to) if forward else (to, at))
        return pairs

    rings = (ring(True), ring(False))
    info = jnp.stack([lax.axis_index("row"), lax.axis_index("col")]).astype(jnp.int32)

    def cut(chosen, run):
        count = len(chosen) * cuts * 2
        flat = run(
            functools.partial(cut_kernel, ratio, cuts, chosen),
            [shape(cols_here, unit)] * count,
            [info, listed, factor_cols],
            smem=2, hbm=1, vmem=48,
            scratch=[pltpu.SemaphoreType.DMA((count,))],
        )
        return [flat[at : at + 2] for at in range(0, count, 2)]

    chunks = cut((0,), call)

    last = [chunks[0][0]]
    held = {}
    moved = []
    received = []

    def heavy(body, outs, args, **options):
        results = call(body, outs, args, after=last[0], **options)
        last[0] = results[0]
        return results

    chunks.extend(cut(tuple(range(1, members)), heavy))

    def ring_flow():
        shapes = [shape(cols_here, unit)] * 2
        for stage in range(stages):
            if stage == 0:
                moving = chunks[0]
            elif stage < chunk_count:
                step = functools.partial(select_step, ratio)
                moving = yield (step, chunks[stage] + received[-1], shapes)
            else:
                moving = yield (pass_step, received[-1], shapes)
            moved.append(moving)
            received.append([lax.ppermute(moving[way], AXES, rings[way]) for way in range(2)])

    def link_flow():
        gathered = parent_factor[None]
        for bit in reversed(range(col_bits)):
            arrived = swap(gathered, "col", col_count, 1 << bit)
            dims = (2 * gathered.shape[0],) + parent_factor.shape
            (gathered,) = yield (stack_step, [gathered, arrived], [shape(*dims)])
        held["links"] = heavy(
            functools.partial(link_kernel, children, 1.0 / row_count),
            [shape(children, width, width, dtype=BF16)] * 2
            + [shape(children, width, group, dtype=BF16)] * 2
            + [shape(children, diag_width, width), shape(children, width, half)],
            [info, gathered, diag_inverse, held["other diag"], held["chooser"], *held["own"][:2]],
            smem=1, vmem=20,
            scratch=[
                pltpu.VMEM((children, width, width), F32),
                pltpu.VMEM((2 * diag_width, width), F32),
                pltpu.VMEM((2 * diag_width, width), F32),
            ],
        )

    def prepare_flow():
        other_region = swap(region_inverse, "col", col_count, 1)
        held["other diag"] = swap(diag_inverse[:1], "col", col_count, 1)
        (held["chooser"],) = heavy(
            functools.partial(chooser_kernel, row_count, col_count),
            [shape(width, width, dtype=BF16)],
            [info],
            smem=1,
        )
        held["own"] = heavy(
            own_kernel,
            [shape(members, group, width, dtype=BF16)] * 2
            + [shape(members, width, group, dtype=BF16)] * 2,
            [info, listed, factor_cols, held["chooser"]],
            smem=2, hbm=1,
            scratch=[
                pltpu.VMEM((members, group, width), F32), pltpu.SemaphoreType.DMA((members,))
            ],
        )
        yield WAIT
        held["region"] = heavy(
            functools.partial(region_kernel, order),
            [shape(rows_here, 2 * cols_here, dtype=BF16)] * 2,
            [info, region_inverse, other_region],
            smem=1, hbm=2, vmem=12,
            scratch=[
                pltpu.VMEM((2, rows_here, cols_here), F32),
                pltpu.SemaphoreType.DMA((2, levels)),
            ],
        )
        for member in range(1, members):
            yield WAIT
            held["turned", member] = heavy(
                functools.partial(factor_kernel, order, member),
                [shape(width, rows_here, dtype=BF16)] * 2,
                [info, listed, factor_cols, held["chooser"]],
                smem=2, hbm=1, vmem=20,
                scratch=[
                    pltpu.VMEM((rows_here, width), F32), pltpu.SemaphoreType.DMA((levels,))
                ],
            )

    def unit_flow(member):
        chunk = (member + 1) * cuts - 1
        while len(received) < chunk + row_count - 1:
            yield WAIT
        final = member == members - 1
        if not final:
            yield WAIT
        candidates = []
        for at in range(member * cuts, (member + 1) * cuts):
            for way in range(2):
                candidates.append(moved[at][way])
                candidates += [received[at + hop][way] for hop in range(row_count - 1)]
        size = rows_here // 2
        keep, send = heavy(
            functools.partial(unit_kernel, row_count, ratio, cuts),
            [shape(size, half)] * 2,
            [info, *held["region"], *candidates],
            smem=1, vmem=16,
        )
        first = (keep, send)
        for bit in range(1, col_bits):
            arrived = swap(send, "col", col_count, 1 << bit)
            if bit == 1:
                if final:
                    yield WAIT
                if member:
                    held["gram", member] = heavy(
                        unit_gram_kernel,
                        [shape(width, half)],
                        [*held["turned", member], *first],
                        vmem=16,
                    )[0]
            if bit + 1 < col_bits:
                size //= 2
                keep, send = yield (halve_step, [keep, arrived], [shape(size, half)] * 2)
        if member == 0:
            held["last", 0] = [keep, arrived]
            return
        mine, theirs = yield (part_step, [keep, arrived], [shape(size // 2, half)] * 2)
        held["sum", member] = [mine, swap(theirs, "col", col_count, 1)]

    def total_flow(pieces):
        count, size, _ = pieces[0].shape
        inputs = [pieces[0]] + [swap(pieces[d], "row", row_count, d) for d in range(1, row_count)]
        (sent,) = yield (pieces_step, inputs, [shape(col_count, count, part, half)])
        arrived = lax.all_to_all(sent, "col", 0, 0, tiled=True)
        (piece,) = yield (join_step, [arrived], [shape(count, part, width)])
        return [piece] + [swap(piece, "row", row_count, d) for d in range(1, row_count)]

    def parent_flow():
        names = [("last", 0), "links"]
        while any(name not in held for name in names):
            yield WAIT
        (mine,) = heavy(
            functools.partial(step_kernel, [(halve_step, 2, 1)]),
            [shape(group, half)],
            [info, *held["last", 0]],
            smem=1,
        )
        other = swap(mine, "col", col_count, 1)
        col, turned, *rest = heavy(
            functools.partial(parent_kernel, children, rows_here),
            [shape(group // 2, width), shape(children, group // 2, width)]
            + [shape(children, group, width, dtype=BF16)] * 2
            + [shape(members, width // row_count, half)] * row_count,
            [info, listed, held["chooser"], *held["own"], *held["links"][:2], mine, other],
            smem=2, vmem=20,
            scratch=[pltpu.VMEM((group, width), F32)],
        )
        held["parent"] = (col, turned, rest[:2])
        yield WAIT
        held["parent totals"] = yield from total_flow(rest[2:])

    def child_flow():
        names = [("gram", 1 + c) for c in range(children)]
        while any(name not in held for name in names + ["parent"]):
            yield WAIT
        pieces = heavy(
            functools.partial(child_kernel, children),
            [shape(children, width // row_count, half)] * row_count,
            [info, held["chooser"], *held["own"], *held["parent"][2], *held["links"][2:4]]
            + [held["links"][5]]
            + [held[name] for name in names],
            smem=1, vmem=20,
        )
        yield WAIT
        held["child totals"] = yield from total_flow(pieces)

    def column_flow():
        names = [("sum", 1 + c) for c in range(children)]
        while any(name not in held for name in names + ["parent"]):
            yield WAIT
        yield WAIT
        yield WAIT
        col, turned, _ = held["parent"]
        held["columns"] = heavy(
            functools.partial(column_kernel, children, rows_here),
            [shape(members, group // 2, width)],
            [info, listed, col, turned] + [value for name in names for value in held[name]],
            smem=2,
        )[0]

    flows = [ring_flow()] + [unit_flow(member) for member in range(children)]
    flows += [link_flow(), prepare_flow(), parent_flow()]
    flows += [unit_flow(children), child_flow(), column_flow()]
    waiting = [(flow, None) for flow in flows]
    while waiting:
        tasks = [wish for _, wish in waiting if wish not in (None, WAIT)]
        results = iter(())
        if tasks:
            outs = [out for _, _, shapes in tasks for out in shapes]
            args = [value for _, values, _ in tasks for value in values]
            sizes = [(body, len(values), len(shapes)) for body, values, shapes in tasks]
            results = iter(
                heavy(functools.partial(step_kernel, sizes), outs, [info, *args], smem=1)
            )
        answered = []
        for flow, wish in waiting:
            answer = None
            if wish not in (None, WAIT):
                answer = [next(results) for _ in wish[2]]
            answered.append((flow, answer))
        waiting = []
        for flow, answer in answered:
            try:
                waiting.append((flow, flow.send(answer)))
            except StopIteration:
                pass

    diags, uppers = heavy(
        functools.partial(finish_kernel, row_count),
        [shape(members, diag_width, width), shape(children, diag_width, width)],
        [info, diag_inverse, held["links"][4]] + held["parent totals"] + held["child totals"],
        smem=1,
    )
    return held["columns"], diags, uppers


def solution(mesh):
    in_specs = (
        P("row", "col"),
        P(None, "row", None),
        P(None, "col", None),
        P(None, "col", None),
        P(),
    )
    out_specs = (P(None, ("row", "col"), None), P(None, "col", None), P(None, "col", None))
    return jax.shard_map(shards, mesh=mesh, in_specs=in_specs, out_specs=out_specs, check_vma=False)
```

```python
import functools

import jax
import jax.numpy as jnp
from jax import lax
from jax.experimental import pallas as pl
from jax.experimental.pallas import tpu as pltpu
from jax.sharding import PartitionSpec as P

AXES = ("row", "col")
F32 = jnp.float32
BF16 = jnp.bfloat16
NN = (((1,), (0,)), ((), ()))
NT = (((1,), (1,)), ((), ()))
MIB = 1024 * 1024
WAIT = ("wait",)


def split(value):
    high = value.astype(BF16)
    return high, (value - high.astype(F32)).astype(BF16)


def one_pass(left, right, dims=NN):
    return lax.dot_general(left, right, dims, preferred_element_type=F32)


def product(left, right):
    return one_pass(left[0], right[0]) + (
        one_pass(left[0], right[1]) + one_pass(left[1], right[0])
    )


def turn(chooser, pair):
    return [one_pass(chooser, half, NT).astype(BF16) for half in pair]


def pair_of(high_ref, low_ref, *index):
    return (high_ref[index], low_ref[index]) if index else (high_ref[...], low_ref[...])


def store_pair(high_ref, low_ref, pair, *index):
    index = index if index else ...
    high_ref[index], low_ref[index] = pair


def shape(*dims, dtype=F32):
    return jax.ShapeDtypeStruct(dims, dtype)


def gray(place):
    return place ^ (place >> 1)


def reversed_bits(count):
    order = [0]
    step = 1
    while step < count:
        order = [value + bit * step for value in order for bit in (0, 1)]
        step *= 2
    return order


def swap(value, axis, size, change):
    return lax.ppermute(value, axis, [(place, place ^ change) for place in range(size)])


def block(index, size):
    return pl.ds(pl.multiple_of(index * size, size), size)


def core_of(info_ref):
    return info_ref[1] & 1


def call(body, outs, args, smem=0, hbm=0, scratch=(), vmem=8, after=None):
    places = [pltpu.SMEM] * smem + [pltpu.HBM] * hbm
    places += [pltpu.VMEM] * (len(args) - len(places))
    count = len(args)
    args = list(args)
    inner = body
    if after is not None:
        args.append(after)
        places.append(pl.ANY)

        def inner(*refs):
            body(*refs[:count], *refs[count + 1 :])

    results = pl.pallas_call(
        inner,
        out_shape=outs,
        in_specs=[pl.BlockSpec(memory_space=place) for place in places],
        out_specs=[pl.BlockSpec(memory_space=pltpu.VMEM)] * len(outs),
        scratch_shapes=scratch,
        compiler_params=pltpu.CompilerParams(vmem_limit_bytes=vmem * MIB),
        cost_estimate=pl.CostEstimate(flops=1024, bytes_accessed=1024, transcendentals=0),
    )(*args)
    return list(results)


def cut_kernel(ratio, cuts, members, info_ref, listed_ref, factors_ref, *refs):
    *outs, sems = refs
    size, unit = outs[0].shape
    width = factors_ref.shape[2]
    column = info_ref[1]
    pair = (column % ratio) // 2
    copies = []
    for at, out_ref in enumerate(outs):
        member, cut, way = members[at // (2 * cuts)], at // 2 % cuts, at % 2
        source = factors_ref.at[
            member, block(2 * pair + way, size), block(core_of(info_ref) * cuts + cut, unit)
        ]
        copies.append(pltpu.make_async_copy(source, out_ref, sems.at[at]))
        copies[-1].start()
    for at, out_ref in enumerate(outs):
        copies[at].wait()
        owner = column - core_of(info_ref) + at % 2
        weight = listed_ref[members[at // (2 * cuts)], owner * size // width]
        out_ref[...] = out_ref[...] * weight.astype(F32)


def chooser_kernel(rows, columns, info_ref, out_ref):
    width = out_ref.shape[0]
    size = width // columns
    part = size // rows
    place = lax.broadcasted_iota(jnp.int32, out_ref.shape, 0)
    inner = place % part
    core = place // part % 2
    level = place // (2 * part) % (columns // 2)
    by_row = place // (2 * part * (columns // 2))
    turned = jnp.zeros_like(level)
    bits = (columns // 2).bit_length() - 1
    for bit in range(bits):
        turned = turned | (((level >> bit) & 1) << (bits - 1 - bit))
    column = (turned * 2 + core) ^ info_ref[1]
    wanted = column * size + (by_row ^ info_ref[0]) * part + inner
    hit = wanted == lax.broadcasted_iota(jnp.int32, out_ref.shape, 1)
    out_ref[...] = hit.astype(F32).astype(BF16)


def region_kernel(order, info_ref, own_ref, other_ref, high_ref, low_ref, held_ref, sems):
    groups = len(order)
    size = own_ref.shape[0] // groups
    width = own_ref.shape[1]
    column = info_ref[1] >> 1
    copies = []
    for g in range(groups):
        for side, source_ref in enumerate((own_ref, other_ref)):
            copies.append(
                pltpu.make_async_copy(
                    source_ref.at[block(order[g] ^ column, size), :],
                    held_ref.at[side, pl.ds(g * size, size), :],
                    sems.at[side, g],
                )
            )
            copies[-1].start()
    for g in range(groups):
        rows = slice(g * size, (g + 1) * size)
        for side in range(2):
            copies[2 * g + side].wait()
            columns = block(core_of(info_ref) ^ side, width)
            high, low = split(held_ref[side, rows, :])
            high_ref[rows, columns] = high
            low_ref[rows, columns] = low


def factor_kernel(
    order, member, info_ref, listed_ref, factors_ref, chooser_ref, high_ref, low_ref, held_ref, sems
):
    groups = len(order)
    _, rows_here, width = factors_ref.shape
    size = rows_here // groups
    column = info_ref[1] >> 1
    copies = []
    for g in range(groups):
        copies.append(
            pltpu.make_async_copy(
                factors_ref.at[member, block(order[g] ^ column, size), :],
                held_ref.at[pl.ds(g * size, size), :],
                sems.at[g],
            )
        )
        copies[-1].start()
    for g in range(groups):
        copies[g].wait()
        rows = slice(g * size, (g + 1) * size)
        first = info_ref[0] * rows_here + (order[g] ^ column) * size
        held_ref[rows, :] = held_ref[rows, :] * listed_ref[member, first // width].astype(F32)
    store_pair(high_ref, low_ref, turn(chooser_ref[...], split(held_ref[...])))


def own_weight(info_ref, listed_ref, member, size, rows_here, width):
    first = info_ref[0] * rows_here + (info_ref[1] >> 1) * size
    return listed_ref[member, first // width].astype(F32)


def own_kernel(
    info_ref, listed_ref, factors_ref, chooser_ref, high_ref, low_ref, thigh_ref, tlow_ref,
    held_ref, sems,
):
    members, rows, width = held_ref.shape
    copies = []
    for j in range(members):
        copies.append(
            pltpu.make_async_copy(
                factors_ref.at[j, block(info_ref[1] >> 1, rows), :], held_ref.at[j], sems.at[j]
            )
        )
        copies[-1].start()
    for j in range(members):
        copies[j].wait()
        weight = own_weight(info_ref, listed_ref, j, rows, factors_ref.shape[1], width)
        pair = split(held_ref[j] * weight)
        store_pair(high_ref, low_ref, pair, j)
        store_pair(thigh_ref, tlow_ref, turn(chooser_ref[...], pair), j)


def link_kernel(
    children, share, info_ref, gathered_ref, diag_ref, other_ref, chooser_ref,
    own_high_ref, own_low_ref, high_ref, low_ref, lift_high_ref, lift_low_ref, framed_ref,
    corner_ref, held_ref, rows_ref, frame_ref,
):
    groups, _, size, width = gathered_ref.shape
    half = corner_ref.shape[2]
    core = core_of(info_ref)
    chooser = chooser_ref[...]
    for g in range(groups):
        for c in range(children):
            held_ref[c, block(info_ref[1] ^ g, size), :] = gathered_ref[g, c]
    rows_ref[block(core, size), :] = diag_ref[0]
    rows_ref[block(1 - core, size), :] = other_ref[0]
    diag = split(rows_ref[...])
    for c in range(children):
        pair = split(held_ref[c])
        store_pair(high_ref, low_ref, pair, c)
        lifted = product(pair_of(own_high_ref, own_low_ref, 0), pair)
        store_pair(lift_high_ref, lift_low_ref, turn(chooser, split(lifted)), c)
        frame_ref[...] = product(diag, pair)
        framed_ref[c] = frame_ref[block(core, size), :]
        slices = split(held_ref[c, block(info_ref[1] >> 1, 2 * size), :])
        corner = product(turn(chooser, slices), split(frame_ref[:, block(core, half)]))
        corner_ref[c] = share * corner


def unit_kernel(count, ratio, cuts, info_ref, high_ref, low_ref, *refs):
    keep_ref, send_ref = refs[-2:]
    middle = keep_ref.shape[0]
    place = info_ref[0] ^ (info_ref[1] // ratio)
    shift = 1
    while shift < count:
        place = place ^ (place >> shift)
        shift *= 2
    places = (place, (count - place) % count)
    parts = []
    for cut in range(cuts):
        chosen = []
        for way in range(2):
            candidates = refs[(2 * cut + way) * count :][:count]
            value = candidates[0][...]
            for at in range(1, count):
                value = jnp.where(places[way] == at, candidates[at][...], value)
            chosen.append(value)
        parts.append(jnp.concatenate(chosen))
    right = split(jnp.concatenate(parts, axis=1))
    send_ref[...] = product((high_ref[middle:], low_ref[middle:]), right)
    keep_ref[...] = product((high_ref[:middle], low_ref[:middle]), right)


def unit_gram_kernel(high_ref, low_ref, keep_ref, send_ref, out_ref):
    middle = keep_ref.shape[0]
    out_ref[...] = product(
        (high_ref[:, :middle], low_ref[:, :middle]), split(keep_ref[...])
    ) + product((high_ref[:, middle:], low_ref[:, middle:]), split(send_ref[...]))


def store_parts(refs, index, value):
    size = refs[0].shape[1]
    for at, ref in enumerate(refs):
        ref[index] = value[at * size : (at + 1) * size]


def parent_kernel(
    children, rows_here, info_ref, listed_ref, chooser_ref, own_high_ref, own_low_ref,
    own_thigh_ref, own_tlow_ref, link_high_ref, link_low_ref, mine_ref, other_ref,
    col_ref, turned_ref, high_ref, low_ref, *refs
):
    *outs, full_ref = refs
    chooser = chooser_ref[...]
    rows, half = mine_ref.shape
    core = core_of(info_ref)
    weight = own_weight(info_ref, listed_ref, 0, rows, rows_here, chooser.shape[0])
    mine = -mine_ref[...] * weight
    full_ref[:, block(core, half)] = mine
    full_ref[:, block(1 - core, half)] = -other_ref[...] * weight
    output_rows = block(core, rows // 2)
    col_ref[...] = full_ref[output_rows, :]
    pair = split(full_ref[...])
    turned_pair = turn(chooser, pair)
    parent = pair_of(own_thigh_ref, own_tlow_ref, 0)
    columns = block(core, half)
    store_parts(outs, 0, -product(parent, split(mine)))
    for c in range(children):
        full_ref[...] = product(pair, pair_of(link_high_ref, link_low_ref, c))
        turned_ref[c] = full_ref[output_rows, :]
        lifted = split(full_ref[:, columns])
        store_pair(high_ref, low_ref, split(full_ref[...]), c)
        own = (own_high_ref[c + 1, :, columns], own_low_ref[c + 1, :, columns])
        store_parts(outs, 1 + c, product(parent, lifted) - product(turned_pair, own))


def child_kernel(
    children, info_ref, chooser_ref, own_high_ref, own_low_ref, own_thigh_ref, own_tlow_ref,
    high_ref, low_ref, lift_high_ref, lift_low_ref, corner_ref, *refs
):
    outs = refs[children:]
    columns = block(core_of(info_ref), corner_ref.shape[2])
    for c in range(children):
        lifted = (high_ref[c, :, columns], low_ref[c, :, columns])
        turned_pair = turn(chooser_ref[...], pair_of(high_ref, low_ref, c))
        own = (own_high_ref[c + 1, :, columns], own_low_ref[c + 1, :, columns])
        total = corner_ref[c] + refs[c][...]
        total += product(pair_of(own_thigh_ref, own_tlow_ref, c + 1), lifted)
        total += product(turned_pair, own)
        total -= product(pair_of(lift_high_ref, lift_low_ref, c), lifted)
        store_parts(outs, c, total)


def column_kernel(children, rows_here, info_ref, listed_ref, col_ref, turned_ref, *refs):
    out_ref = refs[-1]
    rows, width = col_ref.shape
    half = width // 2
    core = core_of(info_ref)
    out_ref[0] = col_ref[...]
    for c in range(children):
        weight = own_weight(info_ref, listed_ref, c + 1, 2 * rows, rows_here, width)
        for side in range(2):
            columns = block(core ^ side, half)
            total = refs[2 * c + side][...] + turned_ref[c, :, columns]
            out_ref[c + 1, :, columns] = -total * weight


def finish_kernel(rows, info_ref, diag_ref, framed_ref, *refs):
    pieces = refs[:rows]
    diags_ref, uppers_ref = refs[rows:]
    part = pieces[0].shape[1]
    children = uppers_ref.shape[0]
    for row in range(rows):
        at = slice(row * part, (row + 1) * part)
        value = pieces[0][...]
        for change in range(1, rows):
            value = jnp.where(info_ref[0] ^ change == row, pieces[change][...], value)
        diags_ref[0, at] = diag_ref[0, at] + value[0]
        uppers_ref[:, at] = value[1 : 1 + children] - framed_ref[:, at]
        diags_ref[1:, at] = diag_ref[1:, at] + value[1 + children :]


def select_step(ratio, info_ref, ins, outs):
    source = info_ref[0] == info_ref[1] // ratio
    for way in range(2):
        outs[way][...] = jnp.where(source, ins[way][...], ins[2 + way][...])


def pass_step(info_ref, ins, outs):
    for way in range(2):
        outs[way][...] = ins[way][...]


def stack_step(info_ref, ins, outs):
    for at in range(ins[0].shape[0]):
        for side in range(2):
            outs[0][2 * at + side] = ins[side][at]


def halve_step(info_ref, ins, outs):
    size = outs[0].shape[-2]
    for at, out in enumerate(outs):
        rows = pl.ds(at * size, size)
        index = (rows,) if len(out.shape) == 2 else (slice(None), rows)
        total = ins[0][index]
        for other in ins[1:]:
            total = total + other[index]
        out[...] = total


def part_step(info_ref, ins, outs):
    size = outs[0].shape[0]
    for side, out in enumerate(outs):
        rows = block(core_of(info_ref) ^ side, size)
        total = ins[0][rows, :]
        for other in ins[1:]:
            total = total + other[rows, :]
        out[...] = total


def join_step(info_ref, ins, outs):
    first = 0
    for at in range(0, len(ins), 2):
        count, _, half = ins[at].shape
        for side in range(2):
            columns = block(core_of(info_ref) ^ side, half)
            outs[0][first : first + count, :, columns] = ins[at + side][...]
        first += count


def step_kernel(tasks, info_ref, *refs):
    start = 0
    end = sum(ins for _, ins, _ in tasks)
    for body, ins, outs in tasks:
        body(info_ref, refs[start : start + ins], refs[end : end + outs])
        start += ins
        end += outs


def shards(region_inverse, factor_cols, parent_factor, diag_inverse, listed):
    row_count = lax.axis_size("row")
    col_count = lax.axis_size("col")
    col_bits = col_count.bit_length() - 1
    rows_here, cols_here = region_inverse.shape
    members, _, width = factor_cols.shape
    children = members - 1
    levels = col_count // 2
    group = rows_here // levels
    ratio = col_count // row_count
    diag_width = width // col_count
    part = diag_width // row_count
    half = width // 2
    cuts = 1
    unit = half // cuts
    chunk_count = members * cuts
    order = reversed_bits(levels)
    stages = chunk_count + row_count - 2

    def ring(forward):
        pairs = []
        for col in range(col_count):
            start = col // ratio
            for place in range(row_count):
                at = (start ^ gray(place)) * col_count + col
                to = (start ^ gray((place + 1) % row_count)) * col_count + col
                pairs.append((at, to) if forward else (to, at))
        return pairs

    rings = (ring(True), ring(False))
    info = jnp.stack([lax.axis_index("row"), lax.axis_index("col")]).astype(jnp.int32)

    def cut(chosen, run):
        count = len(chosen) * cuts * 2
        flat = run(
            functools.partial(cut_kernel, ratio, cuts, chosen),
            [shape(cols_here, unit)] * count,
            [info, listed, factor_cols],
            smem=2, hbm=1, vmem=48,
            scratch=[pltpu.SemaphoreType.DMA((count,))],
        )
        return [flat[at : at + 2] for at in range(0, count, 2)]

    chunks = cut((0,), call)

    last = [chunks[0][0]]
    held = {}
    moved = []
    received = []

    def heavy(body, outs, args, **options):
        results = call(body, outs, args, after=last[0], **options)
        last[0] = results[0]
        return results

    chunks.extend(cut(tuple(range(1, members)), heavy))

    def ring_flow():
        shapes = [shape(cols_here, unit)] * 2
        for stage in range(stages):
            if stage == 0:
                moving = chunks[0]
            elif stage < chunk_count:
                step = functools.partial(select_step, ratio)
                moving = yield (step, chunks[stage] + received[-1], shapes)
            else:
                moving = yield (pass_step, received[-1], shapes)
            moved.append(moving)
            received.append([lax.ppermute(moving[way], AXES, rings[way]) for way in range(2)])

    def link_flow():
        gathered = parent_factor[None]
        for bit in reversed(range(col_bits)):
            arrived = swap(gathered, "col", col_count, 1 << bit)
            dims = (2 * gathered.shape[0],) + parent_factor.shape
            (gathered,) = yield (stack_step, [gathered, arrived], [shape(*dims)])
        held["links"] = heavy(
            functools.partial(link_kernel, children, 1.0 / row_count),
            [shape(children, width, width, dtype=BF16)] * 2
            + [shape(children, width, group, dtype=BF16)] * 2
            + [shape(children, diag_width, width), shape(children, width, half)],
            [info, gathered, diag_inverse, held["other diag"], held["chooser"], *held["own"][:2]],
            smem=1, vmem=20,
            scratch=[
                pltpu.VMEM((children, width, width), F32),
                pltpu.VMEM((2 * diag_width, width), F32),
                pltpu.VMEM((2 * diag_width, width), F32),
            ],
        )

    def prepare_flow():
        other_region = swap(region_inverse, "col", col_count, 1)
        held["other diag"] = swap(diag_inverse[:1], "col", col_count, 1)
        (held["chooser"],) = heavy(
            functools.partial(chooser_kernel, row_count, col_count),
            [shape(width, width, dtype=BF16)],
            [info],
            smem=1,
        )
        held["own"] = heavy(
            own_kernel,
            [shape(members, group, width, dtype=BF16)] * 2
            + [shape(members, width, group, dtype=BF16)] * 2,
            [info, listed, factor_cols, held["chooser"]],
            smem=2, hbm=1,
            scratch=[
                pltpu.VMEM((members, group, width), F32), pltpu.SemaphoreType.DMA((members,))
            ],
        )
        yield WAIT
        held["region"] = heavy(
            functools.partial(region_kernel, order),
            [shape(rows_here, 2 * cols_here, dtype=BF16)] * 2,
            [info, region_inverse, other_region],
            smem=1, hbm=2, vmem=12,
            scratch=[
                pltpu.VMEM((2, rows_here, cols_here), F32),
                pltpu.SemaphoreType.DMA((2, levels)),
            ],
        )
        for member in range(1, members):
            yield WAIT
            held["turned", member] = heavy(
                functools.partial(factor_kernel, order, member),
                [shape(width, rows_here, dtype=BF16)] * 2,
                [info, listed, factor_cols, held["chooser"]],
                smem=2, hbm=1, vmem=20,
                scratch=[
                    pltpu.VMEM((rows_here, width), F32), pltpu.SemaphoreType.DMA((levels,))
                ],
            )

    def unit_flow(member):
        chunk = (member + 1) * cuts - 1
        while len(received) < chunk + row_count - 1:
            yield WAIT
        final = member == members - 1
        if not final:
            yield WAIT
        candidates = []
        for at in range(member * cuts, (member + 1) * cuts):
            for way in range(2):
                candidates.append(moved[at][way])
                candidates += [received[at + hop][way] for hop in range(row_count - 1)]
        size = rows_here // 2
        keep, send = heavy(
            functools.partial(unit_kernel, row_count, ratio, cuts),
            [shape(size, half)] * 2,
            [info, *held["region"], *candidates],
            smem=1, vmem=16,
        )
        first = (keep, send)
        for bit in range(1, col_bits):
            arrived = swap(send, "col", col_count, 1 << bit)
            if bit == 1:
                if final:
                    yield WAIT
                if member:
                    held["gram", member] = heavy(
                        unit_gram_kernel,
                        [shape(width, half)],
                        [*held["turned", member], *first],
                        vmem=16,
                    )[0]
            if bit + 1 < col_bits:
                size //= 2
                keep, send = yield (halve_step, [keep, arrived], [shape(size, half)] * 2)
        if member == 0:
            held["last", 0] = [keep, arrived]
            return
        mine, theirs = yield (part_step, [keep, arrived], [shape(size // 2, half)] * 2)
        held["sum", member] = [mine, swap(theirs, "col", col_count, 1)]

    def total_flow(name, pieces, direct):
        count, size, _ = pieces[0].shape
        inputs = [pieces[0]] + [swap(pieces[d], "row", row_count, d) for d in range(1, row_count)]
        if direct:
            size //= levels
            pieces = yield (halve_step, inputs, [shape(count, size, half)] * levels)
            inputs = [pieces[0]]
            for at in range(1, levels):
                inputs.append(swap(pieces[at], "col", col_count, order[at] << 1))
        else:
            for bit in range(1, col_bits):
                size //= 2
                keep, send = yield (halve_step, inputs, [shape(count, size, half)] * 2)
                inputs = [keep, swap(send, "col", col_count, 1 << bit)]
        size //= 2
        keep, send = yield (halve_step, inputs, [shape(count, size, half)] * 2)
        held[name] = [keep, swap(send, "col", col_count, 1)]

    def gather_flow():
        while "parent totals" not in held or "child totals" not in held:
            yield WAIT
        pairs = held["parent totals"] + held["child totals"]
        (piece,) = yield (join_step, pairs, [shape(members + children, part, width)])
        held["totals"] = [piece] + [swap(piece, "row", row_count, d) for d in range(1, row_count)]

    def parent_flow():
        names = [("last", 0), "links"]
        while any(name not in held for name in names):
            yield WAIT
        (mine,) = heavy(
            functools.partial(step_kernel, [(halve_step, 2, 1)]),
            [shape(group, half)],
            [info, *held["last", 0]],
            smem=1,
        )
        other = swap(mine, "col", col_count, 1)
        col, turned, *rest = heavy(
            functools.partial(parent_kernel, children, rows_here),
            [shape(group // 2, width), shape(children, group // 2, width)]
            + [shape(children, group, width, dtype=BF16)] * 2
            + [shape(members, width // row_count, half)] * row_count,
            [info, listed, held["chooser"], *held["own"], *held["links"][:2], mine, other],
            smem=2, vmem=20,
            scratch=[pltpu.VMEM((group, width), F32)],
        )
        held["parent"] = (col, turned, rest[:2])
        yield WAIT
        yield from total_flow("parent totals", rest[2:], False)

    def child_flow():
        names = [("gram", 1 + c) for c in range(children)]
        while any(name not in held for name in names + ["parent"]):
            yield WAIT
        pieces = heavy(
            functools.partial(child_kernel, children),
            [shape(children, width // row_count, half)] * row_count,
            [info, held["chooser"], *held["own"], *held["parent"][2], *held["links"][2:4]]
            + [held["links"][5]]
            + [held[name] for name in names],
            smem=1, vmem=20,
        )
        yield WAIT
        yield from total_flow("child totals", pieces, True)

    def column_flow():
        names = [("sum", 1 + c) for c in range(children)]
        while any(name not in held for name in names + ["parent"]):
            yield WAIT
        while "totals" not in held:
            yield WAIT
        col, turned, _ = held["parent"]
        held["columns"] = heavy(
            functools.partial(column_kernel, children, rows_here),
            [shape(members, group // 2, width)],
            [info, listed, col, turned] + [value for name in names for value in held[name]],
            smem=2,
        )[0]

    flows = [ring_flow()] + [unit_flow(member) for member in range(children)]
    flows += [link_flow(), prepare_flow(), parent_flow()]
    flows += [unit_flow(children), child_flow(), gather_flow(), column_flow()]
    waiting = [(flow, None) for flow in flows]
    while waiting:
        tasks = [wish for _, wish in waiting if wish not in (None, WAIT)]
        results = iter(())
        if tasks:
            outs = [out for _, _, shapes in tasks for out in shapes]
            args = [value for _, values, _ in tasks for value in values]
            sizes = [(body, len(values), len(shapes)) for body, values, shapes in tasks]
            results = iter(
                heavy(functools.partial(step_kernel, sizes), outs, [info, *args], smem=1)
            )
        answered = []
        for flow, wish in waiting:
            answer = None
            if wish not in (None, WAIT):
                answer = [next(results) for _ in wish[2]]
            answered.append((flow, answer))
        waiting = []
        for flow, answer in answered:
            try:
                waiting.append((flow, flow.send(answer)))
            except StopIteration:
                pass

    diags, uppers = heavy(
        functools.partial(finish_kernel, row_count),
        [shape(members, diag_width, width), shape(children, diag_width, width)],
        [info, diag_inverse, held["links"][4]] + held["totals"],
        smem=1,
    )
    return held["columns"], diags, uppers


def solution(mesh):
    in_specs = (
        P("row", "col"),
        P(None, "row", None),
        P(None, "col", None),
        P(None, "col", None),
        P(),
    )
    out_specs = (P(None, ("row", "col"), None), P(None, "col", None), P(None, "col", None))
    return jax.shard_map(shards, mesh=mesh, in_specs=in_specs, out_specs=out_specs, check_vma=False)
```

```python
import functools

import jax
import jax.numpy as jnp
from jax import lax
from jax.experimental import pallas as pl
from jax.experimental.pallas import tpu as pltpu
from jax.sharding import PartitionSpec as P

AXES = ("row", "col")
F32 = jnp.float32
BF16 = jnp.bfloat16
NN = (((1,), (0,)), ((), ()))
NT = (((1,), (1,)), ((), ()))
MIB = 1024 * 1024
WAIT = ("wait",)


def split(value):
    high = value.astype(BF16)
    return high, (value - high.astype(F32)).astype(BF16)


def one_pass(left, right, dims=NN):
    return lax.dot_general(left, right, dims, preferred_element_type=F32)


def product(left, right):
    return one_pass(left[0], right[0]) + (
        one_pass(left[0], right[1]) + one_pass(left[1], right[0])
    )


def turn(chooser, pair):
    return [one_pass(chooser, half, NT).astype(BF16) for half in pair]


def pair_of(high_ref, low_ref, *index):
    return (high_ref[index], low_ref[index]) if index else (high_ref[...], low_ref[...])


def store_pair(high_ref, low_ref, pair, *index):
    index = index if index else ...
    high_ref[index], low_ref[index] = pair


def shape(*dims, dtype=F32):
    return jax.ShapeDtypeStruct(dims, dtype)


def gray(place):
    return place ^ (place >> 1)


def reversed_bits(count):
    order = [0]
    step = 1
    while step < count:
        order = [value + bit * step for value in order for bit in (0, 1)]
        step *= 2
    return order


def swap(value, axis, size, change):
    return lax.ppermute(value, axis, [(place, place ^ change) for place in range(size)])


def block(index, size):
    return pl.ds(pl.multiple_of(index * size, size), size)


def core_of(info_ref):
    return info_ref[1] & 1


def call(body, outs, args, smem=0, hbm=0, scratch=(), vmem=8, after=None, target=pltpu.VMEM):
    places = [pltpu.SMEM] * smem + [pltpu.HBM] * hbm
    places += [pltpu.VMEM] * (len(args) - len(places))
    count = len(args)
    args = list(args)
    inner = body
    if after is not None:
        args.append(after)
        places.append(pl.ANY)

        def inner(*refs):
            body(*refs[:count], *refs[count + 1 :])

    results = pl.pallas_call(
        inner,
        out_shape=outs,
        in_specs=[pl.BlockSpec(memory_space=place) for place in places],
        out_specs=[pl.BlockSpec(memory_space=target)] * len(outs),
        scratch_shapes=scratch,
        compiler_params=pltpu.CompilerParams(vmem_limit_bytes=vmem * MIB),
        cost_estimate=pl.CostEstimate(flops=1024, bytes_accessed=1024, transcendentals=0),
    )(*args)
    return list(results)


def cut_kernel(ratio, cuts, members, info_ref, listed_ref, factors_ref, *refs):
    *outs, sems = refs
    size, unit = outs[0].shape
    width = factors_ref.shape[2]
    column = info_ref[1]
    pair = (column % ratio) // 2
    copies = []
    for at, out_ref in enumerate(outs):
        member, cut, way = members[at // (2 * cuts)], at // 2 % cuts, at % 2
        source = factors_ref.at[
            member, block(2 * pair + way, size), block(core_of(info_ref) * cuts + cut, unit)
        ]
        copies.append(pltpu.make_async_copy(source, out_ref, sems.at[at]))
        copies[-1].start()
    for at, out_ref in enumerate(outs):
        copies[at].wait()
        owner = column - core_of(info_ref) + at % 2
        weight = listed_ref[members[at // (2 * cuts)], owner * size // width]
        out_ref[...] = out_ref[...] * weight.astype(F32)


def chooser_kernel(rows, columns, info_ref, out_ref):
    width = out_ref.shape[0]
    size = width // columns
    part = size // rows
    place = lax.broadcasted_iota(jnp.int32, out_ref.shape, 0)
    inner = place % part
    core = place // part % 2
    level = place // (2 * part) % (columns // 2)
    by_row = place // (2 * part * (columns // 2))
    turned = jnp.zeros_like(level)
    bits = (columns // 2).bit_length() - 1
    for bit in range(bits):
        turned = turned | (((level >> bit) & 1) << (bits - 1 - bit))
    column = (turned * 2 + core) ^ info_ref[1]
    wanted = column * size + (by_row ^ info_ref[0]) * part + inner
    hit = wanted == lax.broadcasted_iota(jnp.int32, out_ref.shape, 1)
    out_ref[...] = hit.astype(F32).astype(BF16)


def region_kernel(order, info_ref, own_ref, other_ref, high_ref, low_ref, held_ref, sems):
    groups = len(order)
    size = own_ref.shape[0] // groups
    width = own_ref.shape[1]
    column = info_ref[1] >> 1
    copies = []
    for g in range(groups):
        for side, source_ref in enumerate((own_ref, other_ref)):
            copies.append(
                pltpu.make_async_copy(
                    source_ref.at[block(order[g] ^ column, size), :],
                    held_ref.at[side, pl.ds(g * size, size), :],
                    sems.at[side, g],
                )
            )
            copies[-1].start()
    for g in range(groups):
        rows = slice(g * size, (g + 1) * size)
        for side in range(2):
            copies[2 * g + side].wait()
            columns = block(core_of(info_ref) ^ side, width)
            high, low = split(held_ref[side, rows, :])
            high_ref[rows, columns] = high
            low_ref[rows, columns] = low


def factor_kernel(
    order, member, info_ref, listed_ref, factors_ref, chooser_ref, high_ref, low_ref, held_ref, sems
):
    groups = len(order)
    _, rows_here, width = factors_ref.shape
    size = rows_here // groups
    column = info_ref[1] >> 1
    copies = []
    for g in range(groups):
        copies.append(
            pltpu.make_async_copy(
                factors_ref.at[member, block(order[g] ^ column, size), :],
                held_ref.at[pl.ds(g * size, size), :],
                sems.at[g],
            )
        )
        copies[-1].start()
    for g in range(groups):
        copies[g].wait()
        rows = slice(g * size, (g + 1) * size)
        first = info_ref[0] * rows_here + (order[g] ^ column) * size
        held_ref[rows, :] = held_ref[rows, :] * listed_ref[member, first // width].astype(F32)
    store_pair(high_ref, low_ref, turn(chooser_ref[...], split(held_ref[...])))


def own_weight(info_ref, listed_ref, member, size, rows_here, width):
    first = info_ref[0] * rows_here + (info_ref[1] >> 1) * size
    return listed_ref[member, first // width].astype(F32)


def own_kernel(
    info_ref, listed_ref, factors_ref, chooser_ref, high_ref, low_ref, thigh_ref, tlow_ref,
    held_ref, sems,
):
    members, rows, width = held_ref.shape
    copies = []
    for j in range(members):
        copies.append(
            pltpu.make_async_copy(
                factors_ref.at[j, block(info_ref[1] >> 1, rows), :], held_ref.at[j], sems.at[j]
            )
        )
        copies[-1].start()
    for j in range(members):
        copies[j].wait()
        weight = own_weight(info_ref, listed_ref, j, rows, factors_ref.shape[1], width)
        pair = split(held_ref[j] * weight)
        store_pair(high_ref, low_ref, pair, j)
        store_pair(thigh_ref, tlow_ref, turn(chooser_ref[...], pair), j)


def link_kernel(
    children, share, info_ref, gathered_ref, diag_ref, other_ref, chooser_ref,
    own_high_ref, own_low_ref, high_ref, low_ref, lift_high_ref, lift_low_ref, framed_ref,
    corner_ref, held_ref, rows_ref, frame_ref,
):
    groups, _, size, width = gathered_ref.shape
    half = corner_ref.shape[2]
    core = core_of(info_ref)
    chooser = chooser_ref[...]
    for g in range(groups):
        for c in range(children):
            held_ref[c, block(info_ref[1] ^ g, size), :] = gathered_ref[g, c]
    rows_ref[block(core, size), :] = diag_ref[0]
    rows_ref[block(1 - core, size), :] = other_ref[0]
    diag = split(rows_ref[...])
    for c in range(children):
        pair = split(held_ref[c])
        store_pair(high_ref, low_ref, pair, c)
        lifted = product(pair_of(own_high_ref, own_low_ref, 0), pair)
        store_pair(lift_high_ref, lift_low_ref, turn(chooser, split(lifted)), c)
        frame_ref[...] = product(diag, pair)
        framed_ref[c] = frame_ref[block(core, size), :]
        slices = split(held_ref[c, block(info_ref[1] >> 1, 2 * size), :])
        corner = product(turn(chooser, slices), split(frame_ref[:, block(core, half)]))
        corner_ref[c] = share * corner


def unit_kernel(count, ratio, cuts, info_ref, high_ref, low_ref, *refs):
    keep_ref, send_ref = refs[-2:]
    middle = keep_ref.shape[0]
    place = info_ref[0] ^ (info_ref[1] // ratio)
    shift = 1
    while shift < count:
        place = place ^ (place >> shift)
        shift *= 2
    places = (place, (count - place) % count)
    parts = []
    for cut in range(cuts):
        chosen = []
        for way in range(2):
            candidates = refs[(2 * cut + way) * count :][:count]
            value = candidates[0][...]
            for at in range(1, count):
                value = jnp.where(places[way] == at, candidates[at][...], value)
            chosen.append(value)
        parts.append(jnp.concatenate(chosen))
    right = split(jnp.concatenate(parts, axis=1))
    send_ref[...] = product((high_ref[middle:], low_ref[middle:]), right)
    keep_ref[...] = product((high_ref[:middle], low_ref[:middle]), right)


def unit_gram_kernel(high_ref, low_ref, keep_ref, send_ref, out_ref):
    middle = keep_ref.shape[0]
    out_ref[...] = product(
        (high_ref[:, :middle], low_ref[:, :middle]), split(keep_ref[...])
    ) + product((high_ref[:, middle:], low_ref[:, middle:]), split(send_ref[...]))


def store_parts(refs, index, value):
    size = refs[0].shape[1]
    for at, ref in enumerate(refs):
        ref[index] = value[at * size : (at + 1) * size]


def parent_kernel(
    children, rows_here, info_ref, listed_ref, chooser_ref, own_high_ref, own_low_ref,
    own_thigh_ref, own_tlow_ref, link_high_ref, link_low_ref, mine_ref, other_ref,
    col_ref, turned_ref, high_ref, low_ref, *refs
):
    *outs, full_ref = refs
    chooser = chooser_ref[...]
    rows, half = mine_ref.shape
    core = core_of(info_ref)
    weight = own_weight(info_ref, listed_ref, 0, rows, rows_here, chooser.shape[0])
    mine = -mine_ref[...] * weight
    full_ref[:, block(core, half)] = mine
    full_ref[:, block(1 - core, half)] = -other_ref[...] * weight
    output_rows = block(core, rows // 2)
    col_ref[...] = full_ref[output_rows, :]
    pair = split(full_ref[...])
    turned_pair = turn(chooser, pair)
    parent = pair_of(own_thigh_ref, own_tlow_ref, 0)
    columns = block(core, half)
    store_parts(outs, 0, -product(parent, split(mine)))
    for c in range(children):
        full_ref[...] = product(pair, pair_of(link_high_ref, link_low_ref, c))
        turned_ref[c] = full_ref[output_rows, :]
        lifted = split(full_ref[:, columns])
        store_pair(high_ref, low_ref, split(full_ref[...]), c)
        own = (own_high_ref[c + 1, :, columns], own_low_ref[c + 1, :, columns])
        store_parts(outs, 1 + c, product(parent, lifted) - product(turned_pair, own))


def child_kernel(
    children, info_ref, chooser_ref, own_high_ref, own_low_ref, own_thigh_ref, own_tlow_ref,
    high_ref, low_ref, lift_high_ref, lift_low_ref, corner_ref, *refs
):
    outs = refs[children:]
    columns = block(core_of(info_ref), corner_ref.shape[2])
    for c in range(children):
        lifted = (high_ref[c, :, columns], low_ref[c, :, columns])
        turned_pair = turn(chooser_ref[...], pair_of(high_ref, low_ref, c))
        own = (own_high_ref[c + 1, :, columns], own_low_ref[c + 1, :, columns])
        total = corner_ref[c] + refs[c][...]
        total += product(pair_of(own_thigh_ref, own_tlow_ref, c + 1), lifted)
        total += product(turned_pair, own)
        total -= product(pair_of(lift_high_ref, lift_low_ref, c), lifted)
        store_parts(outs, c, total)


def column_kernel(children, rows_here, info_ref, listed_ref, col_ref, turned_ref, *refs):
    *refs, out_ref, held_ref, sem = refs
    rows, width = col_ref.shape
    half = width // 2
    core = core_of(info_ref)
    held_ref[0] = col_ref[...]
    for c in range(children):
        weight = own_weight(info_ref, listed_ref, c + 1, 2 * rows, rows_here, width)
        for side in range(2):
            columns = block(core ^ side, half)
            total = refs[2 * c + side][...] + turned_ref[c, :, columns]
            held_ref[c + 1, :, columns] = -total * weight
    copy = pltpu.make_async_copy(held_ref, out_ref, sem)
    copy.start()
    copy.wait()


def finish_kernel(rows, info_ref, diag_ref, framed_ref, *refs):
    pieces = refs[:rows]
    diags_ref, uppers_ref = refs[rows:]
    part = pieces[0].shape[1]
    children = uppers_ref.shape[0]
    for row in range(rows):
        at = slice(row * part, (row + 1) * part)
        value = pieces[0][...]
        for change in range(1, rows):
            value = jnp.where(info_ref[0] ^ change == row, pieces[change][...], value)
        diags_ref[0, at] = diag_ref[0, at] + value[0]
        uppers_ref[:, at] = value[1 : 1 + children] - framed_ref[:, at]
        diags_ref[1:, at] = diag_ref[1:, at] + value[1 + children :]


def select_step(ratio, info_ref, ins, outs):
    source = info_ref[0] == info_ref[1] // ratio
    for way in range(2):
        outs[way][...] = jnp.where(source, ins[way][...], ins[2 + way][...])


def pass_step(info_ref, ins, outs):
    for way in range(2):
        outs[way][...] = ins[way][...]


def stack_step(info_ref, ins, outs):
    for at in range(ins[0].shape[0]):
        for side in range(2):
            outs[0][2 * at + side] = ins[side][at]


def halve_step(info_ref, ins, outs):
    size = outs[0].shape[-2]
    for at, out in enumerate(outs):
        rows = pl.ds(at * size, size)
        index = (rows,) if len(out.shape) == 2 else (slice(None), rows)
        total = ins[0][index]
        for other in ins[1:]:
            total = total + other[index]
        out[...] = total


def part_step(info_ref, ins, outs):
    size = outs[0].shape[0]
    for side, out in enumerate(outs):
        rows = block(core_of(info_ref) ^ side, size)
        total = ins[0][rows, :]
        for other in ins[1:]:
            total = total + other[rows, :]
        out[...] = total


def join_step(info_ref, ins, outs):
    first = 0
    for at in range(0, len(ins), 2):
        count, _, half = ins[at].shape
        for side in range(2):
            columns = block(core_of(info_ref) ^ side, half)
            outs[0][first : first + count, :, columns] = ins[at + side][...]
        first += count


def step_kernel(tasks, info_ref, *refs):
    start = 0
    end = sum(ins for _, ins, _ in tasks)
    for body, ins, outs in tasks:
        body(info_ref, refs[start : start + ins], refs[end : end + outs])
        start += ins
        end += outs


def shards(region_inverse, factor_cols, parent_factor, diag_inverse, listed):
    row_count = lax.axis_size("row")
    col_count = lax.axis_size("col")
    col_bits = col_count.bit_length() - 1
    rows_here, cols_here = region_inverse.shape
    members, _, width = factor_cols.shape
    children = members - 1
    levels = col_count // 2
    group = rows_here // levels
    ratio = col_count // row_count
    diag_width = width // col_count
    part = diag_width // row_count
    half = width // 2
    cuts = 2
    unit = half // cuts
    chunk_count = members * cuts
    order = reversed_bits(levels)
    stages = chunk_count + row_count - 2

    def ring(forward):
        pairs = []
        for col in range(col_count):
            start = col // ratio
            for place in range(row_count):
                at = (start ^ gray(place)) * col_count + col
                to = (start ^ gray((place + 1) % row_count)) * col_count + col
                pairs.append((at, to) if forward else (to, at))
        return pairs

    rings = (ring(True), ring(False))
    info = jnp.stack([lax.axis_index("row"), lax.axis_index("col")]).astype(jnp.int32)

    def cut(chosen, run):
        count = len(chosen) * cuts * 2
        flat = run(
            functools.partial(cut_kernel, ratio, cuts, chosen),
            [shape(cols_here, unit)] * count,
            [info, listed, factor_cols],
            smem=2, hbm=1, vmem=48,
            scratch=[pltpu.SemaphoreType.DMA((count,))],
        )
        return [flat[at : at + 2] for at in range(0, count, 2)]

    chunks = cut((0,), call)

    last = [chunks[0][0]]
    held = {}
    moved = []
    received = []

    def heavy(body, outs, args, **options):
        results = call(body, outs, args, after=last[0], **options)
        last[0] = results[0]
        return results

    chunks.extend(cut(tuple(range(1, members)), heavy))

    def ring_flow():
        shapes = [shape(cols_here, unit)] * 2
        for stage in range(stages):
            if stage == 0:
                moving = chunks[0]
            elif stage < chunk_count:
                step = functools.partial(select_step, ratio)
                moving = yield (step, chunks[stage] + received[-1], shapes)
            else:
                moving = yield (pass_step, received[-1], shapes)
            moved.append(moving)
            received.append([lax.ppermute(moving[way], AXES, rings[way]) for way in range(2)])

    def link_flow():
        gathered = parent_factor[None]
        for bit in reversed(range(col_bits)):
            arrived = swap(gathered, "col", col_count, 1 << bit)
            if 0 < bit < col_bits - 1:
                yield WAIT
            dims = (2 * gathered.shape[0],) + parent_factor.shape
            (gathered,) = yield (stack_step, [gathered, arrived], [shape(*dims)])
        held["links"] = heavy(
            functools.partial(link_kernel, children, 1.0 / row_count),
            [shape(children, width, width, dtype=BF16)] * 2
            + [shape(children, width, group, dtype=BF16)] * 2
            + [shape(children, diag_width, width), shape(children, width, half)],
            [info, gathered, diag_inverse, held["other diag"], held["chooser"], *held["own"][:2]],
            smem=1, vmem=20,
            scratch=[
                pltpu.VMEM((children, width, width), F32),
                pltpu.VMEM((2 * diag_width, width), F32),
                pltpu.VMEM((2 * diag_width, width), F32),
            ],
        )

    def prepare_flow():
        other_region = swap(region_inverse, "col", col_count, 1)
        held["other diag"] = swap(diag_inverse[:1], "col", col_count, 1)
        (held["chooser"],) = heavy(
            functools.partial(chooser_kernel, row_count, col_count),
            [shape(width, width, dtype=BF16)],
            [info],
            smem=1,
        )
        held["own"] = heavy(
            own_kernel,
            [shape(members, group, width, dtype=BF16)] * 2
            + [shape(members, width, group, dtype=BF16)] * 2,
            [info, listed, factor_cols, held["chooser"]],
            smem=2, hbm=1,
            scratch=[
                pltpu.VMEM((members, group, width), F32), pltpu.SemaphoreType.DMA((members,))
            ],
        )
        yield WAIT
        held["region"] = heavy(
            functools.partial(region_kernel, order),
            [shape(rows_here, 2 * cols_here, dtype=BF16)] * 2,
            [info, region_inverse, other_region],
            smem=1, hbm=2, vmem=12,
            scratch=[
                pltpu.VMEM((2, rows_here, cols_here), F32),
                pltpu.SemaphoreType.DMA((2, levels)),
            ],
        )
        for member in range(1, members):
            yield WAIT
            held["turned", member] = heavy(
                functools.partial(factor_kernel, order, member),
                [shape(width, rows_here, dtype=BF16)] * 2,
                [info, listed, factor_cols, held["chooser"]],
                smem=2, hbm=1, vmem=20,
                scratch=[
                    pltpu.VMEM((rows_here, width), F32), pltpu.SemaphoreType.DMA((levels,))
                ],
            )

    def unit_flow(member):
        chunk = (member + 1) * cuts - 1
        while len(received) < chunk + row_count - 1:
            yield WAIT
        final = member == members - 1
        if not final:
            yield WAIT
        candidates = []
        for at in range(member * cuts, (member + 1) * cuts):
            for way in range(2):
                candidates.append(moved[at][way])
                candidates += [received[at + hop][way] for hop in range(row_count - 1)]
        size = rows_here // 2
        keep, send = heavy(
            functools.partial(unit_kernel, row_count, ratio, cuts),
            [shape(size, half)] * 2,
            [info, *held["region"], *candidates],
            smem=1, vmem=16,
        )
        first = (keep, send)
        for bit in range(1, col_bits):
            arrived = swap(send, "col", col_count, 1 << bit)
            if bit == 1:
                if final:
                    yield WAIT
                if member:
                    held["gram", member] = heavy(
                        unit_gram_kernel,
                        [shape(width, half)],
                        [*held["turned", member], *first],
                        vmem=16,
                    )[0]
                if not final:
                    yield WAIT
            if bit + 1 < col_bits:
                size //= 2
                keep, send = yield (halve_step, [keep, arrived], [shape(size, half)] * 2)
        if member == 0:
            held["last", 0] = [keep, arrived]
            return
        mine, theirs = yield (part_step, [keep, arrived], [shape(size // 2, half)] * 2)
        held["sum", member] = [mine, swap(theirs, "col", col_count, 1)]

    def total_flow(name, pieces, direct):
        count, size, _ = pieces[0].shape
        inputs = [pieces[0]] + [swap(pieces[d], "row", row_count, d) for d in range(1, row_count)]
        if direct:
            size //= levels
            pieces = yield (halve_step, inputs, [shape(count, size, half)] * levels)
            inputs = [pieces[0]]
            for at in range(1, levels):
                inputs.append(swap(pieces[at], "col", col_count, order[at] << 1))
        else:
            for bit in range(1, col_bits):
                size //= 2
                keep, send = yield (halve_step, inputs, [shape(count, size, half)] * 2)
                inputs = [keep, swap(send, "col", col_count, 1 << bit)]
        size //= 2
        keep, send = yield (halve_step, inputs, [shape(count, size, half)] * 2)
        held[name] = [keep, swap(send, "col", col_count, 1)]

    def gather_flow():
        while "parent totals" not in held or "child totals" not in held:
            yield WAIT
        pairs = held["parent totals"] + held["child totals"]
        (piece,) = yield (join_step, pairs, [shape(members + children, part, width)])
        held["totals"] = [piece] + [swap(piece, "row", row_count, d) for d in range(1, row_count)]

    def parent_flow():
        names = [("last", 0), "links"]
        while any(name not in held for name in names):
            yield WAIT
        (mine,) = yield (halve_step, held["last", 0], [shape(group, half)])
        other = swap(mine, "col", col_count, 1)
        col, turned, *rest = heavy(
            functools.partial(parent_kernel, children, rows_here),
            [shape(group // 2, width), shape(children, group // 2, width)]
            + [shape(children, group, width, dtype=BF16)] * 2
            + [shape(members, width // row_count, half)] * row_count,
            [info, listed, held["chooser"], *held["own"], *held["links"][:2], mine, other],
            smem=2, vmem=20,
            scratch=[pltpu.VMEM((group, width), F32)],
        )
        held["parent"] = (col, turned, rest[:2])
        yield WAIT
        yield from total_flow("parent totals", rest[2:], False)

    def child_flow():
        names = [("gram", 1 + c) for c in range(children)]
        while any(name not in held for name in names + ["parent"]):
            yield WAIT
        pieces = heavy(
            functools.partial(child_kernel, children),
            [shape(children, width // row_count, half)] * row_count,
            [info, held["chooser"], *held["own"], *held["parent"][2], *held["links"][2:4]]
            + [held["links"][5]]
            + [held[name] for name in names],
            smem=1, vmem=20,
        )
        yield WAIT
        yield from total_flow("child totals", pieces, True)

    def column_flow():
        names = [("sum", 1 + c) for c in range(children)]
        while any(name not in held for name in names + ["parent"]):
            yield WAIT
        while "totals" not in held:
            yield WAIT
        col, turned, _ = held["parent"]
        held["columns"] = heavy(
            functools.partial(column_kernel, children, rows_here),
            [shape(members, group // 2, width)],
            [info, listed, col, turned] + [value for name in names for value in held[name]],
            smem=2, target=pltpu.HBM,
            scratch=[
                pltpu.VMEM((members, group // 2, width), F32), pltpu.SemaphoreType.DMA(())
            ],
        )[0]

    flows = [ring_flow()] + [unit_flow(member) for member in range(children)]
    flows += [link_flow(), prepare_flow(), parent_flow()]
    flows += [unit_flow(children), child_flow(), gather_flow(), column_flow()]
    waiting = [(flow, None) for flow in flows]
    while waiting:
        tasks = [wish for _, wish in waiting if wish not in (None, WAIT)]
        results = iter(())
        if tasks:
            outs = [out for _, _, shapes in tasks for out in shapes]
            args = [value for _, values, _ in tasks for value in values]
            sizes = [(body, len(values), len(shapes)) for body, values, shapes in tasks]
            results = iter(
                heavy(functools.partial(step_kernel, sizes), outs, [info, *args], smem=1)
            )
        answered = []
        for flow, wish in waiting:
            answer = None
            if wish not in (None, WAIT):
                answer = [next(results) for _ in wish[2]]
            answered.append((flow, answer))
        waiting = []
        for flow, answer in answered:
            try:
                waiting.append((flow, flow.send(answer)))
            except StopIteration:
                pass

    diags, uppers = heavy(
        functools.partial(finish_kernel, row_count),
        [shape(members, diag_width, width), shape(children, diag_width, width)],
        [info, diag_inverse, held["links"][4]] + held["totals"],
        smem=1,
    )
    return held["columns"], diags, uppers


def solution(mesh):
    in_specs = (
        P("row", "col"),
        P(None, "row", None),
        P(None, "col", None),
        P(None, "col", None),
        P(),
    )
    out_specs = (P(None, ("row", "col"), None), P(None, "col", None), P(None, "col", None))
    return jax.shard_map(shards, mesh=mesh, in_specs=in_specs, out_specs=out_specs, check_vma=False)
```

```python
import functools

import jax
import jax.numpy as jnp
from jax import lax
from jax.experimental import pallas as pl
from jax.experimental.pallas import tpu as pltpu
from jax.sharding import PartitionSpec as P

AXES = ("row", "col")
F32 = jnp.float32
BF16 = jnp.bfloat16
NN = (((1,), (0,)), ((), ()))
NT = (((1,), (1,)), ((), ()))
MIB = 1024 * 1024
WAIT = ("wait",)


def split(value):
    high = value.astype(BF16)
    return high, (value - high.astype(F32)).astype(BF16)


def one_pass(left, right, dims=NN):
    return lax.dot_general(left, right, dims, preferred_element_type=F32)


def product(left, right):
    return one_pass(left[0], right[0]) + (
        one_pass(left[0], right[1]) + one_pass(left[1], right[0])
    )


def turn(chooser, pair):
    return [one_pass(chooser, half, NT).astype(BF16) for half in pair]


def pair_of(high_ref, low_ref, *index):
    return (high_ref[index], low_ref[index]) if index else (high_ref[...], low_ref[...])


def store_pair(high_ref, low_ref, pair, *index):
    index = index if index else ...
    high_ref[index], low_ref[index] = pair


def shape(*dims, dtype=F32):
    return jax.ShapeDtypeStruct(dims, dtype)


def gray(place):
    return place ^ (place >> 1)


def reversed_bits(count):
    order = [0]
    step = 1
    while step < count:
        order = [value + bit * step for value in order for bit in (0, 1)]
        step *= 2
    return order


def swap(value, axis, size, change):
    return lax.ppermute(value, axis, [(place, place ^ change) for place in range(size)])


def block(index, size):
    return pl.ds(pl.multiple_of(index * size, size), size)


def core_of(info_ref):
    return info_ref[1] & 1


def call(body, outs, args, smem=0, hbm=0, scratch=(), vmem=8, after=None, target=pltpu.VMEM):
    places = [pltpu.SMEM] * smem + [pltpu.HBM] * hbm
    places += [pltpu.VMEM] * (len(args) - len(places))
    count = len(args)
    args = list(args)
    inner = body
    if after is not None:
        args.append(after)
        places.append(pl.ANY)

        def inner(*refs):
            body(*refs[:count], *refs[count + 1 :])

    results = pl.pallas_call(
        inner,
        out_shape=outs,
        in_specs=[pl.BlockSpec(memory_space=place) for place in places],
        out_specs=[pl.BlockSpec(memory_space=target)] * len(outs),
        scratch_shapes=scratch,
        compiler_params=pltpu.CompilerParams(vmem_limit_bytes=vmem * MIB),
        cost_estimate=pl.CostEstimate(flops=1024, bytes_accessed=1024, transcendentals=0),
    )(*args)
    return list(results)


def cut_kernel(ratio, cuts, members, info_ref, listed_ref, factors_ref, *refs):
    *outs, sems = refs
    size, unit = outs[0].shape
    width = factors_ref.shape[2]
    column = info_ref[1]
    pair = (column % ratio) // 2
    copies = []
    for at, out_ref in enumerate(outs):
        member, cut, way = members[at // (2 * cuts)], at // 2 % cuts, at % 2
        source = factors_ref.at[
            member, block(2 * pair + way, size), block(core_of(info_ref) * cuts + cut, unit)
        ]
        copies.append(pltpu.make_async_copy(source, out_ref, sems.at[at]))
        copies[-1].start()
    for at, out_ref in enumerate(outs):
        copies[at].wait()
        owner = column - core_of(info_ref) + at % 2
        weight = listed_ref[members[at // (2 * cuts)], owner * size // width]
        out_ref[...] = out_ref[...] * weight.astype(F32)


def chooser_kernel(rows, columns, info_ref, out_ref):
    width = out_ref.shape[0]
    size = width // columns
    part = size // rows
    place = lax.broadcasted_iota(jnp.int32, out_ref.shape, 0)
    inner = place % part
    core = place // part % 2
    level = place // (2 * part) % (columns // 2)
    by_row = place // (2 * part * (columns // 2))
    turned = jnp.zeros_like(level)
    bits = (columns // 2).bit_length() - 1
    for bit in range(bits):
        turned = turned | (((level >> bit) & 1) << (bits - 1 - bit))
    column = (turned * 2 + core) ^ info_ref[1]
    wanted = column * size + (by_row ^ info_ref[0]) * part + inner
    hit = wanted == lax.broadcasted_iota(jnp.int32, out_ref.shape, 1)
    out_ref[...] = hit.astype(F32).astype(BF16)


def region_kernel(order, info_ref, own_ref, other_ref, high_ref, low_ref, held_ref, sems):
    groups = len(order)
    size = own_ref.shape[0] // groups
    width = own_ref.shape[1]
    column = info_ref[1] >> 1
    copies = []
    for g in range(groups):
        for side, source_ref in enumerate((own_ref, other_ref)):
            copies.append(
                pltpu.make_async_copy(
                    source_ref.at[block(order[g] ^ column, size), :],
                    held_ref.at[side, pl.ds(g * size, size), :],
                    sems.at[side, g],
                )
            )
            copies[-1].start()
    for g in range(groups):
        rows = slice(g * size, (g + 1) * size)
        for side in range(2):
            copies[2 * g + side].wait()
            columns = block(core_of(info_ref) ^ side, width)
            high, low = split(held_ref[side, rows, :])
            high_ref[rows, columns] = high
            low_ref[rows, columns] = low


def factor_kernel(
    order, member, info_ref, listed_ref, factors_ref, chooser_ref, high_ref, low_ref, held_ref, sems
):
    groups = len(order)
    _, rows_here, width = factors_ref.shape
    size = rows_here // groups
    column = info_ref[1] >> 1
    copies = []
    for g in range(groups):
        copies.append(
            pltpu.make_async_copy(
                factors_ref.at[member, block(order[g] ^ column, size), :],
                held_ref.at[pl.ds(g * size, size), :],
                sems.at[g],
            )
        )
        copies[-1].start()
    for g in range(groups):
        copies[g].wait()
        rows = slice(g * size, (g + 1) * size)
        first = info_ref[0] * rows_here + (order[g] ^ column) * size
        held_ref[rows, :] = held_ref[rows, :] * listed_ref[member, first // width].astype(F32)
    store_pair(high_ref, low_ref, turn(chooser_ref[...], split(held_ref[...])))


def own_weight(info_ref, listed_ref, member, size, rows_here, width):
    first = info_ref[0] * rows_here + (info_ref[1] >> 1) * size
    return listed_ref[member, first // width].astype(F32)


def own_kernel(
    info_ref, listed_ref, factors_ref, chooser_ref, high_ref, low_ref, thigh_ref, tlow_ref,
    held_ref, sems,
):
    members, rows, width = held_ref.shape
    copies = []
    for j in range(members):
        copies.append(
            pltpu.make_async_copy(
                factors_ref.at[j, block(info_ref[1] >> 1, rows), :], held_ref.at[j], sems.at[j]
            )
        )
        copies[-1].start()
    for j in range(members):
        copies[j].wait()
        weight = own_weight(info_ref, listed_ref, j, rows, factors_ref.shape[1], width)
        pair = split(held_ref[j] * weight)
        store_pair(high_ref, low_ref, pair, j)
        store_pair(thigh_ref, tlow_ref, turn(chooser_ref[...], pair), j)


def link_kernel(
    children, share, order, info_ref, gathered_ref, diag_ref, other_ref, chooser_ref,
    own_high_ref, own_low_ref, high_ref, low_ref, lift_high_ref, lift_low_ref, framed_ref,
    corner_ref, held_ref, rows_ref, frame_ref,
):
    groups, _, size, width = gathered_ref.shape
    half = corner_ref.shape[2]
    core = core_of(info_ref)
    chooser = chooser_ref[...]
    for g in range(groups):
        for c in range(children):
            held_ref[c, block(info_ref[1] ^ order[g], size), :] = gathered_ref[g, c]
    rows_ref[block(core, size), :] = diag_ref[0]
    rows_ref[block(1 - core, size), :] = other_ref[0]
    diag = split(rows_ref[...])
    for c in range(children):
        pair = split(held_ref[c])
        store_pair(high_ref, low_ref, pair, c)
        lifted = product(pair_of(own_high_ref, own_low_ref, 0), pair)
        store_pair(lift_high_ref, lift_low_ref, turn(chooser, split(lifted)), c)
        frame_ref[...] = product(diag, pair)
        framed_ref[c] = frame_ref[block(core, size), :]
        slices = split(held_ref[c, block(info_ref[1] >> 1, 2 * size), :])
        corner = product(turn(chooser, slices), split(frame_ref[:, block(core, half)]))
        corner_ref[c] = share * corner


def unit_kernel(count, ratio, cuts, info_ref, high_ref, low_ref, *refs):
    keep_ref, send_ref = refs[-2:]
    middle = keep_ref.shape[0]
    place = info_ref[0] ^ (info_ref[1] // ratio)
    shift = 1
    while shift < count:
        place = place ^ (place >> shift)
        shift *= 2
    places = (place, (count - place) % count)
    parts = []
    for cut in range(cuts):
        chosen = []
        for way in range(2):
            candidates = refs[(2 * cut + way) * count :][:count]
            value = candidates[0][...]
            for at in range(1, count):
                value = jnp.where(places[way] == at, candidates[at][...], value)
            chosen.append(value)
        parts.append(jnp.concatenate(chosen))
    right = split(jnp.concatenate(parts, axis=1))
    send_ref[...] = product((high_ref[middle:], low_ref[middle:]), right)
    keep_ref[...] = product((high_ref[:middle], low_ref[:middle]), right)


def unit_gram_kernel(high_ref, low_ref, keep_ref, send_ref, out_ref):
    middle = keep_ref.shape[0]
    out_ref[...] = product(
        (high_ref[:, :middle], low_ref[:, :middle]), split(keep_ref[...])
    ) + product((high_ref[:, middle:], low_ref[:, middle:]), split(send_ref[...]))


def store_parts(refs, index, value):
    size = refs[0].shape[1]
    for at, ref in enumerate(refs):
        ref[index] = value[at * size : (at + 1) * size]


def parent_kernel(
    children, rows_here, info_ref, listed_ref, chooser_ref, own_high_ref, own_low_ref,
    own_thigh_ref, own_tlow_ref, link_high_ref, link_low_ref, mine_ref, other_ref,
    col_ref, turned_ref, high_ref, low_ref, *refs
):
    *outs, full_ref = refs
    chooser = chooser_ref[...]
    rows, half = mine_ref.shape
    core = core_of(info_ref)
    weight = own_weight(info_ref, listed_ref, 0, rows, rows_here, chooser.shape[0])
    mine = -mine_ref[...] * weight
    full_ref[:, block(core, half)] = mine
    full_ref[:, block(1 - core, half)] = -other_ref[...] * weight
    output_rows = block(core, rows // 2)
    col_ref[...] = full_ref[output_rows, :]
    pair = split(full_ref[...])
    turned_pair = turn(chooser, pair)
    parent = pair_of(own_thigh_ref, own_tlow_ref, 0)
    columns = block(core, half)
    store_parts(outs, 0, -product(parent, split(mine)))
    for c in range(children):
        full_ref[...] = product(pair, pair_of(link_high_ref, link_low_ref, c))
        turned_ref[c] = full_ref[output_rows, :]
        lifted = split(full_ref[:, columns])
        store_pair(high_ref, low_ref, split(full_ref[...]), c)
        own = (own_high_ref[c + 1, :, columns], own_low_ref[c + 1, :, columns])
        store_parts(outs, 1 + c, product(parent, lifted) - product(turned_pair, own))


def child_kernel(
    children, info_ref, chooser_ref, own_high_ref, own_low_ref, own_thigh_ref, own_tlow_ref,
    high_ref, low_ref, lift_high_ref, lift_low_ref, corner_ref, *refs
):
    outs = refs[children:]
    columns = block(core_of(info_ref), corner_ref.shape[2])
    for c in range(children):
        lifted = (high_ref[c, :, columns], low_ref[c, :, columns])
        turned_pair = turn(chooser_ref[...], pair_of(high_ref, low_ref, c))
        own = (own_high_ref[c + 1, :, columns], own_low_ref[c + 1, :, columns])
        total = corner_ref[c] + refs[c][...]
        total += product(pair_of(own_thigh_ref, own_tlow_ref, c + 1), lifted)
        total += product(turned_pair, own)
        total -= product(pair_of(lift_high_ref, lift_low_ref, c), lifted)
        store_parts(outs, c, total)


def column_kernel(children, rows_here, info_ref, listed_ref, col_ref, turned_ref, *refs):
    *refs, out_ref, held_ref, sem = refs
    rows, width = col_ref.shape
    half = width // 2
    core = core_of(info_ref)
    held_ref[0] = col_ref[...]
    for c in range(children):
        weight = own_weight(info_ref, listed_ref, c + 1, 2 * rows, rows_here, width)
        for side in range(2):
            columns = block(core ^ side, half)
            total = refs[2 * c + side][...] + turned_ref[c, :, columns]
            held_ref[c + 1, :, columns] = -total * weight
    copy = pltpu.make_async_copy(held_ref, out_ref, sem)
    copy.start()
    copy.wait()


def finish_kernel(rows, info_ref, diag_ref, framed_ref, *refs):
    pieces = refs[:rows]
    diags_ref, uppers_ref = refs[rows:]
    part = pieces[0].shape[1]
    children = uppers_ref.shape[0]
    for row in range(rows):
        at = slice(row * part, (row + 1) * part)
        value = pieces[0][...]
        for change in range(1, rows):
            value = jnp.where(info_ref[0] ^ change == row, pieces[change][...], value)
        diags_ref[0, at] = diag_ref[0, at] + value[0]
        uppers_ref[:, at] = value[1 : 1 + children] - framed_ref[:, at]
        diags_ref[1:, at] = diag_ref[1:, at] + value[1 + children :]


def select_step(ratio, info_ref, ins, outs):
    source = info_ref[0] == info_ref[1] // ratio
    for way in range(2):
        outs[way][...] = jnp.where(source, ins[way][...], ins[2 + way][...])


def pass_step(info_ref, ins, outs):
    for way in range(2):
        outs[way][...] = ins[way][...]


def stack_step(info_ref, ins, outs):
    for at in range(ins[0].shape[0]):
        for side in range(2):
            outs[0][2 * at + side] = ins[side][at]


def halve_step(info_ref, ins, outs):
    size = outs[0].shape[-2]
    for at, out in enumerate(outs):
        rows = pl.ds(at * size, size)
        index = (rows,) if len(out.shape) == 2 else (slice(None), rows)
        total = ins[0][index]
        for other in ins[1:]:
            total = total + other[index]
        out[...] = total


def part_step(info_ref, ins, outs):
    size = outs[0].shape[0]
    for side, out in enumerate(outs):
        rows = block(core_of(info_ref) ^ side, size)
        total = ins[0][rows, :]
        for other in ins[1:]:
            total = total + other[rows, :]
        out[...] = total


def join_step(info_ref, ins, outs):
    first = 0
    for at in range(0, len(ins), 2):
        count, _, half = ins[at].shape
        for side in range(2):
            columns = block(core_of(info_ref) ^ side, half)
            outs[0][first : first + count, :, columns] = ins[at + side][...]
        first += count


def step_kernel(tasks, info_ref, *refs):
    start = 0
    end = sum(ins for _, ins, _ in tasks)
    for body, ins, outs in tasks:
        body(info_ref, refs[start : start + ins], refs[end : end + outs])
        start += ins
        end += outs


def shards(region_inverse, factor_cols, parent_factor, diag_inverse, listed):
    row_count = lax.axis_size("row")
    col_count = lax.axis_size("col")
    col_bits = col_count.bit_length() - 1
    rows_here, cols_here = region_inverse.shape
    members, _, width = factor_cols.shape
    children = members - 1
    levels = col_count // 2
    group = rows_here // levels
    ratio = col_count // row_count
    diag_width = width // col_count
    part = diag_width // row_count
    half = width // 2
    cuts = 2
    unit = half // cuts
    chunk_count = members * cuts
    order = reversed_bits(levels)
    stages = chunk_count + row_count - 2

    def ring(forward):
        pairs = []
        for col in range(col_count):
            start = col // ratio
            for place in range(row_count):
                at = (start ^ gray(place)) * col_count + col
                to = (start ^ gray((place + 1) % row_count)) * col_count + col
                pairs.append((at, to) if forward else (to, at))
        return pairs

    rings = (ring(True), ring(False))
    link_bits = [*range(1, col_bits), 0]
    link_order = [0]
    for bit in link_bits:
        link_order = [value ^ (side << bit) for value in link_order for side in range(2)]
    info = jnp.stack([lax.axis_index("row"), lax.axis_index("col")]).astype(jnp.int32)

    def cut(chosen, run):
        count = len(chosen) * cuts * 2
        flat = run(
            functools.partial(cut_kernel, ratio, cuts, chosen),
            [shape(cols_here, unit)] * count,
            [info, listed, factor_cols],
            smem=2, hbm=1, vmem=48,
            scratch=[pltpu.SemaphoreType.DMA((count,))],
        )
        return [flat[at : at + 2] for at in range(0, count, 2)]

    chunks = cut((0,), call)

    last = [chunks[0][0]]
    held = {}
    moved = []
    received = []

    def heavy(body, outs, args, **options):
        results = call(body, outs, args, after=last[0], **options)
        last[0] = results[0]
        return results

    chunks.extend(cut(tuple(range(1, members)), heavy))

    def ring_flow():
        shapes = [shape(cols_here, unit)] * 2
        for stage in range(stages):
            if stage == 0:
                moving = chunks[0]
            elif stage < chunk_count:
                step = functools.partial(select_step, ratio)
                moving = yield (step, chunks[stage] + received[-1], shapes)
            else:
                moving = yield (pass_step, received[-1], shapes)
            moved.append(moving)
            received.append([lax.ppermute(moving[way], AXES, rings[way]) for way in range(2)])

    def link_flow():
        gathered = parent_factor[None]
        for bit in link_bits:
            arrived = swap(gathered, "col", col_count, 1 << bit)
            if bit > 1:
                yield WAIT
            dims = (2 * gathered.shape[0],) + parent_factor.shape
            (gathered,) = yield (stack_step, [gathered, arrived], [shape(*dims)])
        held["links"] = heavy(
            functools.partial(link_kernel, children, 1.0 / row_count, link_order),
            [shape(children, width, width, dtype=BF16)] * 2
            + [shape(children, width, group, dtype=BF16)] * 2
            + [shape(children, diag_width, width), shape(children, width, half)],
            [info, gathered, diag_inverse, held["other diag"], held["chooser"], *held["own"][:2]],
            smem=1, vmem=20,
            scratch=[
                pltpu.VMEM((children, width, width), F32),
                pltpu.VMEM((2 * diag_width, width), F32),
                pltpu.VMEM((2 * diag_width, width), F32),
            ],
        )

    def prepare_flow():
        other_region = swap(region_inverse, "col", col_count, 1)
        held["other diag"] = swap(diag_inverse[:1], "col", col_count, 1)
        (held["chooser"],) = heavy(
            functools.partial(chooser_kernel, row_count, col_count),
            [shape(width, width, dtype=BF16)],
            [info],
            smem=1,
        )
        held["own"] = heavy(
            own_kernel,
            [shape(members, group, width, dtype=BF16)] * 2
            + [shape(members, width, group, dtype=BF16)] * 2,
            [info, listed, factor_cols, held["chooser"]],
            smem=2, hbm=1,
            scratch=[
                pltpu.VMEM((members, group, width), F32), pltpu.SemaphoreType.DMA((members,))
            ],
        )
        yield WAIT
        held["region"] = heavy(
            functools.partial(region_kernel, order),
            [shape(rows_here, 2 * cols_here, dtype=BF16)] * 2,
            [info, region_inverse, other_region],
            smem=1, hbm=2, vmem=12,
            scratch=[
                pltpu.VMEM((2, rows_here, cols_here), F32),
                pltpu.SemaphoreType.DMA((2, levels)),
            ],
        )
        for member in range(1, members):
            yield WAIT
            held["turned", member] = heavy(
                functools.partial(factor_kernel, order, member),
                [shape(width, rows_here, dtype=BF16)] * 2,
                [info, listed, factor_cols, held["chooser"]],
                smem=2, hbm=1, vmem=20,
                scratch=[
                    pltpu.VMEM((rows_here, width), F32), pltpu.SemaphoreType.DMA((levels,))
                ],
            )

    def unit_flow(member):
        chunk = (member + 1) * cuts - 1
        while len(received) < chunk + row_count - 1:
            yield WAIT
        final = member == members - 1
        if not final:
            yield WAIT
        candidates = []
        for at in range(member * cuts, (member + 1) * cuts):
            for way in range(2):
                candidates.append(moved[at][way])
                candidates += [received[at + hop][way] for hop in range(row_count - 1)]
        size = rows_here // 2
        keep, send = heavy(
            functools.partial(unit_kernel, row_count, ratio, cuts),
            [shape(size, half)] * 2,
            [info, *held["region"], *candidates],
            smem=1, vmem=16,
        )
        first = (keep, send)
        for bit in range(1, col_bits):
            arrived = swap(send, "col", col_count, 1 << bit)
            if bit == 1:
                if final:
                    yield WAIT
                if member:
                    held["gram", member] = heavy(
                        unit_gram_kernel,
                        [shape(width, half)],
                        [*held["turned", member], *first],
                        vmem=16,
                    )[0]
                if not final:
                    yield WAIT
            if bit + 1 < col_bits:
                size //= 2
                keep, send = yield (halve_step, [keep, arrived], [shape(size, half)] * 2)
        if member == 0:
            held["last", 0] = [keep, arrived]
            return
        mine, theirs = yield (part_step, [keep, arrived], [shape(size // 2, half)] * 2)
        held["sum", member] = [mine, swap(theirs, "col", col_count, 1)]

    def total_flow(name, pieces, direct):
        count, size, _ = pieces[0].shape
        inputs = [pieces[0]] + [swap(pieces[d], "row", row_count, d) for d in range(1, row_count)]
        if direct:
            size //= levels
            pieces = yield (halve_step, inputs, [shape(count, size, half)] * levels)
            inputs = [pieces[0]]
            for at in range(1, levels):
                inputs.append(swap(pieces[at], "col", col_count, order[at] << 1))
        else:
            for bit in range(1, col_bits):
                size //= 2
                keep, send = yield (halve_step, inputs, [shape(count, size, half)] * 2)
                inputs = [keep, swap(send, "col", col_count, 1 << bit)]
        size //= 2
        keep, send = yield (halve_step, inputs, [shape(count, size, half)] * 2)
        held[name] = [keep, swap(send, "col", col_count, 1)]

    def gather_flow():
        while "parent totals" not in held or "child totals" not in held:
            yield WAIT
        pairs = held["parent totals"] + held["child totals"]
        (piece,) = yield (join_step, pairs, [shape(members + children, part, width)])
        held["totals"] = [piece] + [swap(piece, "row", row_count, d) for d in range(1, row_count)]

    def parent_flow():
        names = [("last", 0), "links"]
        while any(name not in held for name in names):
            yield WAIT
        yield WAIT
        (mine,) = heavy(
            functools.partial(step_kernel, [(halve_step, 2, 1)]),
            [shape(group, half)],
            [info, *held["last", 0]],
            smem=1,
        )
        other = swap(mine, "col", col_count, 1)
        col, turned, *rest = heavy(
            functools.partial(parent_kernel, children, rows_here),
            [shape(group // 2, width), shape(children, group // 2, width)]
            + [shape(children, group, width, dtype=BF16)] * 2
            + [shape(members, width // row_count, half)] * row_count,
            [info, listed, held["chooser"], *held["own"], *held["links"][:2], mine, other],
            smem=2, vmem=20,
            scratch=[pltpu.VMEM((group, width), F32)],
        )
        held["parent"] = (col, turned, rest[:2])
        yield WAIT
        yield from total_flow("parent totals", rest[2:], False)

    def child_flow():
        names = [("gram", 1 + c) for c in range(children)]
        while any(name not in held for name in names + ["parent"]):
            yield WAIT
        pieces = heavy(
            functools.partial(child_kernel, children),
            [shape(children, width // row_count, half)] * row_count,
            [info, held["chooser"], *held["own"], *held["parent"][2], *held["links"][2:4]]
            + [held["links"][5]]
            + [held[name] for name in names],
            smem=1, vmem=20,
        )
        yield WAIT
        yield from total_flow("child totals", pieces, True)

    def column_flow():
        names = [("sum", 1 + c) for c in range(children)]
        while any(name not in held for name in names + ["parent"]):
            yield WAIT
        col, turned, _ = held["parent"]
        held["columns"] = heavy(
            functools.partial(column_kernel, children, rows_here),
            [shape(members, group // 2, width)],
            [info, listed, col, turned] + [value for name in names for value in held[name]],
            smem=2, target=pltpu.HBM,
            scratch=[
                pltpu.VMEM((members, group // 2, width), F32), pltpu.SemaphoreType.DMA(())
            ],
        )[0]

    flows = [ring_flow()] + [unit_flow(member) for member in range(children)]
    flows += [link_flow(), prepare_flow(), parent_flow()]
    flows += [unit_flow(children), child_flow(), gather_flow(), column_flow()]
    waiting = [(flow, None) for flow in flows]
    while waiting:
        tasks = [wish for _, wish in waiting if wish not in (None, WAIT)]
        results = iter(())
        if tasks:
            outs = [out for _, _, shapes in tasks for out in shapes]
            args = [value for _, values, _ in tasks for value in values]
            sizes = [(body, len(values), len(shapes)) for body, values, shapes in tasks]
            results = iter(
                heavy(functools.partial(step_kernel, sizes), outs, [info, *args], smem=1)
            )
        answered = []
        for flow, wish in waiting:
            answer = None
            if wish not in (None, WAIT):
                answer = [next(results) for _ in wish[2]]
            answered.append((flow, answer))
        waiting = []
        for flow, answer in answered:
            try:
                waiting.append((flow, flow.send(answer)))
            except StopIteration:
                pass

    diags, uppers = heavy(
        functools.partial(finish_kernel, row_count),
        [shape(members, diag_width, width), shape(children, diag_width, width)],
        [info, diag_inverse, held["links"][4]] + held["totals"],
        smem=1,
    )
    return held["columns"], diags, uppers


def solution(mesh):
    in_specs = (
        P("row", "col"),
        P(None, "row", None),
        P(None, "col", None),
        P(None, "col", None),
        P(),
    )
    out_specs = (P(None, ("row", "col"), None), P(None, "col", None), P(None, "col", None))
    return jax.shard_map(shards, mesh=mesh, in_specs=in_specs, out_specs=out_specs, check_vma=False)
```

```python
import functools

import jax
import jax.numpy as jnp
from jax import lax
from jax.experimental import pallas as pl
from jax.experimental.pallas import tpu as pltpu
from jax.sharding import PartitionSpec as P

AXES = ("row", "col")
F32 = jnp.float32
BF16 = jnp.bfloat16
NN = (((1,), (0,)), ((), ()))
NT = (((1,), (1,)), ((), ()))
MIB = 1024 * 1024
WAIT = ("wait",)


def split(value):
    high = value.astype(BF16)
    return high, (value - high.astype(F32)).astype(BF16)


def one_pass(left, right, dims=NN):
    return lax.dot_general(left, right, dims, preferred_element_type=F32)


def product(left, right):
    return one_pass(left[0], right[0]) + (
        one_pass(left[0], right[1]) + one_pass(left[1], right[0])
    )


def turn(chooser, pair):
    return [one_pass(chooser, half, NT).astype(BF16) for half in pair]


def pair_of(high_ref, low_ref, *index):
    return (high_ref[index], low_ref[index]) if index else (high_ref[...], low_ref[...])


def store_pair(high_ref, low_ref, pair, *index):
    index = index if index else ...
    high_ref[index], low_ref[index] = pair


def shape(*dims, dtype=F32):
    return jax.ShapeDtypeStruct(dims, dtype)


def gray(place):
    return place ^ (place >> 1)


def reversed_bits(count):
    order = [0]
    step = 1
    while step < count:
        order = [value + bit * step for value in order for bit in (0, 1)]
        step *= 2
    return order


def swap(value, axis, size, change):
    return lax.ppermute(value, axis, [(place, place ^ change) for place in range(size)])


def block(index, size):
    return pl.ds(pl.multiple_of(index * size, size), size)


def core_of(info_ref):
    return info_ref[1] & 1


def call(body, outs, args, smem=0, hbm=0, scratch=(), vmem=8, after=None):
    places = [pltpu.SMEM] * smem + [pltpu.HBM] * hbm
    places += [pltpu.VMEM] * (len(args) - len(places))
    count = len(args)
    args = list(args)
    inner = body
    if after is not None:
        args.append(after)
        places.append(pl.ANY)

        def inner(*refs):
            body(*refs[:count], *refs[count + 1 :])

    results = pl.pallas_call(
        inner,
        out_shape=outs,
        in_specs=[pl.BlockSpec(memory_space=place) for place in places],
        out_specs=[pl.BlockSpec(memory_space=pltpu.VMEM)] * len(outs),
        scratch_shapes=scratch,
        compiler_params=pltpu.CompilerParams(vmem_limit_bytes=vmem * MIB),
        cost_estimate=pl.CostEstimate(flops=1024, bytes_accessed=1024, transcendentals=0),
    )(*args)
    return list(results)


def cut_kernel(ratio, cuts, members, info_ref, listed_ref, factors_ref, *refs):
    *outs, sems = refs
    size, unit = outs[0].shape
    width = factors_ref.shape[2]
    column = info_ref[1]
    pair = (column % ratio) // 2
    copies = []
    for at, out_ref in enumerate(outs):
        member, cut, way = members[at // (2 * cuts)], at // 2 % cuts, at % 2
        source = factors_ref.at[
            member, block(2 * pair + way, size), block(core_of(info_ref) * cuts + cut, unit)
        ]
        copies.append(pltpu.make_async_copy(source, out_ref, sems.at[at]))
        copies[-1].start()
    for at, out_ref in enumerate(outs):
        copies[at].wait()
        owner = column - core_of(info_ref) + at % 2
        weight = listed_ref[members[at // (2 * cuts)], owner * size // width]
        out_ref[...] = out_ref[...] * weight.astype(F32)


def chooser_kernel(rows, columns, info_ref, out_ref):
    width = out_ref.shape[0]
    size = width // columns
    part = size // rows
    place = lax.broadcasted_iota(jnp.int32, out_ref.shape, 0)
    inner = place % part
    core = place // part % 2
    level = place // (2 * part) % (columns // 2)
    by_row = place // (2 * part * (columns // 2))
    turned = jnp.zeros_like(level)
    bits = (columns // 2).bit_length() - 1
    for bit in range(bits):
        turned = turned | (((level >> bit) & 1) << (bits - 1 - bit))
    column = (turned * 2 + core) ^ info_ref[1]
    wanted = column * size + (by_row ^ info_ref[0]) * part + inner
    hit = wanted == lax.broadcasted_iota(jnp.int32, out_ref.shape, 1)
    out_ref[...] = hit.astype(F32).astype(BF16)


def region_kernel(order, info_ref, own_ref, other_ref, high_ref, low_ref, held_ref, sems):
    groups = len(order)
    size = own_ref.shape[0] // groups
    width = own_ref.shape[1]
    column = info_ref[1] >> 1
    copies = []
    for g in range(groups):
        for side, source_ref in enumerate((own_ref, other_ref)):
            copies.append(
                pltpu.make_async_copy(
                    source_ref.at[block(order[g] ^ column, size), :],
                    held_ref.at[side, pl.ds(g * size, size), :],
                    sems.at[side, g],
                )
            )
            copies[-1].start()
    for g in range(groups):
        rows = slice(g * size, (g + 1) * size)
        for side in range(2):
            copies[2 * g + side].wait()
            columns = block(core_of(info_ref) ^ side, width)
            high, low = split(held_ref[side, rows, :])
            high_ref[rows, columns] = high
            low_ref[rows, columns] = low


def factor_kernel(
    order, member, info_ref, listed_ref, factors_ref, chooser_ref, high_ref, low_ref, held_ref, sems
):
    groups = len(order)
    _, rows_here, width = factors_ref.shape
    size = rows_here // groups
    column = info_ref[1] >> 1
    copies = []
    for g in range(groups):
        copies.append(
            pltpu.make_async_copy(
                factors_ref.at[member, block(order[g] ^ column, size), :],
                held_ref.at[pl.ds(g * size, size), :],
                sems.at[g],
            )
        )
        copies[-1].start()
    for g in range(groups):
        copies[g].wait()
        rows = slice(g * size, (g + 1) * size)
        first = info_ref[0] * rows_here + (order[g] ^ column) * size
        held_ref[rows, :] = held_ref[rows, :] * listed_ref[member, first // width].astype(F32)
    store_pair(high_ref, low_ref, turn(chooser_ref[...], split(held_ref[...])))


def own_weight(info_ref, listed_ref, member, size, rows_here, width):
    first = info_ref[0] * rows_here + (info_ref[1] >> 1) * size
    return listed_ref[member, first // width].astype(F32)


def own_kernel(
    info_ref, listed_ref, factors_ref, chooser_ref, high_ref, low_ref, thigh_ref, tlow_ref,
    held_ref, sems,
):
    members, rows, width = held_ref.shape
    copies = []
    for j in range(members):
        copies.append(
            pltpu.make_async_copy(
                factors_ref.at[j, block(info_ref[1] >> 1, rows), :], held_ref.at[j], sems.at[j]
            )
        )
        copies[-1].start()
    for j in range(members):
        copies[j].wait()
        weight = own_weight(info_ref, listed_ref, j, rows, factors_ref.shape[1], width)
        pair = split(held_ref[j] * weight)
        store_pair(high_ref, low_ref, pair, j)
        store_pair(thigh_ref, tlow_ref, turn(chooser_ref[...], pair), j)


def link_kernel(
    children, share, order, info_ref, gathered_ref, diag_ref, other_ref, chooser_ref,
    own_high_ref, own_low_ref, high_ref, low_ref, lift_high_ref, lift_low_ref, framed_ref,
    corner_ref, held_ref, rows_ref, frame_ref,
):
    groups, _, size, width = gathered_ref.shape
    half = corner_ref.shape[2]
    core = core_of(info_ref)
    chooser = chooser_ref[...]
    for g in range(groups):
        for c in range(children):
            held_ref[c, block(info_ref[1] ^ order[g], size), :] = gathered_ref[g, c]
    rows_ref[block(core, size), :] = diag_ref[0]
    rows_ref[block(1 - core, size), :] = other_ref[0]
    diag = split(rows_ref[...])
    for c in range(children):
        pair = split(held_ref[c])
        store_pair(high_ref, low_ref, pair, c)
        lifted = product(pair_of(own_high_ref, own_low_ref, 0), pair)
        store_pair(lift_high_ref, lift_low_ref, turn(chooser, split(lifted)), c)
        frame_ref[...] = product(diag, pair)
        framed_ref[c] = frame_ref[block(core, size), :]
        slices = split(held_ref[c, block(info_ref[1] >> 1, 2 * size), :])
        corner = product(turn(chooser, slices), split(frame_ref[:, block(core, half)]))
        corner_ref[c] = share * corner


def unit_kernel(count, ratio, cuts, info_ref, high_ref, low_ref, *refs):
    keep_ref, send_ref = refs[-2:]
    middle = keep_ref.shape[0]
    place = info_ref[0] ^ (info_ref[1] // ratio)
    shift = 1
    while shift < count:
        place = place ^ (place >> shift)
        shift *= 2
    places = (place, (count - place) % count)
    parts = []
    for cut in range(cuts):
        chosen = []
        for way in range(2):
            candidates = refs[(2 * cut + way) * count :][:count]
            value = candidates[0][...]
            for at in range(1, count):
                value = jnp.where(places[way] == at, candidates[at][...], value)
            chosen.append(value)
        parts.append(jnp.concatenate(chosen))
    right = split(jnp.concatenate(parts, axis=1))
    send_ref[...] = product((high_ref[middle:], low_ref[middle:]), right)
    keep_ref[...] = product((high_ref[:middle], low_ref[:middle]), right)


def unit_gram_kernel(high_ref, low_ref, keep_ref, send_ref, out_ref):
    middle = keep_ref.shape[0]
    out_ref[...] = product(
        (high_ref[:, :middle], low_ref[:, :middle]), split(keep_ref[...])
    ) + product((high_ref[:, middle:], low_ref[:, middle:]), split(send_ref[...]))


def store_parts(refs, index, value):
    size = refs[0].shape[1]
    for at, ref in enumerate(refs):
        ref[index] = value[at * size : (at + 1) * size]


def parent_kernel(
    children, rows_here, info_ref, listed_ref, chooser_ref, own_high_ref, own_low_ref,
    own_thigh_ref, own_tlow_ref, link_high_ref, link_low_ref, mine_ref, other_ref,
    col_ref, high_ref, low_ref, *refs
):
    *outs, full_ref = refs
    chooser = chooser_ref[...]
    rows, half = mine_ref.shape
    core = core_of(info_ref)
    weight = own_weight(info_ref, listed_ref, 0, rows, rows_here, chooser.shape[0])
    mine = -mine_ref[...] * weight
    full_ref[:, block(core, half)] = mine
    full_ref[:, block(1 - core, half)] = -other_ref[...] * weight
    col_ref[...] = full_ref[block(core, rows // 2), :]
    pair = split(full_ref[...])
    store_pair(high_ref, low_ref, pair)
    turned_pair = turn(chooser, pair)
    parent = pair_of(own_thigh_ref, own_tlow_ref, 0)
    columns = block(core, half)
    store_parts(outs, 0, -product(parent, split(mine)))
    for c in range(children):
        link = (link_high_ref[c, :, columns], link_low_ref[c, :, columns])
        lifted = split(product(pair, link))
        own = (own_high_ref[c + 1, :, columns], own_low_ref[c + 1, :, columns])
        store_parts(outs, 1 + c, product(parent, lifted) - product(turned_pair, own))


def child_kernel(
    children, info_ref, chooser_ref, own_high_ref, own_low_ref, own_thigh_ref, own_tlow_ref,
    high_ref, low_ref, link_high_ref, link_low_ref, lift_high_ref, lift_low_ref, corner_ref, *refs
):
    *refs, full_ref = refs
    grams, outs, turned_ref = refs[:children], refs[children:-1], refs[-1]
    core = core_of(info_ref)
    columns = block(core, corner_ref.shape[2])
    pair = pair_of(high_ref, low_ref)
    for c in range(children):
        full_ref[...] = product(pair, pair_of(link_high_ref, link_low_ref, c))
        turned_ref[c] = full_ref[block(core, full_ref.shape[0] // 2), :]
        lifted = split(full_ref[:, columns])
        turned_pair = turn(chooser_ref[...], split(full_ref[...]))
        own = (own_high_ref[c + 1, :, columns], own_low_ref[c + 1, :, columns])
        total = corner_ref[c] + grams[c][...]
        total += product(pair_of(own_thigh_ref, own_tlow_ref, c + 1), lifted)
        total += product(turned_pair, own)
        total -= product(pair_of(lift_high_ref, lift_low_ref, c), lifted)
        store_parts(outs, c, total)


def column_kernel(children, rows_here, info_ref, listed_ref, col_ref, turned_ref, *refs):
    out_ref = refs[-1]
    rows, width = col_ref.shape
    half = width // 2
    core = core_of(info_ref)
    out_ref[0] = col_ref[...]
    for c in range(children):
        weight = own_weight(info_ref, listed_ref, c + 1, 2 * rows, rows_here, width)
        for side in range(2):
            columns = block(core ^ side, half)
            total = refs[2 * c + side][...] + turned_ref[c, :, columns]
            out_ref[c + 1, :, columns] = -total * weight


def finish_kernel(rows, info_ref, diag_ref, framed_ref, *refs):
    pieces = refs[:rows]
    diags_ref, uppers_ref = refs[rows:]
    part = pieces[0].shape[1]
    children = uppers_ref.shape[0]
    for row in range(rows):
        at = slice(row * part, (row + 1) * part)
        value = pieces[0][...]
        for change in range(1, rows):
            value = jnp.where(info_ref[0] ^ change == row, pieces[change][...], value)
        diags_ref[0, at] = diag_ref[0, at] + value[0]
        uppers_ref[:, at] = value[1 : 1 + children] - framed_ref[:, at]
        diags_ref[1:, at] = diag_ref[1:, at] + value[1 + children :]


def select_step(ratio, info_ref, ins, outs):
    source = info_ref[0] == info_ref[1] // ratio
    for way in range(2):
        outs[way][...] = jnp.where(source, ins[way][...], ins[2 + way][...])


def pass_step(info_ref, ins, outs):
    for way in range(2):
        outs[way][...] = ins[way][...]


def stack_step(info_ref, ins, outs):
    for at in range(ins[0].shape[0]):
        for side in range(2):
            outs[0][2 * at + side] = ins[side][at]


def halve_step(info_ref, ins, outs):
    size = outs[0].shape[-2]
    for at, out in enumerate(outs):
        rows = pl.ds(at * size, size)
        index = (rows,) if len(out.shape) == 2 else (slice(None), rows)
        total = ins[0][index]
        for other in ins[1:]:
            total = total + other[index]
        out[...] = total


def part_step(info_ref, ins, outs):
    size = outs[0].shape[0]
    for side, out in enumerate(outs):
        rows = block(core_of(info_ref) ^ side, size)
        total = ins[0][rows, :]
        for other in ins[1:]:
            total = total + other[rows, :]
        out[...] = total


def join_step(info_ref, ins, outs):
    first = 0
    for at in range(0, len(ins), 2):
        count, _, half = ins[at].shape
        for side in range(2):
            columns = block(core_of(info_ref) ^ side, half)
            outs[0][first : first + count, :, columns] = ins[at + side][...]
        first += count


def step_kernel(tasks, info_ref, *refs):
    start = 0
    end = sum(ins for _, ins, _ in tasks)
    for body, ins, outs in tasks:
        body(info_ref, refs[start : start + ins], refs[end : end + outs])
        start += ins
        end += outs


def shards(region_inverse, factor_cols, parent_factor, diag_inverse, listed):
    row_count = lax.axis_size("row")
    col_count = lax.axis_size("col")
    col_bits = col_count.bit_length() - 1
    rows_here, cols_here = region_inverse.shape
    members, _, width = factor_cols.shape
    children = members - 1
    levels = col_count // 2
    group = rows_here // levels
    ratio = col_count // row_count
    diag_width = width // col_count
    part = diag_width // row_count
    half = width // 2
    cuts = 1
    unit = half // cuts
    chunk_count = members * cuts
    order = reversed_bits(levels)
    stages = chunk_count + row_count - 2

    def ring(forward):
        pairs = []
        for col in range(col_count):
            start = col // ratio
            for place in range(row_count):
                at = (start ^ gray(place)) * col_count + col
                to = (start ^ gray((place + 1) % row_count)) * col_count + col
                pairs.append((at, to) if forward else (to, at))
        return pairs

    rings = (ring(True), ring(False))
    link_bits = [*range(1, col_bits), 0]
    link_order = [0]
    for bit in link_bits:
        link_order = [value ^ (side << bit) for value in link_order for side in range(2)]
    info = jnp.stack([lax.axis_index("row"), lax.axis_index("col")]).astype(jnp.int32)

    def cut(chosen, run):
        count = len(chosen) * cuts * 2
        flat = run(
            functools.partial(cut_kernel, ratio, cuts, chosen),
            [shape(cols_here, unit)] * count,
            [info, listed, factor_cols],
            smem=2, hbm=1, vmem=48,
            scratch=[pltpu.SemaphoreType.DMA((count,))],
        )
        return [flat[at : at + 2] for at in range(0, count, 2)]

    chunks = cut((0,), call)

    last = [chunks[0][0]]
    held = {}
    moved = []
    received = []

    def heavy(body, outs, args, **options):
        results = call(body, outs, args, after=last[0], **options)
        last[0] = results[0]
        return results

    chunks.extend(cut(tuple(range(1, members)), heavy))

    def ring_flow():
        shapes = [shape(cols_here, unit)] * 2
        for stage in range(stages):
            if stage == 0:
                moving = chunks[0]
            elif stage < chunk_count:
                step = functools.partial(select_step, ratio)
                moving = yield (step, chunks[stage] + received[-1], shapes)
            else:
                moving = yield (pass_step, received[-1], shapes)
            moved.append(moving)
            received.append([lax.ppermute(moving[way], AXES, rings[way]) for way in range(2)])

    def link_flow():
        gathered = parent_factor[None]
        for bit in link_bits:
            arrived = swap(gathered, "col", col_count, 1 << bit)
            dims = (2 * gathered.shape[0],) + parent_factor.shape
            if bit:
                if bit > 1:
                    yield WAIT
                (gathered,) = yield (stack_step, [gathered, arrived], [shape(*dims)])
            else:
                (gathered,) = heavy(
                    functools.partial(step_kernel, [(stack_step, 2, 1)]),
                    [shape(*dims)],
                    [info, gathered, arrived],
                    smem=1,
                )
        held["links"] = heavy(
            functools.partial(link_kernel, children, 1.0 / row_count, link_order),
            [shape(children, width, width, dtype=BF16)] * 2
            + [shape(children, width, group, dtype=BF16)] * 2
            + [shape(children, diag_width, width), shape(children, width, half)],
            [info, gathered, diag_inverse, held["other diag"], held["chooser"], *held["own"][:2]],
            smem=1, vmem=20,
            scratch=[
                pltpu.VMEM((children, width, width), F32),
                pltpu.VMEM((2 * diag_width, width), F32),
                pltpu.VMEM((2 * diag_width, width), F32),
            ],
        )

    def prepare_flow():
        other_region = swap(region_inverse, "col", col_count, 1)
        held["other diag"] = swap(diag_inverse[:1], "col", col_count, 1)
        (held["chooser"],) = heavy(
            functools.partial(chooser_kernel, row_count, col_count),
            [shape(width, width, dtype=BF16)],
            [info],
            smem=1,
        )
        held["own"] = heavy(
            own_kernel,
            [shape(members, group, width, dtype=BF16)] * 2
            + [shape(members, width, group, dtype=BF16)] * 2,
            [info, listed, factor_cols, held["chooser"]],
            smem=2, hbm=1,
            scratch=[
                pltpu.VMEM((members, group, width), F32), pltpu.SemaphoreType.DMA((members,))
            ],
        )
        yield WAIT
        held["region"] = heavy(
            functools.partial(region_kernel, order),
            [shape(rows_here, 2 * cols_here, dtype=BF16)] * 2,
            [info, region_inverse, other_region],
            smem=1, hbm=2, vmem=12,
            scratch=[
                pltpu.VMEM((2, rows_here, cols_here), F32),
                pltpu.SemaphoreType.DMA((2, levels)),
            ],
        )
        for member in range(1, members):
            yield WAIT
            held["turned", member] = heavy(
                functools.partial(factor_kernel, order, member),
                [shape(width, rows_here, dtype=BF16)] * 2,
                [info, listed, factor_cols, held["chooser"]],
                smem=2, hbm=1, vmem=20,
                scratch=[
                    pltpu.VMEM((rows_here, width), F32), pltpu.SemaphoreType.DMA((levels,))
                ],
            )

    def unit_flow(member):
        chunk = (member + 1) * cuts - 1
        while len(received) < chunk + row_count - 1:
            yield WAIT
        final = member == members - 1
        if not final:
            yield WAIT
        candidates = []
        for at in range(member * cuts, (member + 1) * cuts):
            for way in range(2):
                candidates.append(moved[at][way])
                candidates += [received[at + hop][way] for hop in range(row_count - 1)]
        size = rows_here // 2
        keep, send = heavy(
            functools.partial(unit_kernel, row_count, ratio, cuts),
            [shape(size, half)] * 2,
            [info, *held["region"], *candidates],
            smem=1, vmem=16,
        )
        first = (keep, send)
        for bit in range(1, col_bits):
            arrived = swap(send, "col", col_count, 1 << bit)
            if bit == 1:
                if final:
                    yield WAIT
                if member:
                    held["gram", member] = heavy(
                        unit_gram_kernel,
                        [shape(width, half)],
                        [*held["turned", member], *first],
                        vmem=16,
                    )[0]
            if bit + 1 < col_bits:
                size //= 2
                keep, send = yield (halve_step, [keep, arrived], [shape(size, half)] * 2)
        if member == 0:
            held["last", 0] = [keep, arrived]
            return
        mine, theirs = yield (part_step, [keep, arrived], [shape(size // 2, half)] * 2)
        held["sum", member] = [mine, swap(theirs, "col", col_count, 1)]

    def total_flow(name, pieces, direct):
        count, size, _ = pieces[0].shape
        inputs = [pieces[0]] + [swap(pieces[d], "row", row_count, d) for d in range(1, row_count)]
        if direct:
            size //= levels
            pieces = yield (halve_step, inputs, [shape(count, size, half)] * levels)
            inputs = [pieces[0]]
            for at in range(1, levels):
                inputs.append(swap(pieces[at], "col", col_count, order[at] << 1))
        else:
            for bit in range(1, col_bits):
                size //= 2
                keep, send = yield (halve_step, inputs, [shape(count, size, half)] * 2)
                inputs = [keep, swap(send, "col", col_count, 1 << bit)]
        size //= 2
        keep, send = yield (halve_step, inputs, [shape(count, size, half)] * 2)
        held[name] = [keep, swap(send, "col", col_count, 1)]

    def gather_flow():
        while "parent totals" not in held or "child totals" not in held:
            yield WAIT
        pairs = held["parent totals"] + held["child totals"]
        (piece,) = yield (join_step, pairs, [shape(members + children, part, width)])
        held["totals"] = [piece] + [swap(piece, "row", row_count, d) for d in range(1, row_count)]

    def parent_flow():
        names = [("last", 0), "links"]
        while any(name not in held for name in names):
            yield WAIT
        (mine,) = heavy(
            functools.partial(step_kernel, [(halve_step, 2, 1)]),
            [shape(group, half)],
            [info, *held["last", 0]],
            smem=1,
        )
        other = swap(mine, "col", col_count, 1)
        col, *rest = heavy(
            functools.partial(parent_kernel, children, rows_here),
            [shape(group // 2, width)]
            + [shape(group, width, dtype=BF16)] * 2
            + [shape(members, width // row_count, half)] * row_count,
            [info, listed, held["chooser"], *held["own"], *held["links"][:2], mine, other],
            smem=2, vmem=20,
            scratch=[pltpu.VMEM((group, width), F32)],
        )
        held["parent"] = (col, rest[:2])
        yield WAIT
        yield from total_flow("parent totals", rest[2:], False)

    def child_flow():
        names = [("gram", 1 + c) for c in range(children)]
        while any(name not in held for name in names + ["parent"]):
            yield WAIT
        *pieces, held["lifted"] = heavy(
            functools.partial(child_kernel, children),
            [shape(children, width // row_count, half)] * row_count
            + [shape(children, group // 2, width)],
            [info, held["chooser"], *held["own"], *held["parent"][1], *held["links"][:4]]
            + [held["links"][5]]
            + [held[name] for name in names],
            smem=1, vmem=20,
            scratch=[pltpu.VMEM((group, width), F32)],
        )
        yield WAIT
        yield from total_flow("child totals", pieces, True)

    def column_flow():
        names = [("sum", 1 + c) for c in range(children)]
        while any(name not in held for name in names + ["parent"]):
            yield WAIT
        while "totals" not in held:
            yield WAIT
        col, turned = held["parent"][0], held["lifted"]
        held["columns"] = heavy(
            functools.partial(column_kernel, children, rows_here),
            [shape(members, group // 2, width)],
            [info, listed, col, turned] + [value for name in names for value in held[name]],
            smem=2,
        )[0]

    flows = [ring_flow()] + [unit_flow(member) for member in range(children)]
    flows += [link_flow(), prepare_flow(), parent_flow()]
    flows += [unit_flow(children), child_flow(), gather_flow(), column_flow()]
    waiting = [(flow, None) for flow in flows]
    while waiting:
        tasks = [wish for _, wish in waiting if wish not in (None, WAIT)]
        results = iter(())
        if tasks:
            outs = [out for _, _, shapes in tasks for out in shapes]
            args = [value for _, values, _ in tasks for value in values]
            sizes = [(body, len(values), len(shapes)) for body, values, shapes in tasks]
            results = iter(
                heavy(functools.partial(step_kernel, sizes), outs, [info, *args], smem=1)
            )
        answered = []
        for flow, wish in waiting:
            answer = None
            if wish not in (None, WAIT):
                answer = [next(results) for _ in wish[2]]
            answered.append((flow, answer))
        waiting = []
        for flow, answer in answered:
            try:
                waiting.append((flow, flow.send(answer)))
            except StopIteration:
                pass

    diags, uppers = heavy(
        functools.partial(finish_kernel, row_count),
        [shape(members, diag_width, width), shape(children, diag_width, width)],
        [info, diag_inverse, held["links"][4]] + held["totals"],
        smem=1,
    )
    return held["columns"], diags, uppers


def solution(mesh):
    in_specs = (
        P("row", "col"),
        P(None, "row", None),
        P(None, "col", None),
        P(None, "col", None),
        P(),
    )
    out_specs = (P(None, ("row", "col"), None), P(None, "col", None), P(None, "col", None))
    return jax.shard_map(shards, mesh=mesh, in_specs=in_specs, out_specs=out_specs, check_vma=False)
```

```python
import functools

import jax
import jax.numpy as jnp
from jax import lax
from jax.experimental import pallas as pl
from jax.experimental.pallas import tpu as pltpu
from jax.sharding import PartitionSpec as P

AXES = ("row", "col")
F32 = jnp.float32
BF16 = jnp.bfloat16
NN = (((1,), (0,)), ((), ()))
NT = (((1,), (1,)), ((), ()))
MIB = 1024 * 1024
WAIT = ("wait",)


def split(value):
    high = value.astype(BF16)
    return high, (value - high.astype(F32)).astype(BF16)


def one_pass(left, right, dims=NN):
    return lax.dot_general(left, right, dims, preferred_element_type=F32)


def product(left, right):
    return one_pass(left[0], right[0]) + (
        one_pass(left[0], right[1]) + one_pass(left[1], right[0])
    )


def turn(chooser, pair):
    return [one_pass(chooser, half, NT).astype(BF16) for half in pair]


def pair_of(high_ref, low_ref, *index):
    return (high_ref[index], low_ref[index]) if index else (high_ref[...], low_ref[...])


def store_pair(high_ref, low_ref, pair, *index):
    index = index if index else ...
    high_ref[index], low_ref[index] = pair


def shape(*dims, dtype=F32):
    return jax.ShapeDtypeStruct(dims, dtype)


def gray(place):
    return place ^ (place >> 1)


def reversed_bits(count):
    order = [0]
    step = 1
    while step < count:
        order = [value + bit * step for value in order for bit in (0, 1)]
        step *= 2
    return order


def swap(value, axis, size, change):
    return lax.ppermute(value, axis, [(place, place ^ change) for place in range(size)])


def block(index, size):
    return pl.ds(pl.multiple_of(index * size, size), size)


def core_of(info_ref):
    return info_ref[1] & 1


def call(body, outs, args, smem=0, hbm=0, scratch=(), vmem=8, after=None):
    places = [pltpu.SMEM] * smem + [pltpu.HBM] * hbm
    places += [pltpu.VMEM] * (len(args) - len(places))
    count = len(args)
    args = list(args)
    inner = body
    if after is not None:
        args.append(after)
        places.append(pl.ANY)

        def inner(*refs):
            body(*refs[:count], *refs[count + 1 :])

    results = pl.pallas_call(
        inner,
        out_shape=outs,
        in_specs=[pl.BlockSpec(memory_space=place) for place in places],
        out_specs=[pl.BlockSpec(memory_space=pltpu.VMEM)] * len(outs),
        scratch_shapes=scratch,
        compiler_params=pltpu.CompilerParams(vmem_limit_bytes=vmem * MIB),
        cost_estimate=pl.CostEstimate(flops=1024, bytes_accessed=1024, transcendentals=0),
    )(*args)
    return list(results)


def cut_kernel(ratio, cuts, members, info_ref, factors_ref, *refs):
    *outs, sems = refs
    size, unit = outs[0].shape
    pair = (info_ref[1] % ratio) // 2
    copies = []
    for at, out_ref in enumerate(outs):
        member, cut, way = members[at // (2 * cuts)], at // 2 % cuts, at % 2
        source = factors_ref.at[
            member, block(2 * pair + way, size), block(core_of(info_ref) * cuts + cut, unit)
        ]
        copies.append(pltpu.make_async_copy(source, out_ref, sems.at[at]))
        copies[-1].start()
    for copy in copies:
        copy.wait()


def chooser_kernel(rows, columns, info_ref, out_ref):
    width = out_ref.shape[0]
    size = width // columns
    part = size // rows
    place = lax.broadcasted_iota(jnp.int32, out_ref.shape, 0)
    inner = place % part
    core = place // part % 2
    level = place // (2 * part) % (columns // 2)
    by_row = place // (2 * part * (columns // 2))
    turned = jnp.zeros_like(level)
    bits = (columns // 2).bit_length() - 1
    for bit in range(bits):
        turned = turned | (((level >> bit) & 1) << (bits - 1 - bit))
    column = (turned * 2 + core) ^ info_ref[1]
    wanted = column * size + (by_row ^ info_ref[0]) * part + inner
    hit = wanted == lax.broadcasted_iota(jnp.int32, out_ref.shape, 1)
    out_ref[...] = hit.astype(F32).astype(BF16)


def region_kernel(order, info_ref, own_ref, other_ref, high_ref, low_ref, held_ref, sems):
    groups = len(order)
    size = own_ref.shape[0] // groups
    width = own_ref.shape[1]
    column = info_ref[1] >> 1
    copies = []
    for g in range(groups):
        for side, source_ref in enumerate((own_ref, other_ref)):
            copies.append(
                pltpu.make_async_copy(
                    source_ref.at[block(order[g] ^ column, size), :],
                    held_ref.at[side, pl.ds(g * size, size), :],
                    sems.at[side, g],
                )
            )
            copies[-1].start()
    for g in range(groups):
        rows = slice(g * size, (g + 1) * size)
        for side in range(2):
            copies[2 * g + side].wait()
            columns = block(core_of(info_ref) ^ side, width)
            high, low = split(held_ref[side, rows, :])
            high_ref[rows, columns] = high
            low_ref[rows, columns] = low


def factor_kernel(
    order, member, info_ref, listed_ref, factors_ref, chooser_ref, high_ref, low_ref, held_ref, sems
):
    groups = len(order)
    _, rows_here, width = factors_ref.shape
    size = rows_here // groups
    column = info_ref[1] >> 1
    copies = []
    for g in range(groups):
        copies.append(
            pltpu.make_async_copy(
                factors_ref.at[member, block(order[g] ^ column, size), :],
                held_ref.at[pl.ds(g * size, size), :],
                sems.at[g],
            )
        )
        copies[-1].start()
    for g in range(groups):
        copies[g].wait()
        rows = slice(g * size, (g + 1) * size)
        first = info_ref[0] * rows_here + (order[g] ^ column) * size
        held_ref[rows, :] = held_ref[rows, :] * listed_ref[member, first // width].astype(F32)
    store_pair(high_ref, low_ref, turn(chooser_ref[...], split(held_ref[...])))


def own_weight(info_ref, listed_ref, member, size, rows_here, width):
    first = info_ref[0] * rows_here + (info_ref[1] >> 1) * size
    return listed_ref[member, first // width].astype(F32)


def own_kernel(
    info_ref, listed_ref, factors_ref, chooser_ref, high_ref, low_ref, thigh_ref, tlow_ref,
    held_ref, sems,
):
    members, rows, width = held_ref.shape
    copies = []
    for j in range(members):
        copies.append(
            pltpu.make_async_copy(
                factors_ref.at[j, block(info_ref[1] >> 1, rows), :], held_ref.at[j], sems.at[j]
            )
        )
        copies[-1].start()
    for j in range(members):
        copies[j].wait()
        weight = own_weight(info_ref, listed_ref, j, rows, factors_ref.shape[1], width)
        pair = split(held_ref[j] * weight)
        store_pair(high_ref, low_ref, pair, j)
        store_pair(thigh_ref, tlow_ref, turn(chooser_ref[...], pair), j)


def link_kernel(
    children, share, order, info_ref, gathered_ref, diag_ref, other_ref, chooser_ref,
    own_high_ref, own_low_ref, high_ref, low_ref, lift_high_ref, lift_low_ref, framed_ref,
    corner_ref, held_ref, rows_ref, frame_ref,
):
    groups, _, size, width = gathered_ref.shape
    half = corner_ref.shape[2]
    core = core_of(info_ref)
    chooser = chooser_ref[...]
    for g in range(groups):
        for c in range(children):
            held_ref[c, block(info_ref[1] ^ order[g], size), :] = gathered_ref[g, c]
    rows_ref[block(core, size), :] = diag_ref[0]
    rows_ref[block(1 - core, size), :] = other_ref[0]
    diag = split(rows_ref[...])
    for c in range(children):
        pair = split(held_ref[c])
        store_pair(high_ref, low_ref, pair, c)
        lifted = product(pair_of(own_high_ref, own_low_ref, 0), pair)
        store_pair(lift_high_ref, lift_low_ref, turn(chooser, split(lifted)), c)
        frame_ref[...] = product(diag, pair)
        framed_ref[c] = frame_ref[block(core, size), :]
        slices = split(held_ref[c, block(info_ref[1] >> 1, 2 * size), :])
        corner = product(turn(chooser, slices), split(frame_ref[:, block(core, half)]))
        corner_ref[c] = share * corner


def unit_kernel(count, ratio, cuts, member, info_ref, listed_ref, high_ref, low_ref, *refs):
    keep_ref, send_ref = refs[-2:]
    middle = keep_ref.shape[0]
    place = info_ref[0] ^ (info_ref[1] // ratio)
    shift = 1
    while shift < count:
        place = place ^ (place >> shift)
        shift *= 2
    places = (place, (count - place) % count)
    parts = []
    for cut in range(cuts):
        chosen = []
        for way in range(2):
            candidates = refs[(2 * cut + way) * count :][:count]
            value = candidates[0][...]
            for at in range(1, count):
                value = jnp.where(places[way] == at, candidates[at][...], value)
            owner = info_ref[1] - core_of(info_ref) + way
            weight = listed_ref[member, owner * value.shape[0] // (2 * cuts * value.shape[1])]
            chosen.append(value * weight.astype(F32))
        parts.append(jnp.concatenate(chosen))
    right = split(jnp.concatenate(parts, axis=1))
    send_ref[...] = product((high_ref[middle:], low_ref[middle:]), right)
    keep_ref[...] = product((high_ref[:middle], low_ref[:middle]), right)


def unit_gram_kernel(high_ref, low_ref, keep_ref, send_ref, out_ref):
    middle = keep_ref.shape[0]
    out_ref[...] = product(
        (high_ref[:, :middle], low_ref[:, :middle]), split(keep_ref[...])
    ) + product((high_ref[:, middle:], low_ref[:, middle:]), split(send_ref[...]))


def store_parts(refs, index, value):
    size = refs[0].shape[1]
    for at, ref in enumerate(refs):
        ref[index] = value[at * size : (at + 1) * size]


def parent_kernel(
    children, rows_here, info_ref, listed_ref, chooser_ref, own_high_ref, own_low_ref,
    own_thigh_ref, own_tlow_ref, link_high_ref, link_low_ref, mine_ref, other_ref,
    col_ref, high_ref, low_ref, *refs
):
    *outs, full_ref = refs
    chooser = chooser_ref[...]
    rows, half = mine_ref.shape
    core = core_of(info_ref)
    weight = own_weight(info_ref, listed_ref, 0, rows, rows_here, chooser.shape[0])
    mine = -mine_ref[...] * weight
    full_ref[:, block(core, half)] = mine
    full_ref[:, block(1 - core, half)] = -other_ref[...] * weight
    col_ref[...] = full_ref[block(core, rows // 2), :]
    pair = split(full_ref[...])
    store_pair(high_ref, low_ref, pair)
    turned_pair = turn(chooser, pair)
    parent = pair_of(own_thigh_ref, own_tlow_ref, 0)
    columns = block(core, half)
    store_parts(outs, 0, -product(parent, split(mine)))
    for c in range(children):
        link = (link_high_ref[c, :, columns], link_low_ref[c, :, columns])
        lifted = split(product(pair, link))
        own = (own_high_ref[c + 1, :, columns], own_low_ref[c + 1, :, columns])
        store_parts(outs, 1 + c, product(parent, lifted) - product(turned_pair, own))


def child_kernel(
    children, info_ref, chooser_ref, own_high_ref, own_low_ref, own_thigh_ref, own_tlow_ref,
    high_ref, low_ref, link_high_ref, link_low_ref, lift_high_ref, lift_low_ref, corner_ref, *refs
):
    *refs, full_ref = refs
    grams, outs, turned_ref = refs[:children], refs[children:-1], refs[-1]
    core = core_of(info_ref)
    columns = block(core, corner_ref.shape[2])
    pair = pair_of(high_ref, low_ref)
    for c in range(children):
        full_ref[...] = product(pair, pair_of(link_high_ref, link_low_ref, c))
        turned_ref[c] = full_ref[block(core, full_ref.shape[0] // 2), :]
        lifted = split(full_ref[:, columns])
        turned_pair = turn(chooser_ref[...], split(full_ref[...]))
        own = (own_high_ref[c + 1, :, columns], own_low_ref[c + 1, :, columns])
        total = corner_ref[c] + grams[c][...]
        total += product(pair_of(own_thigh_ref, own_tlow_ref, c + 1), lifted)
        total += product(turned_pair, own)
        total -= product(pair_of(lift_high_ref, lift_low_ref, c), lifted)
        store_parts(outs, c, total)


def column_kernel(children, rows_here, info_ref, listed_ref, col_ref, turned_ref, *refs):
    out_ref = refs[-1]
    rows, width = col_ref.shape
    half = width // 2
    core = core_of(info_ref)
    out_ref[0] = col_ref[...]
    for c in range(children):
        weight = own_weight(info_ref, listed_ref, c + 1, 2 * rows, rows_here, width)
        for side in range(2):
            columns = block(core ^ side, half)
            total = refs[2 * c + side][...] + turned_ref[c, :, columns]
            out_ref[c + 1, :, columns] = -total * weight


def finish_kernel(rows, info_ref, diag_ref, framed_ref, *refs):
    pieces = refs[:rows]
    diags_ref, uppers_ref = refs[rows:]
    part = pieces[0].shape[1]
    children = uppers_ref.shape[0]
    for row in range(rows):
        at = slice(row * part, (row + 1) * part)
        value = pieces[0][...]
        for change in range(1, rows):
            value = jnp.where(info_ref[0] ^ change == row, pieces[change][...], value)
        diags_ref[0, at] = diag_ref[0, at] + value[0]
        uppers_ref[:, at] = value[1 : 1 + children] - framed_ref[:, at]
        diags_ref[1:, at] = diag_ref[1:, at] + value[1 + children :]


def select_step(ratio, info_ref, ins, outs):
    source = info_ref[0] == info_ref[1] // ratio
    for way in range(2):
        outs[way][...] = jnp.where(source, ins[way][...], ins[2 + way][...])


def pass_step(info_ref, ins, outs):
    for way in range(2):
        outs[way][...] = ins[way][...]


def stack_step(info_ref, ins, outs):
    for at in range(ins[0].shape[0]):
        for side in range(2):
            outs[0][2 * at + side] = ins[side][at]


def halve_step(info_ref, ins, outs):
    size = outs[0].shape[-2]
    for at, out in enumerate(outs):
        rows = pl.ds(at * size, size)
        index = (rows,) if len(out.shape) == 2 else (slice(None), rows)
        total = ins[0][index]
        for other in ins[1:]:
            total = total + other[index]
        out[...] = total


def part_step(info_ref, ins, outs):
    size = outs[0].shape[0]
    for side, out in enumerate(outs):
        rows = block(core_of(info_ref) ^ side, size)
        total = ins[0][rows, :]
        for other in ins[1:]:
            total = total + other[rows, :]
        out[...] = total


def join_step(info_ref, ins, outs):
    first = 0
    for at in range(0, len(ins), 2):
        count, _, half = ins[at].shape
        for side in range(2):
            columns = block(core_of(info_ref) ^ side, half)
            outs[0][first : first + count, :, columns] = ins[at + side][...]
        first += count


def step_kernel(tasks, info_ref, *refs):
    start = 0
    end = sum(ins for _, ins, _ in tasks)
    for body, ins, outs in tasks:
        body(info_ref, refs[start : start + ins], refs[end : end + outs])
        start += ins
        end += outs


def shards(region_inverse, factor_cols, parent_factor, diag_inverse, listed):
    row_count = lax.axis_size("row")
    col_count = lax.axis_size("col")
    col_bits = col_count.bit_length() - 1
    rows_here, cols_here = region_inverse.shape
    members, _, width = factor_cols.shape
    children = members - 1
    levels = col_count // 2
    group = rows_here // levels
    ratio = col_count // row_count
    diag_width = width // col_count
    part = diag_width // row_count
    half = width // 2
    cuts = 1
    unit = half // cuts
    chunk_count = members * cuts
    order = reversed_bits(levels)
    stages = chunk_count + row_count - 2

    def ring(forward):
        pairs = []
        for col in range(col_count):
            start = col // ratio
            for place in range(row_count):
                at = (start ^ gray(place)) * col_count + col
                to = (start ^ gray((place + 1) % row_count)) * col_count + col
                pairs.append((at, to) if forward else (to, at))
        return pairs

    rings = (ring(True), ring(False))
    link_bits = [*range(1, col_bits), 0]
    link_order = [0]
    for bit in link_bits:
        link_order = [value ^ (side << bit) for value in link_order for side in range(2)]
    info = jnp.stack([lax.axis_index("row"), lax.axis_index("col")]).astype(jnp.int32)

    def cut(chosen, run):
        count = len(chosen) * cuts * 2
        flat = run(
            functools.partial(cut_kernel, ratio, cuts, chosen),
            [shape(cols_here, unit)] * count,
            [info, factor_cols],
            smem=1, hbm=1, vmem=48,
            scratch=[pltpu.SemaphoreType.DMA((count,))],
        )
        return [flat[at : at + 2] for at in range(0, count, 2)]

    chunks = cut((0,), call)

    last = [chunks[0][0]]
    held = {}
    moved = []
    received = []

    def heavy(body, outs, args, **options):
        results = call(body, outs, args, after=last[0], **options)
        last[0] = results[0]
        return results

    chunks.extend(cut(tuple(range(1, members)), heavy))

    def ring_flow():
        shapes = [shape(cols_here, unit)] * 2
        for stage in range(stages):
            if stage == 0:
                moving = chunks[0]
            elif stage < chunk_count:
                step = functools.partial(select_step, ratio)
                moving = yield (step, chunks[stage] + received[-1], shapes)
            else:
                moving = yield (pass_step, received[-1], shapes)
            moved.append(moving)
            received.append([lax.ppermute(moving[way], AXES, rings[way]) for way in range(2)])

    def link_flow():
        gathered = parent_factor[None]
        for bit in link_bits:
            arrived = swap(gathered, "col", col_count, 1 << bit)
            dims = (2 * gathered.shape[0],) + parent_factor.shape
            if bit:
                if bit > 1:
                    yield WAIT
                (gathered,) = yield (stack_step, [gathered, arrived], [shape(*dims)])
            else:
                (gathered,) = heavy(
                    functools.partial(step_kernel, [(stack_step, 2, 1)]),
                    [shape(*dims)],
                    [info, gathered, arrived],
                    smem=1,
                )
        held["links"] = heavy(
            functools.partial(link_kernel, children, 1.0 / row_count, link_order),
            [shape(children, width, width, dtype=BF16)] * 2
            + [shape(children, width, group, dtype=BF16)] * 2
            + [shape(children, diag_width, width), shape(children, width, half)],
            [info, gathered, diag_inverse, held["other diag"], held["chooser"], *held["own"][:2]],
            smem=1, vmem=20,
            scratch=[
                pltpu.VMEM((children, width, width), F32),
                pltpu.VMEM((2 * diag_width, width), F32),
                pltpu.VMEM((2 * diag_width, width), F32),
            ],
        )

    def prepare_flow():
        other_region = swap(region_inverse, "col", col_count, 1)
        held["other diag"] = swap(diag_inverse[:1], "col", col_count, 1)
        (held["chooser"],) = heavy(
            functools.partial(chooser_kernel, row_count, col_count),
            [shape(width, width, dtype=BF16)],
            [info],
            smem=1,
        )
        held["own"] = heavy(
            own_kernel,
            [shape(members, group, width, dtype=BF16)] * 2
            + [shape(members, width, group, dtype=BF16)] * 2,
            [info, listed, factor_cols, held["chooser"]],
            smem=2, hbm=1,
            scratch=[
                pltpu.VMEM((members, group, width), F32), pltpu.SemaphoreType.DMA((members,))
            ],
        )
        yield WAIT
        held["region"] = heavy(
            functools.partial(region_kernel, order),
            [shape(rows_here, 2 * cols_here, dtype=BF16)] * 2,
            [info, region_inverse, other_region],
            smem=1, hbm=2, vmem=12,
            scratch=[
                pltpu.VMEM((2, rows_here, cols_here), F32),
                pltpu.SemaphoreType.DMA((2, levels)),
            ],
        )
        for member in range(1, members):
            yield WAIT
            held["turned", member] = heavy(
                functools.partial(factor_kernel, order, member),
                [shape(width, rows_here, dtype=BF16)] * 2,
                [info, listed, factor_cols, held["chooser"]],
                smem=2, hbm=1, vmem=20,
                scratch=[
                    pltpu.VMEM((rows_here, width), F32), pltpu.SemaphoreType.DMA((levels,))
                ],
            )

    def unit_flow(member):
        chunk = (member + 1) * cuts - 1
        while len(received) < chunk + row_count - 1:
            yield WAIT
        final = member == members - 1
        if not final:
            yield WAIT
        candidates = []
        for at in range(member * cuts, (member + 1) * cuts):
            for way in range(2):
                candidates.append(moved[at][way])
                candidates += [received[at + hop][way] for hop in range(row_count - 1)]
        size = rows_here // 2
        keep, send = heavy(
            functools.partial(unit_kernel, row_count, ratio, cuts, member),
            [shape(size, half)] * 2,
            [info, listed, *held["region"], *candidates],
            smem=2, vmem=16,
        )
        first = (keep, send)
        for bit in range(1, col_bits):
            arrived = swap(send, "col", col_count, 1 << bit)
            if bit == 1:
                if final:
                    yield WAIT
                if member:
                    held["gram", member] = heavy(
                        unit_gram_kernel,
                        [shape(width, half)],
                        [*held["turned", member], *first],
                        vmem=16,
                    )[0]
            if bit + 1 < col_bits:
                size //= 2
                keep, send = yield (halve_step, [keep, arrived], [shape(size, half)] * 2)
        if member == 0:
            held["last", 0] = [keep, arrived]
            return
        if final:
            yield WAIT
        mine, theirs = yield (part_step, [keep, arrived], [shape(size // 2, half)] * 2)
        held["sum", member] = [mine, swap(theirs, "col", col_count, 1)]

    def total_flow(name, pieces, direct):
        count, size, _ = pieces[0].shape
        inputs = [pieces[0]] + [swap(pieces[d], "row", row_count, d) for d in range(1, row_count)]
        if direct:
            size //= levels
            pieces = yield (halve_step, inputs, [shape(count, size, half)] * levels)
            inputs = [pieces[0]]
            for at in range(1, levels):
                inputs.append(swap(pieces[at], "col", col_count, order[at] << 1))
        else:
            for bit in range(1, col_bits):
                size //= 2
                keep, send = yield (halve_step, inputs, [shape(count, size, half)] * 2)
                inputs = [keep, swap(send, "col", col_count, 1 << bit)]
        size //= 2
        keep, send = yield (halve_step, inputs, [shape(count, size, half)] * 2)
        held[name] = [keep, swap(send, "col", col_count, 1)]

    def gather_flow():
        while "parent totals" not in held or "child totals" not in held:
            yield WAIT
        pairs = held["parent totals"] + held["child totals"]
        (piece,) = yield (join_step, pairs, [shape(members + children, part, width)])
        held["totals"] = [piece] + [swap(piece, "row", row_count, d) for d in range(1, row_count)]

    def parent_flow():
        names = [("last", 0), "links"]
        while any(name not in held for name in names):
            yield WAIT
        (mine,) = heavy(
            functools.partial(step_kernel, [(halve_step, 2, 1)]),
            [shape(group, half)],
            [info, *held["last", 0]],
            smem=1,
        )
        other = swap(mine, "col", col_count, 1)
        col, *rest = heavy(
            functools.partial(parent_kernel, children, rows_here),
            [shape(group // 2, width)]
            + [shape(group, width, dtype=BF16)] * 2
            + [shape(members, width // row_count, half)] * row_count,
            [info, listed, held["chooser"], *held["own"], *held["links"][:2], mine, other],
            smem=2, vmem=20,
            scratch=[pltpu.VMEM((group, width), F32)],
        )
        held["parent"] = (col, rest[:2])
        yield WAIT
        yield from total_flow("parent totals", rest[2:], False)

    def child_flow():
        names = [("gram", 1 + c) for c in range(children)]
        while any(name not in held for name in names + ["parent"]):
            yield WAIT
        *pieces, held["lifted"] = heavy(
            functools.partial(child_kernel, children),
            [shape(children, width // row_count, half)] * row_count
            + [shape(children, group // 2, width)],
            [info, held["chooser"], *held["own"], *held["parent"][1], *held["links"][:4]]
            + [held["links"][5]]
            + [held[name] for name in names],
            smem=1, vmem=20,
            scratch=[pltpu.VMEM((group, width), F32)],
        )
        yield WAIT
        yield from total_flow("child totals", pieces, True)

    def column_flow():
        names = [("sum", 1 + c) for c in range(children)]
        while any(name not in held for name in names + ["parent"]):
            yield WAIT
        while "totals" not in held:
            yield WAIT
        col, turned = held["parent"][0], held["lifted"]
        held["columns"] = heavy(
            functools.partial(column_kernel, children, rows_here),
            [shape(members, group // 2, width)],
            [info, listed, col, turned] + [value for name in names for value in held[name]],
            smem=2,
        )[0]

    flows = [ring_flow()] + [unit_flow(member) for member in range(children)]
    flows += [link_flow(), prepare_flow(), parent_flow()]
    flows += [unit_flow(children), child_flow(), gather_flow(), column_flow()]
    waiting = [(flow, None) for flow in flows]
    while waiting:
        tasks = [wish for _, wish in waiting if wish not in (None, WAIT)]
        results = iter(())
        if tasks:
            outs = [out for _, _, shapes in tasks for out in shapes]
            args = [value for _, values, _ in tasks for value in values]
            sizes = [(body, len(values), len(shapes)) for body, values, shapes in tasks]
            results = iter(
                heavy(functools.partial(step_kernel, sizes), outs, [info, *args], smem=1)
            )
        answered = []
        for flow, wish in waiting:
            answer = None
            if wish not in (None, WAIT):
                answer = [next(results) for _ in wish[2]]
            answered.append((flow, answer))
        waiting = []
        for flow, answer in answered:
            try:
                waiting.append((flow, flow.send(answer)))
            except StopIteration:
                pass

    diags, uppers = heavy(
        functools.partial(finish_kernel, row_count),
        [shape(members, diag_width, width), shape(children, diag_width, width)],
        [info, diag_inverse, held["links"][4]] + held["totals"],
        smem=1,
    )
    return held["columns"], diags, uppers


def solution(mesh):
    in_specs = (
        P("row", "col"),
        P(None, "row", None),
        P(None, "col", None),
        P(None, "col", None),
        P(),
    )
    out_specs = (P(None, ("row", "col"), None), P(None, "col", None), P(None, "col", None))
    return jax.shard_map(shards, mesh=mesh, in_specs=in_specs, out_specs=out_specs, check_vma=False)
```

```python
import functools

import jax
import jax.numpy as jnp
from jax import lax
from jax.experimental import pallas as pl
from jax.experimental.pallas import tpu as pltpu
from jax.sharding import PartitionSpec as P

AXES = ("row", "col")
F32 = jnp.float32
BF16 = jnp.bfloat16
NN = (((1,), (0,)), ((), ()))
NT = (((1,), (1,)), ((), ()))
MIB = 1024 * 1024
WAIT = ("wait",)


def split(value):
    high = value.astype(BF16)
    return high, (value - high.astype(F32)).astype(BF16)


def one_pass(left, right, dims=NN):
    return lax.dot_general(left, right, dims, preferred_element_type=F32)


def product(left, right):
    return one_pass(left[0], right[0]) + (
        one_pass(left[0], right[1]) + one_pass(left[1], right[0])
    )


def turn(chooser, pair):
    return [one_pass(chooser, half, NT).astype(BF16) for half in pair]


def pair_of(high_ref, low_ref, *index):
    return (high_ref[index], low_ref[index]) if index else (high_ref[...], low_ref[...])


def store_pair(high_ref, low_ref, pair, *index):
    index = index if index else ...
    high_ref[index], low_ref[index] = pair


def shape(*dims, dtype=F32):
    return jax.ShapeDtypeStruct(dims, dtype)


def gray(place):
    return place ^ (place >> 1)


def reversed_bits(count):
    order = [0]
    step = 1
    while step < count:
        order = [value + bit * step for value in order for bit in (0, 1)]
        step *= 2
    return order


def swap(value, axis, size, change):
    return lax.ppermute(value, axis, [(place, place ^ change) for place in range(size)])


def block(index, size):
    return pl.ds(pl.multiple_of(index * size, size), size)


def core_of(info_ref):
    return info_ref[1] & 1


def call(body, outs, args, smem=0, hbm=0, scratch=(), vmem=8, after=None):
    places = [pltpu.SMEM] * smem + [pltpu.HBM] * hbm
    places += [pltpu.VMEM] * (len(args) - len(places))
    count = len(args)
    args = list(args)
    inner = body
    if after is not None:
        args.append(after)
        places.append(pl.ANY)

        def inner(*refs):
            body(*refs[:count], *refs[count + 1 :])

    results = pl.pallas_call(
        inner,
        out_shape=outs,
        in_specs=[pl.BlockSpec(memory_space=place) for place in places],
        out_specs=[pl.BlockSpec(memory_space=pltpu.VMEM)] * len(outs),
        scratch_shapes=scratch,
        compiler_params=pltpu.CompilerParams(vmem_limit_bytes=vmem * MIB),
        cost_estimate=pl.CostEstimate(flops=1024, bytes_accessed=1024, transcendentals=0),
    )(*args)
    return list(results)


def cut_kernel(ratio, cuts, members, info_ref, factors_ref, *refs):
    *outs, sems = refs
    size, unit = outs[0].shape
    pair = (info_ref[1] % ratio) // 2
    copies = []
    for at, out_ref in enumerate(outs):
        member, cut, way = members[at // (2 * cuts)], at // 2 % cuts, at % 2
        source = factors_ref.at[
            member, block(2 * pair + way, size), block(core_of(info_ref) * cuts + cut, unit)
        ]
        copies.append(pltpu.make_async_copy(source, out_ref, sems.at[at]))
        copies[-1].start()
    for copy in copies:
        copy.wait()


def chooser_kernel(rows, columns, info_ref, out_ref):
    width = out_ref.shape[0]
    size = width // columns
    part = size // rows
    place = lax.broadcasted_iota(jnp.int32, out_ref.shape, 0)
    inner = place % part
    core = place // part % 2
    level = place // (2 * part) % (columns // 2)
    by_row = place // (2 * part * (columns // 2))
    turned = jnp.zeros_like(level)
    bits = (columns // 2).bit_length() - 1
    for bit in range(bits):
        turned = turned | (((level >> bit) & 1) << (bits - 1 - bit))
    column = (turned * 2 + core) ^ info_ref[1]
    wanted = column * size + (by_row ^ info_ref[0]) * part + inner
    hit = wanted == lax.broadcasted_iota(jnp.int32, out_ref.shape, 1)
    out_ref[...] = hit.astype(F32).astype(BF16)


def region_kernel(order, info_ref, own_ref, other_ref, high_ref, low_ref, held_ref, sems):
    groups = len(order)
    size = own_ref.shape[0] // groups
    width = own_ref.shape[1]
    column = info_ref[1] >> 1
    copies = []
    for g in range(groups):
        for side, source_ref in enumerate((own_ref, other_ref)):
            copies.append(
                pltpu.make_async_copy(
                    source_ref.at[block(order[g] ^ column, size), :],
                    held_ref.at[side, pl.ds(g * size, size), :],
                    sems.at[side, g],
                )
            )
            copies[-1].start()
    for g in range(groups):
        rows = slice(g * size, (g + 1) * size)
        for side in range(2):
            copies[2 * g + side].wait()
            columns = block(core_of(info_ref) ^ side, width)
            high, low = split(held_ref[side, rows, :])
            high_ref[rows, columns] = high
            low_ref[rows, columns] = low


def factor_kernel(
    order, member, info_ref, listed_ref, factors_ref, chooser_ref, high_ref, low_ref, held_ref, sems
):
    groups = len(order)
    _, rows_here, width = factors_ref.shape
    size = rows_here // groups
    column = info_ref[1] >> 1
    copies = []
    for g in range(groups):
        copies.append(
            pltpu.make_async_copy(
                factors_ref.at[member, block(order[g] ^ column, size), :],
                held_ref.at[pl.ds(g * size, size), :],
                sems.at[g],
            )
        )
        copies[-1].start()
    for g in range(groups):
        copies[g].wait()
        rows = slice(g * size, (g + 1) * size)
        first = info_ref[0] * rows_here + (order[g] ^ column) * size
        held_ref[rows, :] = held_ref[rows, :] * listed_ref[member, first // width].astype(F32)
    store_pair(high_ref, low_ref, turn(chooser_ref[...], split(held_ref[...])))


def own_weight(info_ref, listed_ref, member, size, rows_here, width):
    first = info_ref[0] * rows_here + (info_ref[1] >> 1) * size
    return listed_ref[member, first // width].astype(F32)


def own_kernel(
    info_ref, listed_ref, factors_ref, chooser_ref, high_ref, low_ref, thigh_ref, tlow_ref,
    held_ref, sems,
):
    members, rows, width = held_ref.shape
    copies = []
    for j in range(members):
        copies.append(
            pltpu.make_async_copy(
                factors_ref.at[j, block(info_ref[1] >> 1, rows), :], held_ref.at[j], sems.at[j]
            )
        )
        copies[-1].start()
    for j in range(members):
        copies[j].wait()
        weight = own_weight(info_ref, listed_ref, j, rows, factors_ref.shape[1], width)
        pair = split(held_ref[j] * weight)
        store_pair(high_ref, low_ref, pair, j)
        store_pair(thigh_ref, tlow_ref, turn(chooser_ref[...], pair), j)


def link_kernel(
    children, share, order, info_ref, gathered_ref, diag_ref, other_ref, chooser_ref,
    own_high_ref, own_low_ref, high_ref, low_ref, lift_high_ref, lift_low_ref, framed_ref,
    corner_ref, held_ref, rows_ref, frame_ref,
):
    groups, _, size, width = gathered_ref.shape
    half = corner_ref.shape[2]
    core = core_of(info_ref)
    chooser = chooser_ref[...]
    for g in range(groups):
        for c in range(children):
            held_ref[c, block(info_ref[1] ^ order[g], size), :] = gathered_ref[g, c]
    rows_ref[block(core, size), :] = diag_ref[0]
    rows_ref[block(1 - core, size), :] = other_ref[0]
    diag = split(rows_ref[...])
    for c in range(children):
        pair = split(held_ref[c])
        store_pair(high_ref, low_ref, pair, c)
        lifted = product(pair_of(own_high_ref, own_low_ref, 0), pair)
        store_pair(lift_high_ref, lift_low_ref, turn(chooser, split(lifted)), c)
        frame_ref[...] = product(diag, pair)
        framed_ref[c] = frame_ref[block(core, size), :]
        slices = split(held_ref[c, block(info_ref[1] >> 1, 2 * size), :])
        corner = product(turn(chooser, slices), split(frame_ref[:, block(core, half)]))
        corner_ref[c] = share * corner


def unit_kernel(count, ratio, cuts, member, info_ref, listed_ref, high_ref, low_ref, *refs):
    keep_ref, send_ref = refs[-2:]
    middle = keep_ref.shape[0]
    place = info_ref[0] ^ (info_ref[1] // ratio)
    shift = 1
    while shift < count:
        place = place ^ (place >> shift)
        shift *= 2
    places = (place, (count - place) % count)
    parts = []
    for cut in range(cuts):
        chosen = []
        for way in range(2):
            candidates = refs[(2 * cut + way) * count :][:count]
            value = candidates[0][...]
            for at in range(1, count):
                value = jnp.where(places[way] == at, candidates[at][...], value)
            owner = info_ref[1] - core_of(info_ref) + way
            weight = listed_ref[member, owner * value.shape[0] // (2 * cuts * value.shape[1])]
            chosen.append(value * weight.astype(F32))
        parts.append(jnp.concatenate(chosen))
    right = split(jnp.concatenate(parts, axis=1))
    send_ref[...] = product((high_ref[middle:], low_ref[middle:]), right)
    keep_ref[...] = product((high_ref[:middle], low_ref[:middle]), right)


def unit_gram_kernel(high_ref, low_ref, keep_ref, send_ref, out_ref):
    middle = keep_ref.shape[0]
    out_ref[...] = product(
        (high_ref[:, :middle], low_ref[:, :middle]), split(keep_ref[...])
    ) + product((high_ref[:, middle:], low_ref[:, middle:]), split(send_ref[...]))


def store_parts(refs, index, value):
    size = refs[0].shape[1]
    for at, ref in enumerate(refs):
        ref[index] = value[at * size : (at + 1) * size]


def parent_kernel(
    children, rows_here, info_ref, listed_ref, chooser_ref, own_high_ref, own_low_ref,
    own_thigh_ref, own_tlow_ref, link_high_ref, link_low_ref, mine_ref, other_ref,
    col_ref, high_ref, low_ref, *refs
):
    *outs, full_ref = refs
    chooser = chooser_ref[...]
    rows, half = mine_ref.shape
    core = core_of(info_ref)
    weight = own_weight(info_ref, listed_ref, 0, rows, rows_here, chooser.shape[0])
    mine = -mine_ref[...] * weight
    full_ref[:, block(core, half)] = mine
    full_ref[:, block(1 - core, half)] = -other_ref[...] * weight
    col_ref[...] = full_ref[block(core, rows // 2), :]
    pair = split(full_ref[...])
    store_pair(high_ref, low_ref, pair)
    turned_pair = turn(chooser, pair)
    parent = pair_of(own_thigh_ref, own_tlow_ref, 0)
    columns = block(core, half)
    store_parts(outs, 0, -product(parent, split(mine)))
    for c in range(children):
        link = (link_high_ref[c, :, columns], link_low_ref[c, :, columns])
        lifted = split(product(pair, link))
        own = (own_high_ref[c + 1, :, columns], own_low_ref[c + 1, :, columns])
        store_parts(outs, 1 + c, product(parent, lifted) - product(turned_pair, own))


def child_kernel(
    children, info_ref, chooser_ref, own_high_ref, own_low_ref, own_thigh_ref, own_tlow_ref,
    high_ref, low_ref, link_high_ref, link_low_ref, lift_high_ref, lift_low_ref, corner_ref, *refs
):
    *refs, full_ref = refs
    grams, outs, turned_ref = refs[:children], refs[children:-1], refs[-1]
    core = core_of(info_ref)
    columns = block(core, corner_ref.shape[2])
    pair = pair_of(high_ref, low_ref)
    for c in range(children):
        full_ref[...] = product(pair, pair_of(link_high_ref, link_low_ref, c))
        turned_ref[c] = full_ref[block(core, full_ref.shape[0] // 2), :]
        lifted = split(full_ref[:, columns])
        turned_pair = turn(chooser_ref[...], split(full_ref[...]))
        own = (own_high_ref[c + 1, :, columns], own_low_ref[c + 1, :, columns])
        total = corner_ref[c] + grams[c][...]
        total += product(pair_of(own_thigh_ref, own_tlow_ref, c + 1), lifted)
        total += product(turned_pair, own)
        total -= product(pair_of(lift_high_ref, lift_low_ref, c), lifted)
        store_parts(outs, c, total)


def column_kernel(children, rows_here, info_ref, listed_ref, col_ref, turned_ref, *refs):
    out_ref = refs[-1]
    rows, width = col_ref.shape
    half = width // 2
    core = core_of(info_ref)
    out_ref[0] = col_ref[...]
    for c in range(children):
        weight = own_weight(info_ref, listed_ref, c + 1, 2 * rows, rows_here, width)
        for side in range(2):
            columns = block(core ^ side, half)
            total = refs[2 * c + side][...] + turned_ref[c, :, columns]
            out_ref[c + 1, :, columns] = -total * weight


def finish_kernel(rows, info_ref, diag_ref, framed_ref, *refs):
    pieces = refs[:rows]
    diags_ref, uppers_ref = refs[rows:]
    part = pieces[0].shape[1]
    children = uppers_ref.shape[0]
    for row in range(rows):
        at = slice(row * part, (row + 1) * part)
        value = pieces[0][...]
        for change in range(1, rows):
            value = jnp.where(info_ref[0] ^ change == row, pieces[change][...], value)
        diags_ref[0, at] = diag_ref[0, at] + value[0]
        uppers_ref[:, at] = value[1 : 1 + children] - framed_ref[:, at]
        diags_ref[1:, at] = diag_ref[1:, at] + value[1 + children :]


def select_step(ratio, info_ref, ins, outs):
    source = info_ref[0] == info_ref[1] // ratio
    for way in range(2):
        outs[way][...] = jnp.where(source, ins[way][...], ins[2 + way][...])


def pass_step(info_ref, ins, outs):
    for way in range(2):
        outs[way][...] = ins[way][...]


def stack_step(info_ref, ins, outs):
    for at in range(ins[0].shape[0]):
        for side in range(2):
            outs[0][2 * at + side] = ins[side][at]


def halve_step(info_ref, ins, outs):
    size = outs[0].shape[-2]
    for at, out in enumerate(outs):
        rows = pl.ds(at * size, size)
        index = (rows,) if len(out.shape) == 2 else (slice(None), rows)
        total = ins[0][index]
        for other in ins[1:]:
            total = total + other[index]
        out[...] = total


def part_step(info_ref, ins, outs):
    size = outs[0].shape[0]
    for side, out in enumerate(outs):
        rows = block(core_of(info_ref) ^ side, size)
        total = ins[0][rows, :]
        for other in ins[1:]:
            total = total + other[rows, :]
        out[...] = total


def join_step(info_ref, ins, outs):
    first = 0
    for at in range(0, len(ins), 2):
        count, _, half = ins[at].shape
        for side in range(2):
            columns = block(core_of(info_ref) ^ side, half)
            outs[0][first : first + count, :, columns] = ins[at + side][...]
        first += count


def step_kernel(tasks, info_ref, *refs):
    start = 0
    end = sum(ins for _, ins, _ in tasks)
    for body, ins, outs in tasks:
        body(info_ref, refs[start : start + ins], refs[end : end + outs])
        start += ins
        end += outs


def shards(region_inverse, factor_cols, parent_factor, diag_inverse, listed):
    row_count = lax.axis_size("row")
    col_count = lax.axis_size("col")
    col_bits = col_count.bit_length() - 1
    rows_here, cols_here = region_inverse.shape
    members, _, width = factor_cols.shape
    children = members - 1
    levels = col_count // 2
    group = rows_here // levels
    ratio = col_count // row_count
    diag_width = width // col_count
    part = diag_width // row_count
    half = width // 2
    cuts = 1
    unit = half // cuts
    chunk_count = members * cuts
    order = reversed_bits(levels)
    stages = chunk_count + row_count - 2

    def ring(forward):
        pairs = []
        for col in range(col_count):
            start = col // ratio
            for place in range(row_count):
                at = (start ^ gray(place)) * col_count + col
                to = (start ^ gray((place + 1) % row_count)) * col_count + col
                pairs.append((at, to) if forward else (to, at))
        return pairs

    rings = (ring(True), ring(False))
    link_bits = [*range(1, col_bits), 0]
    link_order = [0]
    for bit in link_bits:
        link_order = [value ^ (side << bit) for value in link_order for side in range(2)]
    info = jnp.stack([lax.axis_index("row"), lax.axis_index("col")]).astype(jnp.int32)

    def cut(chosen, run):
        count = len(chosen) * cuts * 2
        flat = run(
            functools.partial(cut_kernel, ratio, cuts, chosen),
            [shape(cols_here, unit)] * count,
            [info, factor_cols],
            smem=1, hbm=1, vmem=48,
            scratch=[pltpu.SemaphoreType.DMA((count,))],
        )
        return [flat[at : at + 2] for at in range(0, count, 2)]

    chunks = cut((0,), call)

    last = [chunks[0][0]]
    held = {}
    moved = []
    received = []

    def heavy(body, outs, args, **options):
        results = call(body, outs, args, after=last[0], **options)
        last[0] = results[0]
        return results

    chunks.extend(cut(tuple(range(1, members)), heavy))

    def ring_flow():
        shapes = [shape(cols_here, unit)] * 2
        for stage in range(stages):
            if stage == 0:
                moving = chunks[0]
            elif stage < chunk_count:
                step = functools.partial(select_step, ratio)
                moving = yield (step, chunks[stage] + received[-1], shapes)
            else:
                moving = yield (pass_step, received[-1], shapes)
            moved.append(moving)
            received.append([lax.ppermute(moving[way], AXES, rings[way]) for way in range(2)])

    def link_flow():
        gathered = parent_factor[None]
        for bit in link_bits:
            arrived = swap(gathered, "col", col_count, 1 << bit)
            dims = (2 * gathered.shape[0],) + parent_factor.shape
            if bit:
                if bit > 1:
                    yield WAIT
                (gathered,) = yield (stack_step, [gathered, arrived], [shape(*dims)])
            else:
                (gathered,) = heavy(
                    functools.partial(step_kernel, [(stack_step, 2, 1)]),
                    [shape(*dims)],
                    [info, gathered, arrived],
                    smem=1,
                )
        held["links"] = heavy(
            functools.partial(link_kernel, children, 1.0 / row_count, link_order),
            [shape(children, width, width, dtype=BF16)] * 2
            + [shape(children, width, group, dtype=BF16)] * 2
            + [shape(children, diag_width, width), shape(children, width, half)],
            [info, gathered, diag_inverse, held["other diag"], held["chooser"], *held["own"][:2]],
            smem=1, vmem=20,
            scratch=[
                pltpu.VMEM((children, width, width), F32),
                pltpu.VMEM((2 * diag_width, width), F32),
                pltpu.VMEM((2 * diag_width, width), F32),
            ],
        )

    def prepare_flow():
        other_region = swap(region_inverse, "col", col_count, 1)
        held["other diag"] = swap(diag_inverse[:1], "col", col_count, 1)
        (held["chooser"],) = heavy(
            functools.partial(chooser_kernel, row_count, col_count),
            [shape(width, width, dtype=BF16)],
            [info],
            smem=1,
        )
        held["own"] = heavy(
            own_kernel,
            [shape(members, group, width, dtype=BF16)] * 2
            + [shape(members, width, group, dtype=BF16)] * 2,
            [info, listed, factor_cols, held["chooser"]],
            smem=2, hbm=1,
            scratch=[
                pltpu.VMEM((members, group, width), F32), pltpu.SemaphoreType.DMA((members,))
            ],
        )
        yield WAIT
        held["region"] = heavy(
            functools.partial(region_kernel, order),
            [shape(rows_here, 2 * cols_here, dtype=BF16)] * 2,
            [info, region_inverse, other_region],
            smem=1, hbm=2, vmem=12,
            scratch=[
                pltpu.VMEM((2, rows_here, cols_here), F32),
                pltpu.SemaphoreType.DMA((2, levels)),
            ],
        )
        for member in range(1, members):
            yield WAIT
            held["turned", member] = heavy(
                functools.partial(factor_kernel, order, member),
                [shape(width, rows_here, dtype=BF16)] * 2,
                [info, listed, factor_cols, held["chooser"]],
                smem=2, hbm=1, vmem=20,
                scratch=[
                    pltpu.VMEM((rows_here, width), F32), pltpu.SemaphoreType.DMA((levels,))
                ],
            )

    def unit_flow(member):
        chunk = (member + 1) * cuts - 1
        while len(received) < chunk + row_count - 1:
            yield WAIT
        final = member == members - 1
        if not final:
            yield WAIT
        candidates = []
        for at in range(member * cuts, (member + 1) * cuts):
            for way in range(2):
                candidates.append(moved[at][way])
                candidates += [received[at + hop][way] for hop in range(row_count - 1)]
        size = rows_here // 2
        keep, send = heavy(
            functools.partial(unit_kernel, row_count, ratio, cuts, member),
            [shape(size, half)] * 2,
            [info, listed, *held["region"], *candidates],
            smem=2, vmem=16,
        )
        first = (keep, send)
        for bit in range(1, col_bits):
            arrived = swap(send, "col", col_count, 1 << bit)
            if bit == 1:
                if final:
                    yield WAIT
                if member:
                    held["gram", member] = heavy(
                        unit_gram_kernel,
                        [shape(width, half)],
                        [*held["turned", member], *first],
                        vmem=16,
                    )[0]
            if bit + 1 < col_bits:
                size //= 2
                keep, send = yield (halve_step, [keep, arrived], [shape(size, half)] * 2)
        if member == 0:
            held["last", 0] = [keep, arrived]
            return
        yield WAIT
        if final:
            mine, theirs = yield (part_step, [keep, arrived], [shape(size // 2, half)] * 2)
        else:
            mine, theirs = heavy(
                functools.partial(step_kernel, [(part_step, 2, 2)]),
                [shape(size // 2, half)] * 2,
                [info, keep, arrived],
                smem=1,
            )
        held["sum", member] = [mine, swap(theirs, "col", col_count, 1)]

    def total_flow(name, pieces, direct):
        count, size, _ = pieces[0].shape
        inputs = [pieces[0]] + [swap(pieces[d], "row", row_count, d) for d in range(1, row_count)]
        if direct:
            size //= levels
            pieces = yield (halve_step, inputs, [shape(count, size, half)] * levels)
            inputs = [pieces[0]]
            for at in range(1, levels):
                inputs.append(swap(pieces[at], "col", col_count, order[at] << 1))
        else:
            for bit in range(1, col_bits):
                size //= 2
                keep, send = yield (halve_step, inputs, [shape(count, size, half)] * 2)
                inputs = [keep, swap(send, "col", col_count, 1 << bit)]
        size //= 2
        keep, send = yield (halve_step, inputs, [shape(count, size, half)] * 2)
        held[name] = [keep, swap(send, "col", col_count, 1)]

    def gather_flow():
        while "parent totals" not in held or "child totals" not in held:
            yield WAIT
        pairs = held["parent totals"] + held["child totals"]
        (piece,) = yield (join_step, pairs, [shape(members + children, part, width)])
        held["totals"] = [piece] + [swap(piece, "row", row_count, d) for d in range(1, row_count)]

    def parent_flow():
        names = [("last", 0), "links"]
        while any(name not in held for name in names):
            yield WAIT
        (mine,) = heavy(
            functools.partial(step_kernel, [(halve_step, 2, 1)]),
            [shape(group, half)],
            [info, *held["last", 0]],
            smem=1,
        )
        other = swap(mine, "col", col_count, 1)
        col, *rest = heavy(
            functools.partial(parent_kernel, children, rows_here),
            [shape(group // 2, width)]
            + [shape(group, width, dtype=BF16)] * 2
            + [shape(members, width // row_count, half)] * row_count,
            [info, listed, held["chooser"], *held["own"], *held["links"][:2], mine, other],
            smem=2, vmem=20,
            scratch=[pltpu.VMEM((group, width), F32)],
        )
        held["parent"] = (col, rest[:2])
        yield WAIT
        yield from total_flow("parent totals", rest[2:], False)

    def child_flow():
        names = [("gram", 1 + c) for c in range(children)]
        while any(name not in held for name in names + ["parent"]):
            yield WAIT
        *pieces, held["lifted"] = heavy(
            functools.partial(child_kernel, children),
            [shape(children, width // row_count, half)] * row_count
            + [shape(children, group // 2, width)],
            [info, held["chooser"], *held["own"], *held["parent"][1], *held["links"][:4]]
            + [held["links"][5]]
            + [held[name] for name in names],
            smem=1, vmem=20,
            scratch=[pltpu.VMEM((group, width), F32)],
        )
        yield WAIT
        yield from total_flow("child totals", pieces, True)

    def column_flow():
        names = [("sum", 1 + c) for c in range(children)]
        while any(name not in held for name in names + ["parent"]):
            yield WAIT
        while "totals" not in held:
            yield WAIT
        col, turned = held["parent"][0], held["lifted"]
        held["columns"] = heavy(
            functools.partial(column_kernel, children, rows_here),
            [shape(members, group // 2, width)],
            [info, listed, col, turned] + [value for name in names for value in held[name]],
            smem=2,
        )[0]

    flows = [ring_flow()] + [unit_flow(member) for member in range(children)]
    flows += [link_flow(), prepare_flow(), parent_flow()]
    flows += [unit_flow(children), child_flow(), gather_flow(), column_flow()]
    waiting = [(flow, None) for flow in flows]
    while waiting:
        tasks = [wish for _, wish in waiting if wish not in (None, WAIT)]
        results = iter(())
        if tasks:
            outs = [out for _, _, shapes in tasks for out in shapes]
            args = [value for _, values, _ in tasks for value in values]
            sizes = [(body, len(values), len(shapes)) for body, values, shapes in tasks]
            results = iter(
                heavy(functools.partial(step_kernel, sizes), outs, [info, *args], smem=1)
            )
        answered = []
        for flow, wish in waiting:
            answer = None
            if wish not in (None, WAIT):
                answer = [next(results) for _ in wish[2]]
            answered.append((flow, answer))
        waiting = []
        for flow, answer in answered:
            try:
                waiting.append((flow, flow.send(answer)))
            except StopIteration:
                pass

    diags, uppers = call(
        functools.partial(finish_kernel, row_count),
        [shape(members, diag_width, width), shape(children, diag_width, width)],
        [info, diag_inverse, held["links"][4]] + held["totals"],
        smem=1,
    )
    return held["columns"], diags, uppers


def solution(mesh):
    in_specs = (
        P("row", "col"),
        P(None, "row", None),
        P(None, "col", None),
        P(None, "col", None),
        P(),
    )
    out_specs = (P(None, ("row", "col"), None), P(None, "col", None), P(None, "col", None))
    return jax.shard_map(shards, mesh=mesh, in_specs=in_specs, out_specs=out_specs, check_vma=False)
```

```python
import functools

import jax
import jax.numpy as jnp
from jax import lax
from jax.experimental import pallas as pl
from jax.experimental.pallas import tpu as pltpu
from jax.sharding import PartitionSpec as P

AXES = ("row", "col")
F32 = jnp.float32
BF16 = jnp.bfloat16
NN = (((1,), (0,)), ((), ()))
NT = (((1,), (1,)), ((), ()))
MIB = 1024 * 1024
WAIT = ("wait",)


def split(value):
    high = value.astype(BF16)
    return high, (value - high.astype(F32)).astype(BF16)


def one_pass(left, right, dims=NN):
    return lax.dot_general(left, right, dims, preferred_element_type=F32)


def product(left, right):
    return one_pass(left[0], right[0]) + (
        one_pass(left[0], right[1]) + one_pass(left[1], right[0])
    )


def turn(chooser, pair):
    return [one_pass(chooser, half, NT).astype(BF16) for half in pair]


def pair_of(high_ref, low_ref, *index):
    return (high_ref[index], low_ref[index]) if index else (high_ref[...], low_ref[...])


def store_pair(high_ref, low_ref, pair, *index):
    index = index if index else ...
    high_ref[index], low_ref[index] = pair


def shape(*dims, dtype=F32):
    return jax.ShapeDtypeStruct(dims, dtype)


def gray(place):
    return place ^ (place >> 1)


def reversed_bits(count):
    order = [0]
    step = 1
    while step < count:
        order = [value + bit * step for value in order for bit in (0, 1)]
        step *= 2
    return order


def swap(value, axis, size, change):
    return lax.ppermute(value, axis, [(place, place ^ change) for place in range(size)])


def block(index, size):
    return pl.ds(pl.multiple_of(index * size, size), size)


def core_of(info_ref):
    return info_ref[1] & 1


def call(body, outs, args, smem=0, hbm=0, scratch=(), vmem=8, after=None):
    places = [pltpu.SMEM] * smem + [pltpu.HBM] * hbm
    places += [pltpu.VMEM] * (len(args) - len(places))
    count = len(args)
    args = list(args)
    inner = body
    if after is not None:
        args.append(after)
        places.append(pl.ANY)

        def inner(*refs):
            body(*refs[:count], *refs[count + 1 :])

    results = pl.pallas_call(
        inner,
        out_shape=outs,
        in_specs=[pl.BlockSpec(memory_space=place) for place in places],
        out_specs=[pl.BlockSpec(memory_space=pltpu.VMEM)] * len(outs),
        scratch_shapes=scratch,
        compiler_params=pltpu.CompilerParams(vmem_limit_bytes=vmem * MIB),
        cost_estimate=pl.CostEstimate(flops=1024, bytes_accessed=1024, transcendentals=0),
    )(*args)
    return list(results)


def cut_kernel(ratio, cuts, members, info_ref, factors_ref, *refs):
    *outs, sems = refs
    size, unit = outs[0].shape
    pair = (info_ref[1] % ratio) // 2
    copies = []
    for at, out_ref in enumerate(outs):
        member, cut, way = members[at // (2 * cuts)], at // 2 % cuts, at % 2
        source = factors_ref.at[
            member, block(2 * pair + way, size), block(core_of(info_ref) * cuts + cut, unit)
        ]
        copies.append(pltpu.make_async_copy(source, out_ref, sems.at[at]))
        copies[-1].start()
    for copy in copies:
        copy.wait()


def chooser_kernel(rows, columns, info_ref, out_ref):
    width = out_ref.shape[0]
    size = width // columns
    part = size // rows
    place = lax.broadcasted_iota(jnp.int32, out_ref.shape, 0)
    inner = place % part
    core = place // part % 2
    level = place // (2 * part) % (columns // 2)
    by_row = place // (2 * part * (columns // 2))
    turned = jnp.zeros_like(level)
    bits = (columns // 2).bit_length() - 1
    for bit in range(bits):
        turned = turned | (((level >> bit) & 1) << (bits - 1 - bit))
    column = (turned * 2 + core) ^ info_ref[1]
    wanted = column * size + (by_row ^ info_ref[0]) * part + inner
    hit = wanted == lax.broadcasted_iota(jnp.int32, out_ref.shape, 1)
    out_ref[...] = hit.astype(F32).astype(BF16)


def region_kernel(order, info_ref, own_ref, other_ref, high_ref, low_ref, held_ref, sems):
    groups = len(order)
    size = own_ref.shape[0] // groups
    width = own_ref.shape[1]
    column = info_ref[1] >> 1
    copies = []
    for g in range(groups):
        for side, source_ref in enumerate((own_ref, other_ref)):
            copies.append(
                pltpu.make_async_copy(
                    source_ref.at[block(order[g] ^ column, size), :],
                    held_ref.at[side, pl.ds(g * size, size), :],
                    sems.at[side, g],
                )
            )
            copies[-1].start()
    for g in range(groups):
        rows = slice(g * size, (g + 1) * size)
        for side in range(2):
            copies[2 * g + side].wait()
            columns = block(core_of(info_ref) ^ side, width)
            high, low = split(held_ref[side, rows, :])
            high_ref[rows, columns] = high
            low_ref[rows, columns] = low


def factor_kernel(
    order, member, info_ref, listed_ref, factors_ref, chooser_ref, high_ref, low_ref, held_ref, sems
):
    groups = len(order)
    _, rows_here, width = factors_ref.shape
    size = rows_here // groups
    column = info_ref[1] >> 1
    copies = []
    for g in range(groups):
        copies.append(
            pltpu.make_async_copy(
                factors_ref.at[member, block(order[g] ^ column, size), :],
                held_ref.at[pl.ds(g * size, size), :],
                sems.at[g],
            )
        )
        copies[-1].start()
    for g in range(groups):
        copies[g].wait()
        rows = slice(g * size, (g + 1) * size)
        first = info_ref[0] * rows_here + (order[g] ^ column) * size
        held_ref[rows, :] = held_ref[rows, :] * listed_ref[member, first // width].astype(F32)
    store_pair(high_ref, low_ref, turn(chooser_ref[...], split(held_ref[...])))


def own_weight(info_ref, listed_ref, member, size, rows_here, width):
    first = info_ref[0] * rows_here + (info_ref[1] >> 1) * size
    return listed_ref[member, first // width].astype(F32)


def own_kernel(
    info_ref, listed_ref, factors_ref, chooser_ref, high_ref, low_ref, thigh_ref, tlow_ref,
    held_ref, sems,
):
    members, rows, width = held_ref.shape
    copies = []
    for j in range(members):
        copies.append(
            pltpu.make_async_copy(
                factors_ref.at[j, block(info_ref[1] >> 1, rows), :], held_ref.at[j], sems.at[j]
            )
        )
        copies[-1].start()
    for j in range(members):
        copies[j].wait()
        weight = own_weight(info_ref, listed_ref, j, rows, factors_ref.shape[1], width)
        pair = split(held_ref[j] * weight)
        store_pair(high_ref, low_ref, pair, j)
        store_pair(thigh_ref, tlow_ref, turn(chooser_ref[...], pair), j)


def link_kernel(
    children, share, order, info_ref, gathered_ref, diag_ref, other_ref, chooser_ref,
    own_high_ref, own_low_ref, high_ref, low_ref, lift_high_ref, lift_low_ref, framed_ref,
    corner_ref, held_ref, rows_ref, frame_ref,
):
    groups, _, size, width = gathered_ref.shape
    half = corner_ref.shape[2]
    core = core_of(info_ref)
    chooser = chooser_ref[...]
    for g in range(groups):
        for c in range(children):
            held_ref[c, block(info_ref[1] ^ order[g], size), :] = gathered_ref[g, c]
    rows_ref[block(core, size), :] = diag_ref[0]
    rows_ref[block(1 - core, size), :] = other_ref[0]
    diag = split(rows_ref[...])
    for c in range(children):
        pair = split(held_ref[c])
        store_pair(high_ref, low_ref, pair, c)
        lifted = product(pair_of(own_high_ref, own_low_ref, 0), pair)
        store_pair(lift_high_ref, lift_low_ref, turn(chooser, split(lifted)), c)
        frame_ref[...] = product(diag, pair)
        framed_ref[c] = frame_ref[block(core, size), :]
        slices = split(held_ref[c, block(info_ref[1] >> 1, 2 * size), :])
        corner = product(turn(chooser, slices), split(frame_ref[:, block(core, half)]))
        corner_ref[c] = share * corner


def unit_kernel(count, ratio, cuts, member, info_ref, listed_ref, high_ref, low_ref, *refs):
    keep_ref, send_ref = refs[-2:]
    middle = keep_ref.shape[0]
    place = info_ref[0] ^ (info_ref[1] // ratio)
    shift = 1
    while shift < count:
        place = place ^ (place >> shift)
        shift *= 2
    places = (place, (count - place) % count)
    parts = []
    for cut in range(cuts):
        chosen = []
        for way in range(2):
            candidates = refs[(2 * cut + way) * count :][:count]
            value = candidates[0][...]
            for at in range(1, count):
                value = jnp.where(places[way] == at, candidates[at][...], value)
            owner = info_ref[1] - core_of(info_ref) + way
            weight = listed_ref[member, owner * value.shape[0] // (2 * cuts * value.shape[1])]
            chosen.append(value * weight.astype(F32))
        parts.append(jnp.concatenate(chosen))
    right = split(jnp.concatenate(parts, axis=1))
    send_ref[...] = product((high_ref[middle:], low_ref[middle:]), right)
    keep_ref[...] = product((high_ref[:middle], low_ref[:middle]), right)


def unit_gram_kernel(high_ref, low_ref, keep_ref, send_ref, out_ref):
    middle = keep_ref.shape[0]
    out_ref[...] = product(
        (high_ref[:, :middle], low_ref[:, :middle]), split(keep_ref[...])
    ) + product((high_ref[:, middle:], low_ref[:, middle:]), split(send_ref[...]))


def store_parts(refs, index, value):
    size = refs[0].shape[1]
    for at, ref in enumerate(refs):
        ref[index] = value[at * size : (at + 1) * size]


def parent_kernel(
    children, rows_here, info_ref, listed_ref, chooser_ref, own_high_ref, own_low_ref,
    own_thigh_ref, own_tlow_ref, link_high_ref, link_low_ref, mine_ref, other_ref,
    col_ref, high_ref, low_ref, *refs
):
    *outs, full_ref = refs
    chooser = chooser_ref[...]
    rows, half = mine_ref.shape
    core = core_of(info_ref)
    weight = own_weight(info_ref, listed_ref, 0, rows, rows_here, chooser.shape[0])
    mine = -mine_ref[...] * weight
    full_ref[:, block(core, half)] = mine
    full_ref[:, block(1 - core, half)] = -other_ref[...] * weight
    col_ref[...] = full_ref[block(core, rows // 2), :]
    pair = split(full_ref[...])
    store_pair(high_ref, low_ref, pair)
    turned_pair = turn(chooser, pair)
    parent = pair_of(own_thigh_ref, own_tlow_ref, 0)
    columns = block(core, half)
    store_parts(outs, 0, -product(parent, split(mine)))
    for c in range(children):
        link = (link_high_ref[c, :, columns], link_low_ref[c, :, columns])
        lifted = split(product(pair, link))
        own = (own_high_ref[c + 1, :, columns], own_low_ref[c + 1, :, columns])
        store_parts(outs, 1 + c, product(parent, lifted) - product(turned_pair, own))


def child_kernel(
    children, info_ref, chooser_ref, own_high_ref, own_low_ref, own_thigh_ref, own_tlow_ref,
    high_ref, low_ref, link_high_ref, link_low_ref, lift_high_ref, lift_low_ref, corner_ref, *refs
):
    *refs, full_ref = refs
    grams, outs, turned_ref = refs[:children], refs[children:-1], refs[-1]
    core = core_of(info_ref)
    columns = block(core, corner_ref.shape[2])
    pair = pair_of(high_ref, low_ref)
    for c in range(children):
        full_ref[...] = product(pair, pair_of(link_high_ref, link_low_ref, c))
        turned_ref[c] = full_ref[block(core, full_ref.shape[0] // 2), :]
        lifted = split(full_ref[:, columns])
        turned_pair = turn(chooser_ref[...], split(full_ref[...]))
        own = (own_high_ref[c + 1, :, columns], own_low_ref[c + 1, :, columns])
        total = corner_ref[c] + grams[c][...]
        total += product(pair_of(own_thigh_ref, own_tlow_ref, c + 1), lifted)
        total += product(turned_pair, own)
        total -= product(pair_of(lift_high_ref, lift_low_ref, c), lifted)
        store_parts(outs, c, total)


def column_kernel(children, rows_here, info_ref, listed_ref, col_ref, turned_ref, *refs):
    out_ref = refs[-1]
    rows, width = col_ref.shape
    half = width // 2
    core = core_of(info_ref)
    out_ref[0] = col_ref[...]
    for c in range(children):
        weight = own_weight(info_ref, listed_ref, c + 1, 2 * rows, rows_here, width)
        for side in range(2):
            columns = block(core ^ side, half)
            total = refs[2 * c + side][...] + turned_ref[c, :, columns]
            out_ref[c + 1, :, columns] = -total * weight


def finish_kernel(rows, info_ref, diag_ref, framed_ref, *refs):
    pieces = refs[:rows]
    diags_ref, uppers_ref = refs[rows:]
    part = pieces[0].shape[1]
    children = uppers_ref.shape[0]
    for row in range(rows):
        at = slice(row * part, (row + 1) * part)
        value = pieces[0][...]
        for change in range(1, rows):
            value = jnp.where(info_ref[0] ^ change == row, pieces[change][...], value)
        diags_ref[0, at] = diag_ref[0, at] + value[0]
        uppers_ref[:, at] = value[1 : 1 + children] - framed_ref[:, at]
        diags_ref[1:, at] = diag_ref[1:, at] + value[1 + children :]


def select_step(ratio, info_ref, ins, outs):
    source = info_ref[0] == info_ref[1] // ratio
    for way in range(2):
        outs[way][...] = jnp.where(source, ins[way][...], ins[2 + way][...])


def pass_step(info_ref, ins, outs):
    for way in range(2):
        outs[way][...] = ins[way][...]


def stack_step(info_ref, ins, outs):
    for at in range(ins[0].shape[0]):
        for side in range(2):
            outs[0][2 * at + side] = ins[side][at]


def halve_step(info_ref, ins, outs):
    size = outs[0].shape[-2]
    for at, out in enumerate(outs):
        rows = pl.ds(at * size, size)
        index = (rows,) if len(out.shape) == 2 else (slice(None), rows)
        total = ins[0][index]
        for other in ins[1:]:
            total = total + other[index]
        out[...] = total


def part_step(info_ref, ins, outs):
    size = outs[0].shape[0]
    for side, out in enumerate(outs):
        rows = block(core_of(info_ref) ^ side, size)
        total = ins[0][rows, :]
        for other in ins[1:]:
            total = total + other[rows, :]
        out[...] = total


def join_step(info_ref, ins, outs):
    first = 0
    for at in range(0, len(ins), 2):
        count, _, half = ins[at].shape
        for side in range(2):
            columns = block(core_of(info_ref) ^ side, half)
            outs[0][first : first + count, :, columns] = ins[at + side][...]
        first += count


def step_kernel(tasks, info_ref, *refs):
    start = 0
    end = sum(ins for _, ins, _ in tasks)
    for body, ins, outs in tasks:
        body(info_ref, refs[start : start + ins], refs[end : end + outs])
        start += ins
        end += outs


def shards(region_inverse, factor_cols, parent_factor, diag_inverse, listed):
    row_count = lax.axis_size("row")
    col_count = lax.axis_size("col")
    col_bits = col_count.bit_length() - 1
    rows_here, cols_here = region_inverse.shape
    members, _, width = factor_cols.shape
    children = members - 1
    levels = col_count // 2
    group = rows_here // levels
    ratio = col_count // row_count
    diag_width = width // col_count
    part = diag_width // row_count
    half = width // 2
    cuts = 1
    unit = half // cuts
    chunk_count = members * cuts
    order = reversed_bits(levels)
    stages = chunk_count + row_count - 2

    def ring(forward):
        pairs = []
        for col in range(col_count):
            start = col // ratio
            for place in range(row_count):
                at = (start ^ gray(place)) * col_count + col
                to = (start ^ gray((place + 1) % row_count)) * col_count + col
                pairs.append((at, to) if forward else (to, at))
        return pairs

    rings = (ring(True), ring(False))
    link_bits = [*range(1, col_bits), 0]
    link_order = [0]
    for bit in link_bits:
        link_order = [value ^ (side << bit) for value in link_order for side in range(2)]
    info = jnp.stack([lax.axis_index("row"), lax.axis_index("col")]).astype(jnp.int32)

    def cut(chosen, run):
        count = len(chosen) * cuts * 2
        flat = run(
            functools.partial(cut_kernel, ratio, cuts, chosen),
            [shape(cols_here, unit)] * count,
            [info, factor_cols],
            smem=1, hbm=1, vmem=48,
            scratch=[pltpu.SemaphoreType.DMA((count,))],
        )
        return [flat[at : at + 2] for at in range(0, count, 2)]

    chunks = cut((0,), call)

    last = [chunks[0][0]]
    held = {}
    moved = []
    received = []

    def heavy(body, outs, args, **options):
        results = call(body, outs, args, after=last[0], **options)
        last[0] = results[0]
        return results

    chunks.extend(cut(tuple(range(1, members)), heavy))

    def ring_flow():
        shapes = [shape(cols_here, unit)] * 2
        for stage in range(stages):
            if stage == 0:
                moving = chunks[0]
            elif stage < chunk_count:
                step = functools.partial(select_step, ratio)
                moving = yield (step, chunks[stage] + received[-1], shapes)
            else:
                moving = yield (pass_step, received[-1], shapes)
            moved.append(moving)
            received.append([lax.ppermute(moving[way], AXES, rings[way]) for way in range(2)])

    def link_flow():
        gathered = parent_factor[None]
        for bit in link_bits:
            arrived = swap(gathered, "col", col_count, 1 << bit)
            dims = (2 * gathered.shape[0],) + parent_factor.shape
            if bit:
                if bit > 1:
                    yield WAIT
                (gathered,) = yield (stack_step, [gathered, arrived], [shape(*dims)])
            else:
                (gathered,) = heavy(
                    functools.partial(step_kernel, [(stack_step, 2, 1)]),
                    [shape(*dims)],
                    [info, gathered, arrived],
                    smem=1,
                )
        held["links"] = heavy(
            functools.partial(link_kernel, children, 1.0 / row_count, link_order),
            [shape(children, width, width, dtype=BF16)] * 2
            + [shape(children, width, group, dtype=BF16)] * 2
            + [shape(children, diag_width, width), shape(children, width, half)],
            [info, gathered, diag_inverse, held["other diag"], held["chooser"], *held["own"][:2]],
            smem=1, vmem=20,
            scratch=[
                pltpu.VMEM((children, width, width), F32),
                pltpu.VMEM((2 * diag_width, width), F32),
                pltpu.VMEM((2 * diag_width, width), F32),
            ],
        )

    def prepare_flow():
        other_region = swap(region_inverse, "col", col_count, 1)
        held["other diag"] = swap(diag_inverse[:1], "col", col_count, 1)
        (held["chooser"],) = heavy(
            functools.partial(chooser_kernel, row_count, col_count),
            [shape(width, width, dtype=BF16)],
            [info],
            smem=1,
        )
        held["own"] = heavy(
            own_kernel,
            [shape(members, group, width, dtype=BF16)] * 2
            + [shape(members, width, group, dtype=BF16)] * 2,
            [info, listed, factor_cols, held["chooser"]],
            smem=2, hbm=1,
            scratch=[
                pltpu.VMEM((members, group, width), F32), pltpu.SemaphoreType.DMA((members,))
            ],
        )
        yield WAIT
        held["region"] = heavy(
            functools.partial(region_kernel, order),
            [shape(rows_here, 2 * cols_here, dtype=BF16)] * 2,
            [info, region_inverse, other_region],
            smem=1, hbm=2, vmem=12,
            scratch=[
                pltpu.VMEM((2, rows_here, cols_here), F32),
                pltpu.SemaphoreType.DMA((2, levels)),
            ],
        )
        for member in range(1, members):
            yield WAIT
            held["turned", member] = heavy(
                functools.partial(factor_kernel, order, member),
                [shape(width, rows_here, dtype=BF16)] * 2,
                [info, listed, factor_cols, held["chooser"]],
                smem=2, hbm=1, vmem=20,
                scratch=[
                    pltpu.VMEM((rows_here, width), F32), pltpu.SemaphoreType.DMA((levels,))
                ],
            )

    def unit_flow(member):
        chunk = (member + 1) * cuts - 1
        while len(received) < chunk + row_count - 1:
            yield WAIT
        final = member == members - 1
        if not final:
            yield WAIT
        candidates = []
        for at in range(member * cuts, (member + 1) * cuts):
            for way in range(2):
                candidates.append(moved[at][way])
                candidates += [received[at + hop][way] for hop in range(row_count - 1)]
        size = rows_here // 2
        keep, send = heavy(
            functools.partial(unit_kernel, row_count, ratio, cuts, member),
            [shape(size, half)] * 2,
            [info, listed, *held["region"], *candidates],
            smem=2, vmem=16,
        )
        first = (keep, send)
        for bit in range(1, col_bits):
            arrived = swap(send, "col", col_count, 1 << bit)
            if bit == 1:
                if final:
                    yield WAIT
                if member:
                    held["gram", member] = heavy(
                        unit_gram_kernel,
                        [shape(width, half)],
                        [*held["turned", member], *first],
                        vmem=16,
                    )[0]
            if bit + 1 < col_bits:
                size //= 2
                keep, send = yield (halve_step, [keep, arrived], [shape(size, half)] * 2)
        if member == 0:
            held["last", 0] = [keep, arrived]
            return
        if final:
            yield WAIT
        mine, theirs = yield (part_step, [keep, arrived], [shape(size // 2, half)] * 2)
        held["sum", member] = [mine, swap(theirs, "col", col_count, 1)]

    def total_flow(name, pieces, direct):
        count, size, _ = pieces[0].shape
        inputs = [pieces[0]] + [swap(pieces[d], "row", row_count, d) for d in range(1, row_count)]
        if direct:
            size //= levels
            pieces = yield (halve_step, inputs, [shape(count, size, half)] * levels)
            inputs = [pieces[0]]
            for at in range(1, levels):
                inputs.append(swap(pieces[at], "col", col_count, order[at] << 1))
        else:
            for bit in range(1, col_bits):
                size //= 2
                keep, send = yield (halve_step, inputs, [shape(count, size, half)] * 2)
                inputs = [keep, swap(send, "col", col_count, 1 << bit)]
        size //= 2
        keep, send = yield (halve_step, inputs, [shape(count, size, half)] * 2)
        held[name] = [keep, swap(send, "col", col_count, 1)]

    def gather_flow():
        while "parent totals" not in held or "child totals" not in held:
            yield WAIT
        pairs = held["parent totals"] + held["child totals"]
        (piece,) = yield (join_step, pairs, [shape(members + children, part, width)])
        held["totals"] = [piece] + [swap(piece, "row", row_count, d) for d in range(1, row_count)]

    def parent_flow():
        names = [("last", 0), "links"]
        while any(name not in held for name in names):
            yield WAIT
        (mine,) = heavy(
            functools.partial(step_kernel, [(halve_step, 2, 1)]),
            [shape(group, half)],
            [info, *held["last", 0]],
            smem=1,
        )
        other = swap(mine, "col", col_count, 1)
        col, *rest = heavy(
            functools.partial(parent_kernel, children, rows_here),
            [shape(group // 2, width)]
            + [shape(group, width, dtype=BF16)] * 2
            + [shape(members, width // row_count, half)] * row_count,
            [info, listed, held["chooser"], *held["own"], *held["links"][:2], mine, other],
            smem=2, vmem=20,
            scratch=[pltpu.VMEM((group, width), F32)],
        )
        held["parent"] = (col, rest[:2])
        yield WAIT
        yield from total_flow("parent totals", rest[2:], False)

    def child_flow():
        names = [("gram", 1 + c) for c in range(children)]
        while any(name not in held for name in names + ["parent"]):
            yield WAIT
        *pieces, held["lifted"] = heavy(
            functools.partial(child_kernel, children),
            [shape(children, width // row_count, half)] * row_count
            + [shape(children, group // 2, width)],
            [info, held["chooser"], *held["own"], *held["parent"][1], *held["links"][:4]]
            + [held["links"][5]]
            + [held[name] for name in names],
            smem=1, vmem=20,
            scratch=[pltpu.VMEM((group, width), F32)],
        )
        yield WAIT
        yield from total_flow("child totals", pieces, True)

    def column_flow():
        names = [("sum", 1 + c) for c in range(children)]
        while any(name not in held for name in names + ["parent"]):
            yield WAIT
        while "totals" not in held:
            yield WAIT
        col, turned = held["parent"][0], held["lifted"]
        held["columns"] = heavy(
            functools.partial(column_kernel, children, rows_here),
            [shape(members, group // 2, width)],
            [info, listed, col, turned] + [value for name in names for value in held[name]],
            smem=2,
        )[0]

    flows = [ring_flow()] + [unit_flow(member) for member in range(children)]
    flows += [link_flow(), prepare_flow(), parent_flow()]
    flows += [unit_flow(children), child_flow(), gather_flow(), column_flow()]
    waiting = [(flow, None) for flow in flows]
    while waiting:
        tasks = [wish for _, wish in waiting if wish not in (None, WAIT)]
        results = iter(())
        if tasks:
            outs = [out for _, _, shapes in tasks for out in shapes]
            args = [value for _, values, _ in tasks for value in values]
            sizes = [(body, len(values), len(shapes)) for body, values, shapes in tasks]
            results = iter(
                heavy(functools.partial(step_kernel, sizes), outs, [info, *args], smem=1)
            )
        answered = []
        for flow, wish in waiting:
            answer = None
            if wish not in (None, WAIT):
                answer = [next(results) for _ in wish[2]]
            answered.append((flow, answer))
        waiting = []
        for flow, answer in answered:
            try:
                waiting.append((flow, flow.send(answer)))
            except StopIteration:
                pass

    diags, uppers = call(
        functools.partial(finish_kernel, row_count),
        [shape(members, diag_width, width), shape(children, diag_width, width)],
        [info, diag_inverse, held["links"][4]] + held["totals"],
        smem=1,
    )
    return held["columns"], diags, uppers


def solution(mesh):
    in_specs = (
        P("row", "col"),
        P(None, "row", None),
        P(None, "col", None),
        P(None, "col", None),
        P(),
    )
    out_specs = (P(None, ("row", "col"), None), P(None, "col", None), P(None, "col", None))
    return jax.shard_map(shards, mesh=mesh, in_specs=in_specs, out_specs=out_specs, check_vma=False)
```
